512 devices in a mesh: row: 64 (over y_hi, z, x), col: 8 (over y_lo, core).
Axes of the slice: x: 4, y: 8 (y_hi: 2, y_lo: 4; y = y_hi * 4 + y_lo), z: 8, core: 2. Of those that a mesh axis runs over, the one named last changes fastest.
Arguments:
- pair_field: bfloat16 [384, 384, 128], P('row', 'col'), may hold values from -6 to 6
- proj_weight: bfloat16 [2, 128, 640], replicated, may hold values from -0.5 to 0.5
- out_weight: bfloat16 [2, 128, 128], replicated, may hold values from -0.5 to 0.5
- in_gain: float32 [2, 128], replicated, may hold values from 0.1 to 1.9
- out_gain: float32 [2, 128], replicated, may hold values from 0.1 to 1.9
Outputs:
- updated_pair: bfloat16 [384, 384, 128], P('row', 'col')
The draws below stay inside these ranges and needn't reach their ends.
All inputs are finite; a program needn't handle non-finite values.
Results may differ from the reference program's by a relative error of at most 0.022.
Values may be sent and summed in bfloat16 or wider, within the bound.
No kernel may reach another device: no remote copies, remote signals or barrier semaphores. Data moves between devices by JAX's collectives and lax.ppermute only.
A program may use at most 64 MiB of HBM per device.

```python
import jax
import jax.numpy as jnp
from jax import lax

PAIR_DIM = 128
HIDDEN_SIZE = 128
RESIDUES = 384


def levels(stream_key, extent, cuts, smallest, top_value):
    level = 1.0
    for axis_at, parts in cuts:
        steps = jax.random.uniform(jax.random.fold_in(jax.random.fold_in(stream_key, 6), axis_at), (parts,), jnp.float32, smallest / len(cuts), top_value / len(cuts))
        level = level * jnp.repeat(jnp.exp(steps), extent[axis_at] // parts).reshape((-1,) + (1,) * (len(extent) - 1 - axis_at))
    return level


def scatter_about(rng, dims, scale, reach, split=(), dtype=jnp.bfloat16):
    level = levels(rng, dims, split, -0.22, 0.18) if split else 1.0
    array = jax.random.normal(rng, dims, jnp.float32) * scale * level
    return jnp.minimum(jnp.maximum(array, -reach), reach).astype(dtype)


def setup_inputs(seed: int = 0) -> dict:
    arg_keys = jax.random.split(jax.random.key(seed), 6)
    return {
        "pair_field": scatter_about(arg_keys[0], (RESIDUES, RESIDUES, PAIR_DIM), 1.0, 6.0, ((0, 64), (1, 8))),
        "proj_weight": scatter_about(arg_keys[1], (2, PAIR_DIM, 4 * HIDDEN_SIZE + PAIR_DIM), PAIR_DIM ** -0.5, 0.5),
        "out_weight": scatter_about(arg_keys[2], (2, HIDDEN_SIZE, PAIR_DIM), HIDDEN_SIZE ** -0.5, 0.5),
        "in_gain": jnp.clip(1.0 + 0.18 * jax.random.normal(arg_keys[3], (2, PAIR_DIM), jnp.float32), 0.1, 1.9),
        "out_gain": jnp.clip(1.0 + 0.18 * jax.random.normal(arg_keys[4], (2, HIDDEN_SIZE), jnp.float32), 0.1, 1.9),
    }


def normalize(values, gain):
    mean = lax.optimization_barrier(jnp.mean(values, axis=-1, keepdims=True))
    centred = values - mean
    spread = lax.optimization_barrier(jnp.mean(centred * centred, axis=-1, keepdims=True))
    return centred * lax.rsqrt(spread + 1e-05) * gain

def prepare(field, weight, gain):
    widened = field.astype(jnp.float32)
    normed = normalize(widened, gain).astype(jnp.bfloat16)
    projected = jnp.einsum('ijc,cd->ijd', normed.astype(jnp.float32), weight.astype(jnp.float32))
    left_side = (jax.nn.sigmoid(projected[..., HIDDEN_SIZE:2 * HIDDEN_SIZE]) * projected[..., :HIDDEN_SIZE]).astype(jnp.bfloat16)
    right_side = (jax.nn.sigmoid(projected[..., 3 * HIDDEN_SIZE:4 * HIDDEN_SIZE]) * projected[..., 2 * HIDDEN_SIZE:3 * HIDDEN_SIZE]).astype(jnp.bfloat16)
    gating = jax.nn.sigmoid(projected[..., 4 * HIDDEN_SIZE:])
    return (widened, left_side, right_side, gating)

def finish(widened, summed, gating, weight, gain):
    mixed = normalize(summed, gain).astype(jnp.bfloat16)
    update = gating * jnp.einsum('ijh,hc->ijc', mixed.astype(jnp.float32), weight.astype(jnp.float32))
    return (widened + update).astype(jnp.bfloat16)

def reference(pair_field, proj_weight, out_weight, in_gain, out_gain):
    widened, left_side, right_side, gating = prepare(pair_field, proj_weight[0], in_gain[0])
    summed = jnp.einsum('ikh,jkh->ijh', left_side.astype(jnp.float32), right_side.astype(jnp.float32))
    first_pair = finish(widened, summed, gating, out_weight[0], out_gain[0])
    widened, left_side, right_side, gating = prepare(first_pair, proj_weight[1], in_gain[1])
    summed = jnp.einsum('kih,kjh->ijh', left_side.astype(jnp.float32), right_side.astype(jnp.float32))
    return finish(widened, summed, gating, out_weight[1], out_gain[1])
```

```python
import functools

import jax
import jax.numpy as jnp
import numpy as np
from jax import lax
from jax.experimental import pallas as pl
from jax.experimental.pallas import tpu as pltpu
from jax.sharding import Mesh
from jax.sharding import PartitionSpec as P

H = 128
HALF = 64
SPREAD = ("yl", "core", "yh", "x")
F32 = jnp.float32
BF16 = jnp.bfloat16


def normalize(values, gain, axis):
    mean = jnp.mean(values, axis=axis, keepdims=True)
    centred = values - mean
    spread = jnp.mean(centred * centred, axis=axis, keepdims=True)
    return centred * lax.rsqrt(spread + 1e-05) * gain


def swap(tile):
    return pltpu.roll(tile, HALF, 1)


def lower(shape):
    return lax.broadcasted_iota(jnp.int32, shape, 1) < HALF


def halves(top, bottom):
    low = lower(top.shape)
    return jnp.where(low, top, swap(bottom)), jnp.where(low, swap(top), bottom)


def widen_groups(values, scratch):
    rows = values.shape[0]
    scratch[0:rows, :] = values
    keep = lax.broadcasted_iota(jnp.int32, (8, H), 0) < 6
    return jnp.concatenate(
        [jnp.where(keep, scratch[6 * n : 6 * n + 8, :], 0.0) for n in range(rows // 6)], axis=0
    )


def spread_sides(normed, weight):
    projected = lax.dot_general(
        weight[:, : 4 * H], normed, (((0,), (1,)), ((), ())), preferred_element_type=F32
    )
    rows = []
    for side in range(2):
        value = projected[2 * side * H : (2 * side + 1) * H]
        gate = projected[(2 * side + 1) * H : (2 * side + 2) * H]
        turned = jax.nn.sigmoid(gate) * value
        for t in range(3):
            tile = turned[:, t * H : (t + 1) * H]
            rows.extend(halves(tile[:HALF], tile[HALF:]))
        rows.extend([jnp.zeros((HALF, H), F32)] * 2)
    return jnp.swapaxes(jnp.stack(rows, axis=0), 0, 1).astype(BF16)


def gate_of(normed, weight):
    return jax.nn.sigmoid(jnp.dot(normed, weight[:, 4 * H :], preferred_element_type=F32))


def finish(arrived, field, gating, weight, gain):
    by_row = jnp.swapaxes(arrived.astype(F32), 0, 1)
    tiles = []
    for t in range(3):
        tiles.append(jnp.concatenate(halves(by_row[2 * t], by_row[2 * t + 1]), axis=0))
    summed = jnp.concatenate(tiles, axis=1)
    mixed = normalize(summed, gain, 0).astype(BF16)
    update = lax.dot_general(
        mixed, weight, (((0,), (0,)), ((), ())), preferred_element_type=F32
    )
    return field + gating * update


def send_back(product, out_ref):
    for u in range(4):
        tile = product[:, u * H : (u + 1) * H]
        for e, part in enumerate(halves(tile[:HALF], tile[HALF:])):
            c = 2 * u + e
            out_ref[c * 8 : (c + 1) * 8] = part.reshape(8, 8, H).astype(BF16)


def start_kernel(pair_ref, weight_ref, gain_ref, out_ref, field_ref, gate_ref, scratch):
    field = widen_groups(pair_ref[...].reshape(288, H).astype(F32), scratch)
    normed = normalize(field, gain_ref[...], 1).astype(BF16)
    weight = weight_ref[...]
    out_ref[...] = spread_sides(normed, weight)
    field_ref[...] = field
    gate_ref[...] = gate_of(normed, weight)


def outgoing_kernel(own_ref, right_ref, out_ref):
    left = own_ref[:, 0:8, :].astype(F32).reshape(8, HALF, H)
    low = lower((HALF, H))
    left_all, right_all = [], []
    for c in range(8):
        part = left[c]
        left_all.append(
            jnp.concatenate([jnp.where(low, part, 0.0), jnp.where(low, 0.0, part)], axis=0).astype(BF16)
        )
        right = right_ref[:, c * 8 : (c + 1) * 8].astype(F32)
        right_all.append(
            jnp.concatenate([right[:, :4].reshape(256, H), right[:, 4:].reshape(256, H)], axis=0).astype(BF16)
        )
    product = lax.dot_general(
        jnp.concatenate(left_all, axis=1),
        jnp.concatenate(right_all, axis=1),
        (((1,), (1,)), ((), ())),
        preferred_element_type=F32,
    )
    send_back(product, out_ref)


def middle_kernel(
    arrived_ref, field_ref, gate_ref, out_weight_ref, out_gain_ref, weight_ref, gain_ref, out_ref, first_ref, next_gate_ref
):
    first = finish(
        arrived_ref[...], field_ref[...], gate_ref[...], out_weight_ref[...], out_gain_ref[...]
    ).astype(BF16).astype(F32)
    normed = normalize(first, gain_ref[...], 1).astype(BF16)
    weight = weight_ref[...]
    out_ref[...] = spread_sides(normed, weight)
    first_ref[...] = first
    next_gate_ref[...] = gate_of(normed, weight)


def incoming_kernel(own_ref, squeeze_ref, out_ref):
    sides = []
    for side in range(2):
        part = own_ref[:, side * 8 : side * 8 + 8, :].astype(F32).reshape(8, HALF, H)
        tiles = [halves(part[2 * u], part[2 * u + 1]) for u in range(4)]
        for channel in range(2):
            sides.append(jnp.concatenate([tile[channel] for tile in tiles], axis=1))
    packed = jnp.dot(
        jnp.concatenate(sides, axis=0).astype(BF16), squeeze_ref[...], preferred_element_type=F32
    ).astype(BF16)
    for channel in range(2):
        left = packed[channel * HALF : (channel + 1) * HALF]
        right = packed[(2 + channel) * HALF : (3 + channel) * HALF]
        product = lax.dot_general(
            left, right, (((0,), (0,)), ((), ())), preferred_element_type=F32
        )
        out_ref[:, channel] = product.reshape(8, 48, 384).astype(BF16)


def sum_kernel(parts_ref, stretch_ref, out_ref, scratch):
    products = []
    for channel in range(2):
        total = parts_ref[0, channel].astype(F32)
        for z in range(1, 8):
            total = total + parts_ref[z, channel].astype(F32)
        wide = jnp.concatenate(
            [widen_groups(total[:, t * H : (t + 1) * H], scratch.at[3 * channel + t]) for t in range(3)], axis=1
        )
        products.append(wide.astype(BF16))
    send_back(
        jnp.dot(jnp.concatenate(products, axis=0), stretch_ref[...], preferred_element_type=F32), out_ref
    )


def end_kernel(arrived_ref, field_ref, gate_ref, out_weight_ref, out_gain_ref, out_ref, scratch):
    final = finish(
        arrived_ref[...], field_ref[...], gate_ref[...], out_weight_ref[...], out_gain_ref[...]
    )
    for n in range(48):
        scratch[6 * n : 6 * n + 8, :] = final[8 * n : 8 * n + 8]
    out_ref[...] = scratch[0:288, :].reshape(6, 48, H).astype(BF16)


def squeeze_matrix():
    places = np.arange(512).reshape(2, 8, 4, 8)[..., :6].transpose(1, 0, 2, 3).reshape(-1)
    return (np.arange(512)[:, None] == places[None, :]).astype(jnp.bfloat16)


def call(kernel, outs, scratch=(), cost=20_000_000):
    return pl.pallas_call(
        kernel,
        out_shape=[jax.ShapeDtypeStruct(shape, dtype) for shape, dtype in outs],
        scratch_shapes=list(scratch),
        compiler_params=pltpu.CompilerParams(vmem_limit_bytes=48 * 1024 * 1024),
        cost_estimate=pl.CostEstimate(flops=cost, bytes_accessed=1_000_000, transcendentals=100_000),
    )


def shards(pair_field, proj_weight, out_weight, in_gain, out_gain):
    exchange = functools.partial(lax.all_to_all, split_axis=0, concat_axis=0, tiled=True)
    squeeze = squeeze_matrix()
    wide, narrow = (384, H), (64, 8, H)

    sides, field, gating = call(
        start_kernel, [((64, 16, H), BF16), (wide, F32), (wide, F32)], [pltpu.VMEM((296, H), F32)]
    )(pair_field, proj_weight[0], in_gain[0][None])
    own = exchange(sides, SPREAD)
    right = lax.all_gather(own[:, 8:], "z", axis=0, tiled=False)
    [back] = call(outgoing_kernel, [(narrow, BF16)])(own, right)
    arrived = exchange(back, SPREAD)

    sides, field, gating = call(
        middle_kernel, [((64, 16, H), BF16), (wide, F32), (wide, F32)]
    )(arrived, field, gating, out_weight[0], out_gain[0][:, None], proj_weight[1], in_gain[1][None])
    own = exchange(sides, SPREAD)
    [parts] = call(incoming_kernel, [((8, 2, 48, 384), BF16)])(own, jnp.asarray(squeeze))
    parts = exchange(parts, "z")
    [back] = call(sum_kernel, [(narrow, BF16)], [pltpu.VMEM((6, 56, H), F32)])(
        parts, jnp.asarray(squeeze.T)
    )
    arrived = exchange(back, SPREAD)
    [out] = call(end_kernel, [((6, 48, H), BF16)], [pltpu.VMEM((296, H), F32)])(
        arrived, field, gating, out_weight[1], out_gain[1][:, None]
    )
    return out


def solution(mesh):
    fine = Mesh(mesh.devices.reshape(2, 8, 4, 4, 2), ("yh", "z", "x", "yl", "core"))
    row, col = ("yh", "z", "x"), ("yl", "core")
    return jax.shard_map(
        shards,
        mesh=fine,
        in_specs=(P(row, col, None), P(), P(), P(), P()),
        out_specs=P(row, col, None),
        check_vma=False,
    )
```

```python
import functools

import jax
import jax.numpy as jnp
import numpy as np
from jax import lax
from jax.experimental import pallas as pl
from jax.experimental.pallas import tpu as pltpu
from jax.sharding import Mesh
from jax.sharding import PartitionSpec as P

H = 128
HALF = 64
SPREAD = ("yl", "core", "yh", "z")
F32 = jnp.float32
BF16 = jnp.bfloat16


def normalize(values, gain, axis):
    mean = jnp.mean(values, axis=axis, keepdims=True)
    centred = values - mean
    spread = jnp.mean(centred * centred, axis=axis, keepdims=True)
    return centred * lax.rsqrt(spread + 1e-05) * gain


def halves(top, bottom):
    low = lax.broadcasted_iota(jnp.int32, top.shape, 1) < HALF
    return jnp.where(low, top, pltpu.roll(bottom, HALF, 1)), jnp.where(low, pltpu.roll(top, HALF, 1), bottom)


def by_device(rows):
    return jnp.swapaxes(jnp.stack(rows, axis=0), 0, 1).astype(BF16)


def widen_groups(values, scratch):
    scratch[0:288, :] = values
    keep = lax.broadcasted_iota(jnp.int32, (8, H), 0) < 6
    return jnp.concatenate(
        [jnp.where(keep, scratch[6 * n : 6 * n + 8, :], 0.0) for n in range(48)], axis=0
    )


def spread_sides(normed, weight):
    projected = lax.dot_general(
        weight[:, : 4 * H], normed, (((0,), (1,)), ((), ())), preferred_element_type=F32
    )
    rows = []
    for side in range(2):
        value = projected[2 * side * H : (2 * side + 1) * H]
        gate = projected[(2 * side + 1) * H : (2 * side + 2) * H]
        turned = jax.nn.sigmoid(gate) * value
        rows.extend(turned[:, t * H : (t + 1) * H] for t in range(3))
        rows.append(jnp.zeros((H, H), F32))
    return by_device(rows)


def gate_of(normed, weight):
    return jax.nn.sigmoid(jnp.dot(normed, weight[:, 4 * H :], preferred_element_type=F32))


def finish(arrived, field, gating, weight, gain):
    by_row = jnp.swapaxes(arrived.astype(F32), 0, 1)
    summed = jnp.concatenate([by_row[t] for t in range(3)], axis=1)
    column = jnp.swapaxes(jnp.broadcast_to(gain, (8, H)), 0, 1)[:, :1]
    mixed = normalize(summed, column, 0).astype(BF16)
    update = lax.dot_general(
        mixed, weight, (((0,), (0,)), ((), ())), preferred_element_type=F32
    )
    return field + gating * update


def matrices(own, squeeze):
    by_row = jnp.swapaxes(own.astype(F32), 0, 1)
    rows = []
    for side in range(2):
        for t in range(3):
            part = by_row[4 * side + t]
            tiles = [
                halves(part[32 * u : 32 * u + 16], part[32 * u + 16 : 32 * u + 32]) for u in range(4)
            ]
            for e in range(2):
                rows.append(jnp.concatenate([tile[e] for tile in tiles], axis=1))
    packed = jnp.dot(
        jnp.concatenate(rows, axis=0).astype(BF16), squeeze, preferred_element_type=F32
    ).astype(BF16)
    return packed[:96], packed[96:]


def send_back(product, stretch):
    wide = jnp.dot(product.astype(BF16), stretch, preferred_element_type=F32)
    rows = []
    for t in range(3):
        parts = []
        for u in range(4):
            tile = wide[32 * t : 32 * t + 32, u * H : (u + 1) * H]
            parts.extend(halves(tile[:16], tile[16:]))
        rows.append(jnp.concatenate(parts, axis=0))
    rows.append(jnp.zeros((H, H), F32))
    return by_device(rows)


def start_kernel(pair_ref, weight_ref, gain_ref, out_ref, field_ref, gate_ref, scratch):
    field = widen_groups(pair_ref[...].reshape(288, H).astype(F32), scratch)
    normed = normalize(field, gain_ref[0:1, :], 1).astype(BF16)
    weight = weight_ref[0]
    out_ref[...] = spread_sides(normed, weight)
    field_ref[...] = field
    gate_ref[...] = gate_of(normed, weight)


def pack_kernel(own_ref, squeeze_ref, left_ref, right_ref):
    left, right = matrices(own_ref[...], squeeze_ref[...])
    left_ref[...] = left
    for x in range(4):
        right_ref[x] = right


def outgoing_kernel(left_ref, right_ref, stretch_ref, out_ref):
    product = lax.dot_general(
        left_ref[...],
        right_ref[...].reshape(384, 384),
        (((1,), (1,)), ((), ())),
        preferred_element_type=F32,
    )
    out_ref[...] = send_back(product, stretch_ref[...])


def middle_kernel(
    arrived_ref, field_ref, gate_ref, out_weight_ref, out_gain_ref, weight_ref, gain_ref, out_ref, first_ref, next_gate_ref
):
    first = finish(
        arrived_ref[...], field_ref[...], gate_ref[...], out_weight_ref[0], out_gain_ref[0:1, :]
    ).astype(BF16).astype(F32)
    normed = normalize(first, gain_ref[1:2, :], 1).astype(BF16)
    weight = weight_ref[1]
    out_ref[...] = spread_sides(normed, weight)
    first_ref[...] = first
    next_gate_ref[...] = gate_of(normed, weight)


def incoming_kernel(own_ref, squeeze_ref, out_ref):
    left, right = matrices(own_ref[...], squeeze_ref[...])
    product = lax.dot_general(
        left, right, (((0,), (0,)), ((), ())), preferred_element_type=F32
    )
    out_ref[...] = product.reshape(4, 96, 384).astype(BF16)


def sum_kernel(parts_ref, stretch_ref, out_ref):
    total = parts_ref[0].astype(F32)
    for x in range(1, 4):
        total = total + parts_ref[x].astype(F32)
    out_ref[...] = send_back(total, stretch_ref[...])


def end_kernel(arrived_ref, field_ref, gate_ref, out_weight_ref, out_gain_ref, out_ref, scratch):
    final = finish(
        arrived_ref[...], field_ref[...], gate_ref[...], out_weight_ref[1], out_gain_ref[1:2, :]
    )
    for n in range(48):
        scratch[6 * n : 6 * n + 8, :] = final[8 * n : 8 * n + 8]
    out_ref[...] = scratch[0:288, :].reshape(6, 48, H).astype(BF16)


def squeeze_matrix():
    places = np.arange(512).reshape(2, 8, 4, 8)[..., :6].transpose(2, 3, 0, 1).reshape(-1)
    return (np.arange(512)[:, None] == places[None, :]).astype(jnp.bfloat16)


def call(kernel, outs, scratch=(), cost=20_000_000):
    return pl.pallas_call(
        kernel,
        out_shape=[jax.ShapeDtypeStruct(shape, dtype) for shape, dtype in outs],
        scratch_shapes=list(scratch),
        compiler_params=pltpu.CompilerParams(vmem_limit_bytes=48 * 1024 * 1024),
        cost_estimate=pl.CostEstimate(flops=cost, bytes_accessed=1_000_000, transcendentals=100_000),
    )


def shards(pair_field, proj_weight, out_weight, in_gain, out_gain):
    exchange = functools.partial(lax.all_to_all, split_axis=0, concat_axis=0, tiled=True)
    squeeze, stretch = jnp.asarray(squeeze_matrix()), jnp.asarray(squeeze_matrix().T)
    pairs = ((384, H), F32)
    sides, results = ((H, 8, H), BF16), ((H, 4, H), BF16)
    block, blocks = ((96, 384), BF16), ((4, 96, 384), BF16)
    padded = pltpu.VMEM((296, H), F32)

    sent, field, gating = call(start_kernel, [sides, pairs, pairs], [padded])(
        pair_field, proj_weight, in_gain
    )
    own = exchange(sent, SPREAD)
    left, right = call(pack_kernel, [block, blocks])(own, squeeze)
    right = exchange(right, "x")
    [back] = call(outgoing_kernel, [results])(left, right, stretch)
    arrived = exchange(back, SPREAD)

    sent, field, gating = call(middle_kernel, [sides, pairs, pairs])(
        arrived, field, gating, out_weight, out_gain, proj_weight, in_gain
    )
    own = exchange(sent, SPREAD)
    [parts] = call(incoming_kernel, [blocks])(own, squeeze)
    parts = exchange(parts, "x")
    [back] = call(sum_kernel, [results])(parts, stretch)
    arrived = exchange(back, SPREAD)
    [out] = call(end_kernel, [((6, 48, H), BF16)], [padded])(
        arrived, field, gating, out_weight, out_gain
    )
    return out


def solution(mesh):
    fine = Mesh(mesh.devices.reshape(2, 8, 4, 4, 2), ("yh", "z", "x", "yl", "core"))
    row, col = ("yh", "z", "x"), ("yl", "core")
    return jax.shard_map(
        shards,
        mesh=fine,
        in_specs=(P(row, col, None), P(), P(), P(), P()),
        out_specs=P(row, col, None),
        check_vma=False,
    )
```

```python
import functools

import jax
import jax.numpy as jnp
import numpy as np
from jax import lax
from jax.experimental import pallas as pl
from jax.experimental.pallas import tpu as pltpu
from jax.sharding import Mesh
from jax.sharding import PartitionSpec as P

H = 128
HALF = 64
SPREAD = ("yl", "core", "yh", "z")
START_ROOM = 60 * 1024
F32 = jnp.float32
BF16 = jnp.bfloat16


def normalize(values, gain, axis):
    mean = jnp.mean(values, axis=axis, keepdims=True)
    centred = values - mean
    spread = jnp.mean(centred * centred, axis=axis, keepdims=True)
    return centred * lax.rsqrt(spread + 1e-05) * gain


def halves(top, bottom):
    low = lax.broadcasted_iota(jnp.int32, top.shape, 1) < HALF
    return jnp.where(low, top, pltpu.roll(bottom, HALF, 1)), jnp.where(low, pltpu.roll(top, HALF, 1), bottom)


def by_device(rows):
    return jnp.swapaxes(jnp.stack(rows, axis=0), 0, 1)


def widen_groups(values, scratch):
    scratch[0:288, :] = values
    keep = lax.broadcasted_iota(jnp.int32, (8, H), 0) < 6
    return jnp.concatenate(
        [jnp.where(keep, scratch[6 * n : 6 * n + 8, :], 0.0) for n in range(48)], axis=0
    )


def spread_sides(normed, weight):
    projected = lax.dot_general(
        weight[:, : 4 * H], normed, (((0,), (1,)), ((), ())), preferred_element_type=F32
    )
    rows = []
    for side in range(2):
        value = projected[2 * side * H : (2 * side + 1) * H]
        gate = projected[(2 * side + 1) * H : (2 * side + 2) * H]
        turned = jax.nn.sigmoid(gate) * value
        rows.extend(turned[:, t * H : (t + 1) * H] for t in range(3))
    return by_device(rows).reshape(H, 3, 2, H).astype(BF16)


def gate_of(normed, weight):
    return jax.nn.sigmoid(jnp.dot(normed, weight[:, 4 * H :], preferred_element_type=F32))


def finish(arrived, field, gating, weight, gain):
    by_row = jnp.swapaxes(arrived.astype(F32), 0, 1)
    summed = jnp.concatenate([by_row[t] for t in range(3)], axis=1)
    column = jnp.swapaxes(jnp.broadcast_to(gain, (8, H)), 0, 1)[:, :1]
    mixed = normalize(summed, column, 0).astype(BF16)
    update = lax.dot_general(
        mixed, weight, (((0,), (0,)), ((), ())), preferred_element_type=F32
    )
    return field.astype(F32) + gating * update


def matrices(own, squeeze):
    by_row = jnp.swapaxes(own.astype(F32).reshape(H, 6, H), 0, 1)
    rows = []
    for side in range(2):
        for t in range(3):
            part = by_row[3 * side + t]
            tiles = [
                halves(part[32 * u : 32 * u + 16], part[32 * u + 16 : 32 * u + 32]) for u in range(4)
            ]
            for e in range(2):
                rows.append(jnp.concatenate([tile[e] for tile in tiles], axis=1))
    packed = jnp.dot(
        jnp.concatenate(rows, axis=0).astype(BF16), squeeze, preferred_element_type=F32
    ).astype(BF16)
    return packed[:96], packed[96:]


def send_back(product, stretch):
    wide = jnp.dot(product.astype(BF16), stretch, preferred_element_type=F32)
    rows = []
    for t in range(3):
        parts = []
        for u in range(4):
            tile = wide[32 * t : 32 * t + 32, u * H : (u + 1) * H]
            parts.extend(halves(tile[:16], tile[16:]))
        rows.append(jnp.concatenate(parts, axis=0))
    rows.append(jnp.zeros((H, H), F32))
    return by_device(rows).astype(BF16)


def start_kernel(
    pair_hbm, weight_hbm, gain_hbm, out_gain_hbm,
    out_ref, field_ref, gate_ref,
    scratch, pair_ref, weight_ref, gain_ref, out_gain_ref, sems,
):
    moves = [
        (pair_hbm, pair_ref),
        (gain_hbm, gain_ref),
        (weight_hbm.at[0], weight_ref),
        (out_gain_hbm, out_gain_ref),
    ]
    copies = [pltpu.make_async_copy(source, target, sems.at[n]) for n, (source, target) in enumerate(moves)]
    for copy in copies:
        copy.start()
    copies[0].wait()
    field = widen_groups(pair_ref[...].reshape(288, H).astype(F32), scratch)
    field_ref[...] = field.astype(BF16)
    copies[1].wait()
    normed = normalize(field, gain_ref[0:1, :], 1).astype(BF16)
    copies[2].wait()
    weight = weight_ref[...]
    out_ref[...] = spread_sides(normed, weight)
    gate_ref[:384] = gate_of(normed, weight)
    copies[3].wait()
    gate_ref[384:392] = jnp.concatenate([gain_ref[...], out_gain_ref[...], jnp.zeros((4, H), F32)], axis=0)


def pack_kernel(own_ref, squeeze_ref, left_ref, right_ref):
    left, right = matrices(own_ref[...], squeeze_ref[...])
    left_ref[...] = left
    for x in range(4):
        right_ref[x] = right


def outgoing_kernel(left_ref, right_ref, stretch_ref, out_ref):
    product = lax.dot_general(
        left_ref[...],
        right_ref[...].reshape(384, 384),
        (((1,), (1,)), ((), ())),
        preferred_element_type=F32,
    )
    out_ref[...] = send_back(product, stretch_ref[...])


def middle_kernel(
    arrived_ref, field_ref, gate_ref, out_weight_ref, weight_ref, out_ref, first_ref, next_gate_ref
):
    first = finish(
        arrived_ref[...], field_ref[...], gate_ref[:384], out_weight_ref[0], gate_ref[386:387]
    ).astype(BF16)
    normed = normalize(first.astype(F32), gate_ref[385:386], 1).astype(BF16)
    weight = weight_ref[1]
    out_ref[...] = spread_sides(normed, weight)
    first_ref[...] = first
    next_gate_ref[...] = gate_of(normed, weight)


def incoming_kernel(own_ref, squeeze_ref, out_ref):
    left, right = matrices(own_ref[...], squeeze_ref[...])
    product = lax.dot_general(
        left, right, (((0,), (0,)), ((), ())), preferred_element_type=F32
    )
    out_ref[...] = product.reshape(4, 96, 384).astype(BF16)


def sum_kernel(parts_ref, stretch_ref, out_ref):
    total = parts_ref[0].astype(F32)
    for x in range(1, 4):
        total = total + parts_ref[x].astype(F32)
    out_ref[...] = send_back(total, stretch_ref[...])


def end_kernel(arrived_ref, field_ref, gate_ref, out_weight_ref, gains_ref, out_ref, scratch):
    final = finish(
        arrived_ref[...], field_ref[...], gate_ref[...], out_weight_ref[1], gains_ref[387:388]
    )
    for n in range(48):
        scratch[6 * n : 6 * n + 8, :] = final[8 * n : 8 * n + 8]
    out_ref[...] = scratch[0:288, :].reshape(6, 48, H).astype(BF16)


def squeeze_matrix():
    places = np.arange(512).reshape(2, 8, 4, 8)[..., :6].transpose(2, 3, 0, 1).reshape(-1)
    return (np.arange(512)[:, None] == places[None, :]).astype(jnp.bfloat16)


def call(kernel, outs, scratch=(), room=48 * 1024, **specs):
    return pl.pallas_call(
        kernel,
        out_shape=[jax.ShapeDtypeStruct(shape, dtype) for shape, dtype in outs],
        scratch_shapes=list(scratch),
        compiler_params=pltpu.CompilerParams(vmem_limit_bytes=room * 1024),
        cost_estimate=pl.CostEstimate(flops=20_000_000, bytes_accessed=1_000_000, transcendentals=100_000),
        **specs,
    )


def shards(pair_field, proj_weight, out_weight, in_gain, out_gain):
    exchange = functools.partial(lax.all_to_all, split_axis=0, concat_axis=0, tiled=True)
    squeeze, stretch = jnp.asarray(squeeze_matrix()), jnp.asarray(squeeze_matrix().T)
    pairs = ((384, H), BF16)
    sides, results = ((H, 3, 2, H), BF16), ((H, 4, H), BF16)
    block, blocks = ((96, 384), BF16), ((4, 96, 384), BF16)
    padded = pltpu.VMEM((296, H), F32)

    sent, field, gating = call(
        start_kernel,
        [sides, pairs, ((392, H), F32)],
        [
            padded,
            pltpu.VMEM((6, 48, H), BF16),
            pltpu.VMEM((H, 5 * H), BF16),
            pltpu.VMEM((2, H), F32),
            pltpu.VMEM((2, H), F32),
            pltpu.SemaphoreType.DMA((4,)),
        ],
        START_ROOM,
        in_specs=[pl.BlockSpec(memory_space=pltpu.HBM)] * 4,
    )(pair_field, proj_weight, in_gain, out_gain)
    own = exchange(sent, SPREAD)
    left, right = call(pack_kernel, [block, blocks])(own, squeeze)
    right = exchange(right, "x")
    [back] = call(outgoing_kernel, [results])(left, right, stretch)
    arrived = exchange(back, SPREAD)

    sent, field, next_gating = call(middle_kernel, [sides, pairs, ((384, H), F32)])(
        arrived, field, gating, out_weight, proj_weight
    )
    own = exchange(sent, SPREAD)
    [parts] = call(incoming_kernel, [blocks])(own, squeeze)
    parts = exchange(parts, "x")
    [back] = call(sum_kernel, [results])(parts, stretch)
    arrived = exchange(back, SPREAD)
    [out] = call(end_kernel, [((6, 48, H), BF16)], [padded])(
        arrived, field, next_gating, out_weight, gating
    )
    return out


def solution(mesh):
    fine = Mesh(mesh.devices.reshape(2, 8, 4, 4, 2), ("yh", "z", "x", "yl", "core"))
    row, col = ("yh", "z", "x"), ("yl", "core")
    return jax.shard_map(
        shards,
        mesh=fine,
        in_specs=(P(row, col, None), P(), P(), P(), P()),
        out_specs=P(row, col, None),
        check_vma=False,
    )
```

```python
import functools

import jax
import jax.numpy as jnp
import numpy as np
from jax import lax
from jax.experimental import pallas as pl
from jax.experimental.pallas import tpu as pltpu
from jax.sharding import Mesh
from jax.sharding import PartitionSpec as P

H = 128
HALF = 64
SPREAD = ("yl", "z1", "yh", "z2", "z0")
START_ROOM = 60 * 1024
F32 = jnp.float32
BF16 = jnp.bfloat16


def normalize(values, gain, axis):
    mean = jnp.mean(values, axis=axis, keepdims=True)
    centred = values - mean
    spread = jnp.mean(centred * centred, axis=axis, keepdims=True)
    return centred * lax.rsqrt(spread + 1e-05) * gain


def halves(top, bottom):
    low = lax.broadcasted_iota(jnp.int32, top.shape, 1) < HALF
    return jnp.where(low, top, pltpu.roll(bottom, HALF, 1)), jnp.where(low, pltpu.roll(top, HALF, 1), bottom)


def by_device(rows):
    return jnp.swapaxes(jnp.stack(rows, axis=0), 0, 1)


def widen_groups(values, scratch):
    scratch[0:288, :] = values
    keep = lax.broadcasted_iota(jnp.int32, (8, H), 0) < 6
    return jnp.concatenate(
        [jnp.where(keep, scratch[6 * n : 6 * n + 8, :], 0.0) for n in range(48)], axis=0
    )


def spread_sides(normed, weight):
    projected = lax.dot_general(
        weight[:, : 4 * H], normed, (((0,), (1,)), ((), ())), preferred_element_type=F32
    )
    rows = []
    for side in range(2):
        value = projected[2 * side * H : (2 * side + 1) * H]
        gate = projected[(2 * side + 1) * H : (2 * side + 2) * H]
        turned = jax.nn.sigmoid(gate) * value
        for channel in range(2):
            part = turned[channel * HALF : (channel + 1) * HALF]
            rows.extend(part[:, t * H : (t + 1) * H] for t in range(3))
    return by_device(rows).reshape(HALF, 3, 4, H).astype(BF16)


def gate_of(normed, weight):
    return jax.nn.sigmoid(jnp.dot(normed, weight[:, 4 * H :], preferred_element_type=F32))


def finish(arrived, field, gating, weight, gain):
    by_row = jnp.swapaxes(arrived.astype(F32).reshape(HALF, 6, H), 0, 1)
    summed = jnp.concatenate(
        [jnp.concatenate([by_row[3 * channel + t] for t in range(3)], axis=1) for channel in range(2)], axis=0
    )
    column = jnp.swapaxes(jnp.broadcast_to(gain, (8, H)), 0, 1)[:, :1]
    mixed = normalize(summed, column, 0).astype(BF16)
    update = lax.dot_general(
        mixed, weight, (((0,), (0,)), ((), ())), preferred_element_type=F32
    )
    return field.astype(F32) + gating * update


def rows_of(own):
    return jnp.swapaxes(own.astype(F32).reshape(HALF, 12, H), 0, 1)


def matrix(by_row, side, channel):
    found = ([], [])
    for t in range(3):
        part = by_row[6 * side + 3 * channel + t]
        tiles = [halves(part[32 * u : 32 * u + 16], part[32 * u + 16 : 32 * u + 32]) for u in range(2)]
        for e in range(2):
            both = jnp.concatenate([tile[e] for tile in tiles], axis=1)
            for z1 in range(2):
                found[z1].append(both[8 * z1 : 8 * z1 + 8])
    return [jnp.concatenate(pieces, axis=0) for pieces in found]


def whole_matrix(cores, side, channel):
    parts = [matrix(by_row, side, channel) for by_row in cores]
    return [jnp.concatenate([parts[0][z1], parts[1][z1]], axis=1) for z1 in range(2)]


def squeezed(rows, squeeze):
    return jnp.dot(
        jnp.concatenate(rows, axis=0).astype(BF16), squeeze, preferred_element_type=F32
    ).astype(BF16)


def send_back(product, stretch):
    wide = jnp.dot(product.astype(BF16), stretch, preferred_element_type=F32)
    rows = []
    for channel in range(2):
        for t in range(3):
            parts = []
            for u in range(2):
                lanes = slice((2 * channel + u) * H, (2 * channel + u + 1) * H)
                pair = [
                    jnp.concatenate([wide[8 * a : 8 * a + 8, lanes], wide[48 + 8 * a : 56 + 8 * a, lanes]], axis=0)
                    for a in (2 * t, 2 * t + 1)
                ]
                parts.extend(halves(*pair))
            rows.append(jnp.concatenate(parts, axis=0))
    return by_device(rows).reshape(HALF, 3, 2, H).astype(BF16)


def start_kernel(
    pair_hbm, weight_hbm, gain_hbm, out_gain_hbm,
    out_ref, field_ref, gate_ref,
    scratch, pair_ref, weight_ref, gain_ref, out_gain_ref, sems,
):
    moves = [
        (pair_hbm, pair_ref),
        (gain_hbm, gain_ref),
        (weight_hbm.at[0], weight_ref),
        (out_gain_hbm, out_gain_ref),
    ]
    copies = [pltpu.make_async_copy(source, target, sems.at[n]) for n, (source, target) in enumerate(moves)]
    for copy in copies:
        copy.start()
    copies[0].wait()
    field = widen_groups(pair_ref[...].reshape(288, H).astype(F32), scratch)
    field_ref[...] = field.astype(BF16)
    copies[1].wait()
    normed = normalize(field, gain_ref[0:1, :], 1).astype(BF16)
    copies[2].wait()
    weight = weight_ref[...]
    out_ref[...] = spread_sides(normed, weight)
    gate_ref[:384] = gate_of(normed, weight)
    copies[3].wait()
    gate_ref[384:392] = jnp.concatenate([gain_ref[...], out_gain_ref[...], jnp.zeros((4, H), F32)], axis=0)


def pack_kernel(both_ref, squeeze_ref, left_ref, right_ref):
    cores = [rows_of(both_ref[core]) for core in range(2)]
    first = lax.axis_index("core") == 0
    rows = []
    for channel in range(2):
        rows.extend(whole_matrix(cores, 0, channel))
    for channel in range(2):
        rows.append(jnp.where(first, *whole_matrix(cores, 1, channel)))
    packed = squeezed(rows, squeeze_ref[...])
    left_ref[...] = packed[:192]
    for x in range(4):
        right_ref[x] = packed[192:]


def outgoing_kernel(left_ref, right_ref, stretch_ref, out_ref):
    left = jnp.concatenate([left_ref[:96], left_ref[96:]], axis=1)
    none = jnp.zeros((192, 384), BF16)
    right = [right_ref[:, 48 * channel : 48 * channel + 48].reshape(192, 384) for channel in range(2)]
    right = jnp.concatenate(
        [jnp.concatenate([right[0], none], axis=1), jnp.concatenate([none, right[1]], axis=1)], axis=0
    )
    product = lax.dot_general(left, right, (((1,), (1,)), ((), ())), preferred_element_type=F32)
    out_ref[...] = send_back(product, stretch_ref[...])


def middle_kernel(
    arrived_ref, field_ref, gate_ref, out_weight_ref, weight_ref, out_ref, first_ref, next_gate_ref
):
    first = finish(
        arrived_ref[...], field_ref[...], gate_ref[:384], out_weight_ref[0], gate_ref[386:387]
    ).astype(BF16)
    normed = normalize(first.astype(F32), gate_ref[385:386], 1).astype(BF16)
    weight = weight_ref[1]
    out_ref[...] = spread_sides(normed, weight)
    first_ref[...] = first
    next_gate_ref[...] = gate_of(normed, weight)


def incoming_kernel(own_ref, both_ref, squeeze_ref, out_ref):
    cores = [rows_of(both_ref[core]) for core in range(2)]
    own = rows_of(own_ref[...])
    none = jnp.zeros((96, 256), F32)
    rows = []
    for channel in range(2):
        rows.extend(whole_matrix(cores, 0, channel))
    for channel in range(2):
        part = jnp.concatenate(matrix(own, 1, channel), axis=0)
        rows.append(jnp.concatenate([none, part] if channel else [part, none], axis=1))
    packed = squeezed(rows, squeeze_ref[...])
    product = lax.dot_general(
        packed[:192], packed[192:], (((0,), (0,)), ((), ())), preferred_element_type=F32
    ).astype(BF16)
    for x in range(4):
        for z1 in range(2):
            at = 192 * z1 + 48 * x
            out_ref[x, 48 * z1 : 48 * z1 + 48] = product[at : at + 48]


def sum_kernel(parts_ref, stretch_ref, out_ref):
    total = parts_ref[0].astype(F32)
    for x in range(1, 4):
        total = total + parts_ref[x].astype(F32)
    out_ref[...] = send_back(total, stretch_ref[...])


def end_kernel(arrived_ref, field_ref, gate_ref, out_weight_ref, gains_ref, out_ref, scratch):
    final = finish(
        arrived_ref[...], field_ref[...], gate_ref[...], out_weight_ref[1], gains_ref[387:388]
    )
    for n in range(48):
        scratch[6 * n : 6 * n + 8, :] = final[8 * n : 8 * n + 8]
    out_ref[...] = scratch[0:288, :].reshape(6, 48, H).astype(BF16)


def squeeze_matrix():
    places = np.arange(256).reshape(2, 2, 2, 4, 8)[..., :6].transpose(3, 4, 0, 1, 2).reshape(-1)
    block = np.arange(256)[:, None] == places[None, :]
    return np.kron(np.eye(2, dtype=bool), block).astype(jnp.bfloat16)


def call(kernel, outs, scratch=(), room=48 * 1024, **specs):
    return pl.pallas_call(
        kernel,
        out_shape=[jax.ShapeDtypeStruct(shape, dtype) for shape, dtype in outs],
        scratch_shapes=list(scratch),
        compiler_params=pltpu.CompilerParams(vmem_limit_bytes=room * 1024),
        cost_estimate=pl.CostEstimate(flops=20_000_000, bytes_accessed=1_000_000, transcendentals=100_000),
        **specs,
    )


def shards(pair_field, proj_weight, out_weight, in_gain, out_gain):
    exchange = functools.partial(lax.all_to_all, split_axis=0, concat_axis=0, tiled=True)
    squeeze, stretch = jnp.asarray(squeeze_matrix()), jnp.asarray(squeeze_matrix().T)
    pairs = ((384, H), BF16)
    sides, results = ((HALF, 3, 4, H), BF16), ((HALF, 3, 2, H), BF16)
    block, blocks = ((192, 384), BF16), ((4, 96, 384), BF16)
    padded = pltpu.VMEM((296, H), F32)

    sent, field, gating = call(
        start_kernel,
        [sides, pairs, ((392, H), F32)],
        [
            padded,
            pltpu.VMEM((6, 48, H), BF16),
            pltpu.VMEM((H, 5 * H), BF16),
            pltpu.VMEM((2, H), F32),
            pltpu.VMEM((2, H), F32),
            pltpu.SemaphoreType.DMA((4,)),
        ],
        START_ROOM,
        in_specs=[pl.BlockSpec(memory_space=pltpu.HBM)] * 4,
    )(pair_field, proj_weight, in_gain, out_gain)
    own = exchange(sent, SPREAD)
    both = lax.all_gather(own, "core", axis=0, tiled=False)
    left, right = call(pack_kernel, [block, blocks])(both, squeeze)
    right = exchange(right, "x")
    [back] = call(outgoing_kernel, [results])(left, right, stretch)
    arrived = exchange(back, SPREAD)

    sent, field, next_gating = call(middle_kernel, [sides, pairs, ((384, H), F32)])(
        arrived, field, gating, out_weight, proj_weight
    )
    own = exchange(sent, SPREAD)
    both = lax.all_gather(own, "core", axis=0, tiled=False)
    [parts] = call(incoming_kernel, [blocks])(own, both, squeeze)
    parts = exchange(parts, "x")
    [back] = call(sum_kernel, [results])(parts, stretch)
    arrived = exchange(back, SPREAD)
    [out] = call(end_kernel, [((6, 48, H), BF16)], [padded])(
        arrived, field, next_gating, out_weight, gating
    )
    return out


def solution(mesh):
    fine = Mesh(mesh.devices.reshape(2, 2, 2, 2, 4, 4, 2), ("yh", "z2", "z1", "z0", "x", "yl", "core"))
    row, col = ("yh", "z2", "z1", "z0", "x"), ("yl", "core")
    return jax.shard_map(
        shards,
        mesh=fine,
        in_specs=(P(row, col, None), P(), P(), P(), P()),
        out_specs=P(row, col, None),
        check_vma=False,
    )
```

```python
import functools

import jax
import jax.numpy as jnp
import numpy as np
from jax import lax
from jax.experimental import pallas as pl
from jax.experimental.pallas import tpu as pltpu
from jax.sharding import Mesh
from jax.sharding import PartitionSpec as P

H = 128
HALF = 64
SPREAD = ("yl", "z1", "yh", "z2", "z0")
SPREAD_NEXT = ("yl", "x", "yh", "z0")
GATHER_NEXT = ("z1", "z2", *SPREAD_NEXT)
START_ROOM = 60 * 1024
F32 = jnp.float32
BF16 = jnp.bfloat16


def normalize(values, gain, axis):
    mean = jnp.mean(values, axis=axis, keepdims=True)
    centred = values - mean
    spread = jnp.mean(centred * centred, axis=axis, keepdims=True)
    return centred * lax.rsqrt(spread + 1e-05) * gain


def halves(top, bottom):
    low = lax.broadcasted_iota(jnp.int32, top.shape, 1) < HALF
    return jnp.where(low, top, pltpu.roll(bottom, HALF, 1)), jnp.where(low, pltpu.roll(top, HALF, 1), bottom)


def by_device(rows):
    return jnp.swapaxes(jnp.stack(rows, axis=0), 0, 1)


def widen_groups(values, scratch):
    scratch[0:288, :] = values
    keep = lax.broadcasted_iota(jnp.int32, (8, H), 0) < 6
    return jnp.concatenate(
        [jnp.where(keep, scratch[6 * n : 6 * n + 8, :], 0.0) for n in range(48)], axis=0
    )


def spread_sides(normed, weight):
    projected = lax.dot_general(
        weight[:, : 4 * H], normed, (((0,), (1,)), ((), ())), preferred_element_type=F32
    )
    rows = []
    for side in range(2):
        value = projected[2 * side * H : (2 * side + 1) * H]
        gate = projected[(2 * side + 1) * H : (2 * side + 2) * H]
        turned = jax.nn.sigmoid(gate) * value
        for channel in range(2):
            part = turned[channel * HALF : (channel + 1) * HALF]
            rows.extend(part[:, t * H : (t + 1) * H] for t in range(3))
    return by_device(rows).reshape(HALF, 3, 4, H).astype(BF16)


def gate_of(normed, weight):
    return jax.nn.sigmoid(jnp.dot(normed, weight[:, 4 * H :], preferred_element_type=F32))


def finish(arrived, field, gating, weight, gain):
    devices = arrived.shape[0]
    by_row = jnp.swapaxes(arrived.astype(F32).reshape(devices, 6, H), 0, 1)
    by_row = sum(by_row[:, at : at + HALF] for at in range(0, devices, HALF))
    summed = jnp.concatenate(
        [jnp.concatenate([by_row[3 * channel + t] for t in range(3)], axis=1) for channel in range(2)], axis=0
    )
    column = jnp.swapaxes(jnp.broadcast_to(gain, (8, H)), 0, 1)[:, :1]
    mixed = normalize(summed, column, 0).astype(BF16)
    update = lax.dot_general(
        mixed, weight, (((0,), (0,)), ((), ())), preferred_element_type=F32
    )
    return field.astype(F32) + gating * update


def rows_of(own):
    return jnp.swapaxes(own.astype(F32).reshape(HALF, 12, H), 0, 1)


def matrix(by_row, side, channel):
    found = ([], [])
    for t in range(3):
        part = by_row[6 * side + 3 * channel + t]
        tiles = [halves(part[32 * u : 32 * u + 16], part[32 * u + 16 : 32 * u + 32]) for u in range(2)]
        for e in range(2):
            both = jnp.concatenate([tile[e] for tile in tiles], axis=1)
            for z1 in range(2):
                found[z1].append(both[8 * z1 : 8 * z1 + 8])
    return [jnp.concatenate(pieces, axis=0) for pieces in found]


def whole_matrix(cores, side, channel):
    parts = [matrix(by_row, side, channel) for by_row in cores]
    return [jnp.concatenate([parts[0][z1], parts[1][z1]], axis=1) for z1 in range(2)]


def squeezed(rows, squeeze):
    return jnp.dot(
        jnp.concatenate(rows, axis=0).astype(BF16), squeeze, preferred_element_type=F32
    ).astype(BF16)


def send_back(product, stretch):
    wide = jnp.dot(product.astype(BF16), stretch, preferred_element_type=F32)
    rows = []
    for channel in range(2):
        for t in range(3):
            parts = []
            for u in range(2):
                lanes = slice((2 * channel + u) * H, (2 * channel + u + 1) * H)
                pair = [
                    jnp.concatenate([wide[8 * a : 8 * a + 8, lanes], wide[48 + 8 * a : 56 + 8 * a, lanes]], axis=0)
                    for a in (2 * t, 2 * t + 1)
                ]
                parts.extend(halves(*pair))
            rows.append(jnp.concatenate(parts, axis=0))
    return by_device(rows).reshape(HALF, 3, 2, H).astype(BF16)


def start_kernel(
    pair_hbm, weight_hbm, gain_hbm, out_gain_hbm,
    out_ref, field_ref, gate_ref,
    scratch, pair_ref, weight_ref, gain_ref, out_gain_ref, sems,
):
    moves = [
        (pair_hbm, pair_ref),
        (gain_hbm, gain_ref),
        (weight_hbm.at[0], weight_ref),
        (out_gain_hbm, out_gain_ref),
    ]
    copies = [pltpu.make_async_copy(source, target, sems.at[n]) for n, (source, target) in enumerate(moves)]
    for copy in copies:
        copy.start()
    copies[0].wait()
    field = widen_groups(pair_ref[...].reshape(288, H).astype(F32), scratch)
    field_ref[...] = field.astype(BF16)
    copies[1].wait()
    normed = normalize(field, gain_ref[0:1, :], 1).astype(BF16)
    copies[2].wait()
    weight = weight_ref[...]
    out_ref[...] = spread_sides(normed, weight)
    gate_ref[:384] = gate_of(normed, weight)
    copies[3].wait()
    gate_ref[384:392] = jnp.concatenate([gain_ref[...], out_gain_ref[...], jnp.zeros((4, H), F32)], axis=0)


def pack_kernel(both_ref, squeeze_ref, left_ref, right_ref):
    cores = [rows_of(both_ref[core]) for core in range(2)]
    first = lax.axis_index("core") == 0
    rows = []
    for channel in range(2):
        rows.extend(whole_matrix(cores, 0, channel))
    for channel in range(2):
        rows.append(jnp.where(first, *whole_matrix(cores, 1, channel)))
    packed = squeezed(rows, squeeze_ref[...])
    left_ref[...] = packed[:192]
    for x in range(4):
        right_ref[x] = packed[192:]


def outgoing_kernel(left_ref, right_ref, stretch_ref, out_ref):
    left = jnp.concatenate([left_ref[:96], left_ref[96:]], axis=1)
    none = jnp.zeros((192, 384), BF16)
    right = [right_ref[:, 48 * channel : 48 * channel + 48].reshape(192, 384) for channel in range(2)]
    right = jnp.concatenate(
        [jnp.concatenate([right[0], none], axis=1), jnp.concatenate([none, right[1]], axis=1)], axis=0
    )
    product = lax.dot_general(left, right, (((1,), (1,)), ((), ())), preferred_element_type=F32)
    out_ref[...] = send_back(product, stretch_ref[...])


def middle_kernel(
    arrived_ref, field_ref, gate_ref, out_weight_ref, weight_ref, out_ref, first_ref, next_gate_ref
):
    first = finish(
        arrived_ref[...], field_ref[...], gate_ref[:384], out_weight_ref[0], gate_ref[386:387]
    ).astype(BF16)
    normed = normalize(first.astype(F32), gate_ref[385:386], 1).astype(BF16)
    weight = weight_ref[1]
    out_ref[...] = spread_sides(normed, weight)
    first_ref[...] = first
    next_gate_ref[...] = gate_of(normed, weight)


def incoming_kernel(own_ref, both_ref, squeeze_ref, out_ref):
    cores = [rows_of(both_ref[core]) for core in range(2)]
    own = rows_of(own_ref[...])
    none = jnp.zeros((96, 256), F32)
    left, right = [], []
    for channel in range(2):
        left.extend(whole_matrix(cores, 0, channel))
        part = jnp.concatenate(matrix(own, 1, channel), axis=0)
        right.append(jnp.concatenate([none, part] if channel else [part, none], axis=1))
    wide = lax.dot_general(
        squeezed(left, squeeze_ref[...]),
        jnp.concatenate(right, axis=0).astype(BF16),
        (((0,), (0,)), ((), ())),
        preferred_element_type=F32,
    )
    rows = []
    for channel in range(2):
        for t in range(3):
            found = []
            for u in range(2):
                lanes = slice((2 * channel + u) * H, (2 * channel + u + 1) * H)
                pair = [
                    jnp.concatenate([wide[32 * a : 32 * a + 32, lanes], wide[192 + 32 * a : 224 + 32 * a, lanes]], axis=0)
                    for a in (2 * t, 2 * t + 1)
                ]
                found.extend(halves(*pair))
            rows.append(
                jnp.concatenate([part[16 * z : 16 * z + 16] for z in range(4) for part in found], axis=0)
            )
    out_ref[...] = by_device(rows).reshape(256, 3, 2, H).astype(BF16)


def end_kernel(arrived_ref, field_ref, gate_ref, out_weight_ref, gains_ref, out_ref, scratch):
    final = finish(
        arrived_ref[...], field_ref[...], gate_ref[...], out_weight_ref[1], gains_ref[387:388]
    )
    for n in range(48):
        scratch[6 * n : 6 * n + 8, :] = final[8 * n : 8 * n + 8]
    out_ref[...] = scratch[0:288, :].reshape(6, 48, H).astype(BF16)


def squeeze_matrix(order):
    places = np.arange(256).reshape(2, 2, 2, 4, 8)[..., :6].transpose(order).reshape(-1)
    block = np.arange(256)[:, None] == places[None, :]
    return np.kron(np.eye(2, dtype=bool), block).astype(jnp.bfloat16)


def call(kernel, outs, scratch=(), room=48 * 1024, **specs):
    return pl.pallas_call(
        kernel,
        out_shape=[jax.ShapeDtypeStruct(shape, dtype) for shape, dtype in outs],
        scratch_shapes=list(scratch),
        compiler_params=pltpu.CompilerParams(vmem_limit_bytes=room * 1024),
        cost_estimate=pl.CostEstimate(flops=20_000_000, bytes_accessed=1_000_000, transcendentals=100_000),
        **specs,
    )


def shards(pair_field, proj_weight, out_weight, in_gain, out_gain):
    exchange = functools.partial(lax.all_to_all, split_axis=0, concat_axis=0, tiled=True)
    squeeze = jnp.asarray(squeeze_matrix((4, 1, 3, 0, 2)))
    stretch = jnp.asarray(squeeze_matrix((3, 4, 0, 1, 2)).T)
    pairs = ((384, H), BF16)
    sides, results = ((HALF, 3, 4, H), BF16), ((HALF, 3, 2, H), BF16)
    block, blocks = ((192, 384), BF16), ((4, 96, 384), BF16)
    padded = pltpu.VMEM((296, H), F32)

    sent, field, gating = call(
        start_kernel,
        [sides, pairs, ((392, H), F32)],
        [
            padded,
            pltpu.VMEM((6, 48, H), BF16),
            pltpu.VMEM((H, 5 * H), BF16),
            pltpu.VMEM((2, H), F32),
            pltpu.VMEM((2, H), F32),
            pltpu.SemaphoreType.DMA((4,)),
        ],
        START_ROOM,
        in_specs=[pl.BlockSpec(memory_space=pltpu.HBM)] * 4,
    )(pair_field, proj_weight, in_gain, out_gain)
    own = exchange(sent, SPREAD)
    both = lax.all_gather(own, "core", axis=0, tiled=False)
    left, right = call(pack_kernel, [block, blocks])(both, squeeze)
    right = exchange(right, "x")
    [back] = call(outgoing_kernel, [results])(left, right, stretch)
    arrived = exchange(back, SPREAD)

    sent, field, next_gating = call(middle_kernel, [sides, pairs, ((384, H), F32)])(
        arrived, field, gating, out_weight, proj_weight
    )
    own = exchange(sent, SPREAD_NEXT)
    both = lax.all_gather(own, "core", axis=0, tiled=False)
    [parts] = call(incoming_kernel, [((256, 3, 2, H), BF16)])(own, both, squeeze)
    arrived = exchange(parts, GATHER_NEXT)
    [out] = call(end_kernel, [((6, 48, H), BF16)], [padded])(
        arrived, field, next_gating, out_weight, gating
    )
    return out


def solution(mesh):
    fine = Mesh(mesh.devices.reshape(2, 2, 2, 2, 4, 4, 2), ("yh", "z2", "z1", "z0", "x", "yl", "core"))
    row, col = ("yh", "z2", "z1", "z0", "x"), ("yl", "core")
    return jax.shard_map(
        shards,
        mesh=fine,
        in_specs=(P(row, col, None), P(), P(), P(), P()),
        out_specs=P(row, col, None),
        check_vma=False,
    )
```

```python
import functools

import jax
import jax.numpy as jnp
import numpy as np
from jax import lax
from jax.experimental import pallas as pl
from jax.experimental.pallas import tpu as pltpu
from jax.sharding import Mesh
from jax.sharding import PartitionSpec as P

H = 128
HALF = 64
SPREAD = ("yl", "z1", "yh", "z2", "z0")
SPREAD_NEXT = ("yl", "yh", "z0", "x")
GATHER_NEXT = ("yl", "yh", "z2", "z1", "z0", "x")
START_ROOM = 60 * 1024
F32 = jnp.float32
BF16 = jnp.bfloat16


def normalize(values, gain, axis):
    mean = jnp.mean(values, axis=axis, keepdims=True)
    centred = values - mean
    spread = jnp.mean(centred * centred, axis=axis, keepdims=True)
    return centred * lax.rsqrt(spread + 1e-05) * gain


def halves(top, bottom):
    low = lax.broadcasted_iota(jnp.int32, top.shape, 1) < HALF
    return jnp.where(low, top, pltpu.roll(bottom, HALF, 1)), jnp.where(low, pltpu.roll(top, HALF, 1), bottom)


def by_device(rows):
    return jnp.swapaxes(jnp.stack(rows, axis=0), 0, 1)


def widen_groups(values, scratch):
    scratch[0:288, :] = values
    keep = lax.broadcasted_iota(jnp.int32, (8, H), 0) < 6
    return jnp.concatenate(
        [jnp.where(keep, scratch[6 * n : 6 * n + 8, :], 0.0) for n in range(48)], axis=0
    )


def spread_sides(normed, weight):
    projected = lax.dot_general(
        weight[:, : 4 * H], normed, (((0,), (1,)), ((), ())), preferred_element_type=F32
    )
    rows = []
    for side in range(2):
        value = projected[2 * side * H : (2 * side + 1) * H]
        gate = projected[(2 * side + 1) * H : (2 * side + 2) * H]
        turned = jax.nn.sigmoid(gate) * value
        for channel in range(2):
            part = turned[channel * HALF : (channel + 1) * HALF]
            rows.extend(part[:, t * H : (t + 1) * H] for t in range(3))
    return by_device(rows).reshape(HALF, 3, 4, H).astype(BF16)


def gate_of(normed, weight):
    return jax.nn.sigmoid(jnp.dot(normed, weight[:, 4 * H :], preferred_element_type=F32))


def finish(arrived, field, gating, weight, gain):
    parts = arrived.shape[0] // HALF
    total = arrived.astype(F32).reshape(8, parts, 8, 3, 2, H)
    total = sum(total[:, n] for n in range(parts)).reshape(HALF, 6, H)
    by_row = jnp.swapaxes(total, 0, 1)
    summed = jnp.concatenate(
        [jnp.concatenate([by_row[3 * channel + t] for t in range(3)], axis=1) for channel in range(2)], axis=0
    )
    column = jnp.swapaxes(jnp.broadcast_to(gain, (8, H)), 0, 1)[:, :1]
    mixed = normalize(summed, column, 0).astype(BF16)
    update = lax.dot_general(
        mixed, weight, (((0,), (0,)), ((), ())), preferred_element_type=F32
    )
    return field.astype(F32) + gating * update


def rows_of(own):
    return jnp.swapaxes(own.astype(F32).reshape(HALF, 12, H), 0, 1)


def matrix(by_row, side, channel):
    found = ([], [])
    for t in range(3):
        part = by_row[6 * side + 3 * channel + t]
        tiles = [halves(part[32 * u : 32 * u + 16], part[32 * u + 16 : 32 * u + 32]) for u in range(2)]
        for e in range(2):
            both = jnp.concatenate([tile[e] for tile in tiles], axis=1)
            for z1 in range(2):
                found[z1].append(both[8 * z1 : 8 * z1 + 8])
    return [jnp.concatenate(pieces, axis=0) for pieces in found]


def whole_matrix(cores, side, channel):
    parts = [matrix(by_row, side, channel) for by_row in cores]
    return [jnp.concatenate([parts[0][z1], parts[1][z1]], axis=1) for z1 in range(2)]


def squeezed(rows, squeeze):
    return jnp.dot(
        jnp.concatenate(rows, axis=0).astype(BF16), squeeze, preferred_element_type=F32
    ).astype(BF16)


def send_back(product, stretch):
    wide = jnp.dot(product.astype(BF16), stretch, preferred_element_type=F32)
    rows = []
    for channel in range(2):
        for t in range(3):
            parts = []
            for u in range(2):
                lanes = slice((2 * channel + u) * H, (2 * channel + u + 1) * H)
                pair = [
                    jnp.concatenate([wide[8 * a : 8 * a + 8, lanes], wide[48 + 8 * a : 56 + 8 * a, lanes]], axis=0)
                    for a in (2 * t, 2 * t + 1)
                ]
                parts.extend(halves(*pair))
            rows.append(jnp.concatenate(parts, axis=0))
    return by_device(rows).reshape(HALF, 3, 2, H).astype(BF16)


def start_kernel(
    pair_hbm, weight_hbm, gain_hbm, out_gain_hbm,
    out_ref, field_ref, gate_ref,
    scratch, pair_ref, weight_ref, gain_ref, out_gain_ref, sems,
):
    moves = [
        (pair_hbm, pair_ref),
        (gain_hbm, gain_ref),
        (weight_hbm.at[0], weight_ref),
        (out_gain_hbm, out_gain_ref),
    ]
    copies = [pltpu.make_async_copy(source, target, sems.at[n]) for n, (source, target) in enumerate(moves)]
    for copy in copies:
        copy.start()
    copies[0].wait()
    field = widen_groups(pair_ref[...].reshape(288, H).astype(F32), scratch)
    field_ref[...] = field.astype(BF16)
    copies[1].wait()
    normed = normalize(field, gain_ref[0:1, :], 1).astype(BF16)
    copies[2].wait()
    weight = weight_ref[...]
    out_ref[...] = spread_sides(normed, weight)
    gate_ref[:384] = gate_of(normed, weight)
    copies[3].wait()
    gate_ref[384:392] = jnp.concatenate([gain_ref[...], out_gain_ref[...], jnp.zeros((4, H), F32)], axis=0)


def pack_kernel(both_ref, squeeze_ref, left_ref, right_ref):
    cores = [rows_of(both_ref[core]) for core in range(2)]
    first = lax.axis_index("core") == 0
    rows = []
    for channel in range(2):
        rows.extend(whole_matrix(cores, 0, channel))
    for channel in range(2):
        rows.append(jnp.where(first, *whole_matrix(cores, 1, channel)))
    packed = squeezed(rows, squeeze_ref[...])
    left_ref[...] = packed[:192]
    for x in range(4):
        right_ref[x] = packed[192:]


def outgoing_kernel(left_ref, right_ref, stretch_ref, out_ref):
    left = jnp.concatenate([left_ref[:96], left_ref[96:]], axis=1)
    none = jnp.zeros((192, 384), BF16)
    right = [right_ref[:, 48 * channel : 48 * channel + 48].reshape(192, 384) for channel in range(2)]
    right = jnp.concatenate(
        [jnp.concatenate([right[0], none], axis=1), jnp.concatenate([none, right[1]], axis=1)], axis=0
    )
    product = lax.dot_general(left, right, (((1,), (1,)), ((), ())), preferred_element_type=F32)
    out_ref[...] = send_back(product, stretch_ref[...])


def middle_kernel(
    arrived_ref, field_ref, gate_ref, out_weight_ref, weight_ref, out_ref, first_ref, next_gate_ref
):
    first = finish(
        arrived_ref[...], field_ref[...], gate_ref[:384], out_weight_ref[0], gate_ref[386:387]
    ).astype(BF16)
    normed = normalize(first.astype(F32), gate_ref[385:386], 1).astype(BF16)
    weight = weight_ref[1]
    out_ref[...] = spread_sides(normed, weight)
    first_ref[...] = first
    next_gate_ref[...] = gate_of(normed, weight)


def incoming_kernel(own_ref, both_ref, squeeze_ref, out_ref):
    cores = [rows_of(both_ref[core]) for core in range(2)]
    own = rows_of(own_ref[...])
    none = jnp.zeros((96, 256), F32)
    left, right = [], []
    for channel in range(2):
        left.extend(whole_matrix(cores, 0, channel))
        part = jnp.concatenate(matrix(own, 1, channel), axis=0)
        right.append(jnp.concatenate([none, part] if channel else [part, none], axis=1))
    wide = lax.dot_general(
        squeezed(left, squeeze_ref[...]),
        jnp.concatenate(right, axis=0).astype(BF16),
        (((0,), (0,)), ((), ())),
        preferred_element_type=F32,
    )
    rows = []
    for channel in range(2):
        for t in range(3):
            found = []
            for u in range(2):
                lanes = slice((2 * channel + u) * H, (2 * channel + u + 1) * H)
                pair = [
                    jnp.concatenate([wide[32 * a : 32 * a + 32, lanes], wide[192 + 32 * a : 224 + 32 * a, lanes]], axis=0)
                    for a in (2 * t, 2 * t + 1)
                ]
                found.extend(halves(*pair))
            at = [32 * z1 + 8 * pair for pair in range(4) for z1 in range(2)]
            rows.append(jnp.concatenate([part[n : n + 8] for part in found for n in at], axis=0))
    out_ref[...] = by_device(rows).reshape(256, 3, 2, H).astype(BF16)


def end_kernel(arrived_ref, field_ref, gate_ref, out_weight_ref, gains_ref, out_ref, scratch):
    final = finish(
        arrived_ref[...], field_ref[...], gate_ref[...], out_weight_ref[1], gains_ref[387:388]
    )
    for n in range(48):
        scratch[6 * n : 6 * n + 8, :] = final[8 * n : 8 * n + 8]
    out_ref[...] = scratch[0:288, :].reshape(6, 48, H).astype(BF16)


def squeeze_matrix(order):
    places = np.arange(256).reshape(2, 2, 2, 4, 8)[..., :6].transpose(order).reshape(-1)
    block = np.arange(256)[:, None] == places[None, :]
    return np.kron(np.eye(2, dtype=bool), block).astype(jnp.bfloat16)


def call(kernel, outs, scratch=(), room=48 * 1024, **specs):
    return pl.pallas_call(
        kernel,
        out_shape=[jax.ShapeDtypeStruct(shape, dtype) for shape, dtype in outs],
        scratch_shapes=list(scratch),
        compiler_params=pltpu.CompilerParams(vmem_limit_bytes=room * 1024),
        cost_estimate=pl.CostEstimate(flops=20_000_000, bytes_accessed=1_000_000, transcendentals=100_000),
        **specs,
    )


def shards(pair_field, proj_weight, out_weight, in_gain, out_gain):
    exchange = functools.partial(lax.all_to_all, split_axis=0, concat_axis=0, tiled=True)
    squeeze = jnp.asarray(squeeze_matrix((4, 0, 1, 2, 3)))
    stretch = jnp.asarray(squeeze_matrix((3, 4, 0, 1, 2)).T)
    pairs = ((384, H), BF16)
    sides, results = ((HALF, 3, 4, H), BF16), ((HALF, 3, 2, H), BF16)
    block, blocks = ((192, 384), BF16), ((4, 96, 384), BF16)
    padded = pltpu.VMEM((296, H), F32)

    sent, field, gating = call(
        start_kernel,
        [sides, pairs, ((392, H), F32)],
        [
            padded,
            pltpu.VMEM((6, 48, H), BF16),
            pltpu.VMEM((H, 5 * H), BF16),
            pltpu.VMEM((2, H), F32),
            pltpu.VMEM((2, H), F32),
            pltpu.SemaphoreType.DMA((4,)),
        ],
        START_ROOM,
        in_specs=[pl.BlockSpec(memory_space=pltpu.HBM)] * 4,
    )(pair_field, proj_weight, in_gain, out_gain)
    own = exchange(sent, SPREAD)
    both = lax.all_gather(own, "core", axis=0, tiled=False)
    left, right = call(pack_kernel, [block, blocks])(both, squeeze)
    right = exchange(right, "x")
    [back] = call(outgoing_kernel, [results])(left, right, stretch)
    arrived = exchange(back, SPREAD)

    sent, field, next_gating = call(middle_kernel, [sides, pairs, ((384, H), F32)])(
        arrived, field, gating, out_weight, proj_weight
    )
    own = exchange(sent, SPREAD_NEXT)
    both = lax.all_gather(own, "core", axis=0, tiled=False)
    [parts] = call(incoming_kernel, [((256, 3, 2, H), BF16)])(own, both, squeeze)
    arrived = exchange(parts, GATHER_NEXT)
    [out] = call(end_kernel, [((6, 48, H), BF16)], [padded])(
        arrived, field, next_gating, out_weight, gating
    )
    return out


def solution(mesh):
    fine = Mesh(mesh.devices.reshape(2, 2, 2, 2, 4, 4, 2), ("yh", "z2", "z1", "z0", "x", "yl", "core"))
    row, col = ("yh", "z2", "z1", "z0", "x"), ("yl", "core")
    return jax.shard_map(
        shards,
        mesh=fine,
        in_specs=(P(row, col, None), P(), P(), P(), P()),
        out_specs=P(row, col, None),
        check_vma=False,
    )
```

```python
import functools

import jax
import jax.numpy as jnp
import numpy as np
from jax import lax
from jax.experimental import pallas as pl
from jax.experimental.pallas import tpu as pltpu
from jax.sharding import Mesh
from jax.sharding import PartitionSpec as P

H = 128
HALF = 64
SPREAD = ("yl", "z1", "yh", "z2", "z0")
F32 = jnp.float32
BF16 = jnp.bfloat16


def normalize(values, gain, axis):
    mean = jnp.mean(values, axis=axis, keepdims=True)
    centred = values - mean
    spread = jnp.mean(centred * centred, axis=axis, keepdims=True)
    return centred * lax.rsqrt(spread + 1e-05) * gain


def halves(top, bottom):
    low = lax.broadcasted_iota(jnp.int32, top.shape, 1) < HALF
    return jnp.where(low, top, pltpu.roll(bottom, HALF, 1)), jnp.where(low, pltpu.roll(top, HALF, 1), bottom)


def by_device(rows):
    return jnp.swapaxes(jnp.stack(rows, axis=0), 0, 1)


def widen_groups(values, scratch):
    scratch[0:288, :] = values
    keep = lax.broadcasted_iota(jnp.int32, (8, H), 0) < 6
    return jnp.concatenate(
        [jnp.where(keep, scratch[6 * n : 6 * n + 8, :], 0.0) for n in range(48)], axis=0
    )


def spread_sides(normed, weight):
    projected = lax.dot_general(
        weight[:, : 4 * H], normed, (((0,), (1,)), ((), ())), preferred_element_type=F32
    )
    rows = []
    for side in range(2):
        value = projected[2 * side * H : (2 * side + 1) * H]
        gate = projected[(2 * side + 1) * H : (2 * side + 2) * H]
        turned = jax.nn.sigmoid(gate) * value
        for channel in range(2):
            part = turned[channel * HALF : (channel + 1) * HALF]
            rows.extend(part[:, t * H : (t + 1) * H] for t in range(3))
    return by_device(rows).reshape(HALF, 3, 4, H).astype(BF16)


def gate_of(normed, weight):
    return jax.nn.sigmoid(jnp.dot(normed, weight[:, 4 * H :], preferred_element_type=F32))


def finish(arrived, field, gating, weight, gain):
    by_row = jnp.swapaxes(arrived.astype(F32).reshape(HALF, 6, H), 0, 1)
    summed = jnp.concatenate(
        [jnp.concatenate([by_row[3 * channel + t] for t in range(3)], axis=1) for channel in range(2)], axis=0
    )
    column = jnp.swapaxes(jnp.broadcast_to(gain, (8, H)), 0, 1)[:, :1]
    mixed = normalize(summed, column, 0).astype(BF16)
    update = lax.dot_general(
        mixed, weight, (((0,), (0,)), ((), ())), preferred_element_type=F32
    )
    return field.astype(F32) + gating * update


def rows_of(own):
    return jnp.swapaxes(own.astype(F32).reshape(HALF, 12, H), 0, 1)


def matrix(by_row, side, channel):
    found = ([], [])
    for t in range(3):
        part = by_row[6 * side + 3 * channel + t]
        tiles = [halves(part[32 * u : 32 * u + 16], part[32 * u + 16 : 32 * u + 32]) for u in range(2)]
        for e in range(2):
            both = jnp.concatenate([tile[e] for tile in tiles], axis=1)
            for z1 in range(2):
                found[z1].append(both[8 * z1 : 8 * z1 + 8])
    return [jnp.concatenate(pieces, axis=0) for pieces in found]


def whole_matrix(cores, side, channel):
    parts = [matrix(by_row, side, channel) for by_row in cores]
    return [jnp.concatenate([parts[0][z1], parts[1][z1]], axis=1) for z1 in range(2)]


def squeezed(rows, squeeze):
    return jnp.dot(
        jnp.concatenate(rows, axis=0).astype(BF16), squeeze, preferred_element_type=F32
    ).astype(BF16)


def send_back(wide):
    rows = []
    for channel in range(2):
        for t in range(3):
            parts = []
            for u in range(2):
                lanes = slice((2 * channel + u) * H, (2 * channel + u + 1) * H)
                pair = [
                    jnp.concatenate([wide[8 * a : 8 * a + 8, lanes], wide[48 + 8 * a : 56 + 8 * a, lanes]], axis=0)
                    for a in (2 * t, 2 * t + 1)
                ]
                parts.extend(halves(*pair))
            rows.append(jnp.concatenate(parts, axis=0))
    return by_device(rows).reshape(HALF, 3, 2, H).astype(BF16)


def start_kernel(pair_ref, weight_ref, gain_ref, out_ref, field_ref, gate_ref, scratch):
    field = widen_groups(pair_ref[...].reshape(288, H).astype(F32), scratch)
    field_ref[...] = field.astype(BF16)
    normed = normalize(field, gain_ref[...], 1).astype(BF16)
    weight = weight_ref[...]
    out_ref[...] = spread_sides(normed, weight)
    gate_ref[...] = gate_of(normed, weight)


def pack_kernel(both_ref, squeeze_ref, left_ref, right_ref):
    cores = [rows_of(both_ref[core]) for core in range(2)]
    first = lax.axis_index("core") == 0
    rows = []
    for channel in range(2):
        rows.extend(whole_matrix(cores, 0, channel))
    for channel in range(2):
        rows.append(jnp.where(first, *whole_matrix(cores, 1, channel)))
    packed = squeezed(rows, squeeze_ref[...])
    left_ref[...] = packed[:192]
    for x in range(4):
        right_ref[x] = packed[192:]


def outgoing_kernel(left_ref, right_ref, stretch_ref, out_ref):
    wide = []
    for channel in range(2):
        product = lax.dot_general(
            left_ref[96 * channel : 96 * channel + 96],
            right_ref[:, 48 * channel : 48 * channel + 48].reshape(192, 384),
            (((1,), (1,)), ((), ())),
            preferred_element_type=F32,
        ).astype(BF16)
        wide.append(jnp.dot(product, stretch_ref[:192, :256], preferred_element_type=F32))
    out_ref[...] = send_back(jnp.concatenate(wide, axis=1))


def middle_kernel(
    arrived_ref, field_ref, gate_ref, out_weight_ref, out_gain_ref, weight_ref, gain_ref, out_ref, first_ref, next_gate_ref
):
    first = finish(
        arrived_ref[...], field_ref[...], gate_ref[...], out_weight_ref[0], out_gain_ref[...]
    ).astype(BF16)
    normed = normalize(first.astype(F32), gain_ref[...], 1).astype(BF16)
    weight = weight_ref[...]
    out_ref[...] = spread_sides(normed, weight)
    first_ref[...] = first
    next_gate_ref[...] = gate_of(normed, weight)


def incoming_kernel(own_ref, both_ref, squeeze_ref, out_ref):
    cores = [rows_of(both_ref[core]) for core in range(2)]
    own = rows_of(own_ref[...])
    none = jnp.zeros((96, 256), F32)
    rows = []
    for channel in range(2):
        rows.extend(whole_matrix(cores, 0, channel))
    for channel in range(2):
        part = jnp.concatenate(matrix(own, 1, channel), axis=0)
        rows.append(jnp.concatenate([none, part] if channel else [part, none], axis=1))
    packed = squeezed(rows, squeeze_ref[...])
    product = lax.dot_general(
        packed[:192], packed[192:], (((0,), (0,)), ((), ())), preferred_element_type=F32
    ).astype(BF16)
    for x in range(4):
        for z1 in range(2):
            at = 192 * z1 + 48 * x
            out_ref[x, 48 * z1 : 48 * z1 + 48] = product[at : at + 48]


def sum_kernel(parts_ref, stretch_ref, out_ref):
    total = parts_ref[0].astype(F32)
    for x in range(1, 4):
        total = total + parts_ref[x].astype(F32)
    out_ref[...] = send_back(jnp.dot(total.astype(BF16), stretch_ref[...], preferred_element_type=F32))


def end_kernel(arrived_ref, field_ref, gate_ref, out_weight_ref, gain_ref, out_ref, scratch):
    final = finish(
        arrived_ref[...], field_ref[...], gate_ref[...], out_weight_ref[1], gain_ref[...]
    )
    for n in range(48):
        scratch[6 * n : 6 * n + 8, :] = final[8 * n : 8 * n + 8]
    out_ref[...] = scratch[0:288, :].reshape(6, 48, H).astype(BF16)


def squeeze_matrix():
    places = np.arange(256).reshape(2, 2, 2, 4, 8)[..., :6].transpose(3, 4, 0, 1, 2).reshape(-1)
    block = np.arange(256)[:, None] == places[None, :]
    return np.kron(np.eye(2, dtype=bool), block).astype(jnp.bfloat16)


def call(kernel, outs, scratch=()):
    return pl.pallas_call(
        kernel,
        out_shape=[jax.ShapeDtypeStruct(shape, dtype) for shape, dtype in outs],
        scratch_shapes=list(scratch),
        compiler_params=pltpu.CompilerParams(vmem_limit_bytes=48 * 1024 * 1024),
        cost_estimate=pl.CostEstimate(flops=20_000_000, bytes_accessed=1_000_000, transcendentals=100_000),
    )


def shards(pair_field, proj_weight, out_weight, in_gain, out_gain):
    exchange = functools.partial(lax.all_to_all, split_axis=0, concat_axis=0, tiled=True)
    squeeze, stretch = jnp.asarray(squeeze_matrix()), jnp.asarray(squeeze_matrix().T)
    pairs, gates = ((384, H), BF16), ((384, H), F32)
    sides, results = ((HALF, 3, 4, H), BF16), ((HALF, 3, 2, H), BF16)
    block, blocks = ((192, 384), BF16), ((4, 96, 384), BF16)
    padded = pltpu.VMEM((296, H), F32)

    sent, field, gating = call(start_kernel, [sides, pairs, gates], [padded])(
        pair_field, proj_weight[0], in_gain[:1]
    )
    own = exchange(sent, SPREAD)
    both = lax.all_gather(own, "core", axis=0, tiled=False)
    left, right = call(pack_kernel, [block, blocks])(both, squeeze)
    right = exchange(right, "x")
    [back] = call(outgoing_kernel, [results])(left, right, stretch)
    arrived = exchange(back, SPREAD)

    sent, field, gating = call(middle_kernel, [sides, pairs, gates])(
        arrived, field, gating, out_weight, out_gain[:1], proj_weight[1], in_gain[1:]
    )
    own = exchange(sent, SPREAD)
    both = lax.all_gather(own, "core", axis=0, tiled=False)
    [parts] = call(incoming_kernel, [blocks])(own, both, squeeze)
    parts = exchange(parts, "x")
    [back] = call(sum_kernel, [results])(parts, stretch)
    arrived = exchange(back, SPREAD)
    [out] = call(end_kernel, [((6, 48, H), BF16)], [padded])(
        arrived, field, gating, out_weight, out_gain[1:]
    )
    return out


def solution(mesh):
    fine = Mesh(mesh.devices.reshape(2, 2, 2, 2, 4, 4, 2), ("yh", "z2", "z1", "z0", "x", "yl", "core"))
    row, col = ("yh", "z2", "z1", "z0", "x"), ("yl", "core")
    return jax.shard_map(
        shards,
        mesh=fine,
        in_specs=(P(row, col, None), P(), P(), P(), P()),
        out_specs=P(row, col, None),
        check_vma=False,
    )
```

```python
import functools

import jax
import jax.numpy as jnp
import numpy as np
from jax import lax
from jax.experimental import pallas as pl
from jax.experimental.pallas import tpu as pltpu
from jax.sharding import Mesh
from jax.sharding import PartitionSpec as P

H = 128
HALF = 64
SPREAD = ("yl", "z1", "yh", "z2", "z0")
F32 = jnp.float32
BF16 = jnp.bfloat16


def normalize(values, gain, axis):
    mean = jnp.mean(values, axis=axis, keepdims=True)
    centred = values - mean
    spread = jnp.mean(centred * centred, axis=axis, keepdims=True)
    return centred * lax.rsqrt(spread + 1e-05) * gain


def halves(top, bottom):
    low = lax.broadcasted_iota(jnp.int32, top.shape, 1) < HALF
    return jnp.where(low, top, pltpu.roll(bottom, HALF, 1)), jnp.where(low, pltpu.roll(top, HALF, 1), bottom)


def by_device(rows):
    return jnp.swapaxes(jnp.stack(rows, axis=0), 0, 1)


def widen_groups(values, scratch):
    scratch[0:288, :] = values
    keep = lax.broadcasted_iota(jnp.int32, (8, H), 0) < 6
    return jnp.concatenate(
        [jnp.where(keep, scratch[6 * n : 6 * n + 8, :], 0.0) for n in range(48)], axis=0
    )


def spread_sides(normed, weight):
    projected = lax.dot_general(
        weight[:, : 4 * H], normed, (((0,), (1,)), ((), ())), preferred_element_type=F32
    )
    rows = []
    for side in range(2):
        value = projected[2 * side * H : (2 * side + 1) * H]
        gate = projected[(2 * side + 1) * H : (2 * side + 2) * H]
        turned = jax.nn.sigmoid(gate) * value
        for channel in range(2):
            part = turned[channel * HALF : (channel + 1) * HALF]
            rows.extend(part[:, t * H : (t + 1) * H] for t in range(3))
    return by_device(rows).reshape(HALF, 3, 4, H).astype(BF16)


def gate_of(normed, weight):
    return jax.nn.sigmoid(jnp.dot(normed, weight[:, 4 * H :], preferred_element_type=F32))


def finish(arrived, field, gating, weight, gain):
    by_row = jnp.swapaxes(arrived.astype(F32).reshape(HALF, 6, H), 0, 1)
    summed = jnp.concatenate(
        [jnp.concatenate([by_row[3 * channel + t] for t in range(3)], axis=1) for channel in range(2)], axis=0
    )
    column = jnp.swapaxes(jnp.broadcast_to(gain, (8, H)), 0, 1)[:, :1]
    mixed = normalize(summed, column, 0).astype(BF16)
    update = lax.dot_general(
        mixed, weight, (((0,), (0,)), ((), ())), preferred_element_type=F32
    )
    return field.astype(F32) + gating * update


def rows_of(own):
    return jnp.swapaxes(own.astype(F32).reshape(HALF, 12, H), 0, 1)


def matrix(by_row, side, channel):
    found = ([], [])
    for t in range(3):
        part = by_row[6 * side + 3 * channel + t]
        tiles = [halves(part[32 * u : 32 * u + 16], part[32 * u + 16 : 32 * u + 32]) for u in range(2)]
        for e in range(2):
            both = jnp.concatenate([tile[e] for tile in tiles], axis=1)
            for z1 in range(2):
                found[z1].append(both[8 * z1 : 8 * z1 + 8])
    return [jnp.concatenate(pieces, axis=0) for pieces in found]


def whole_matrix(cores, side, channel):
    parts = [matrix(by_row, side, channel) for by_row in cores]
    return [jnp.concatenate([parts[0][z1], parts[1][z1]], axis=1) for z1 in range(2)]


def squeezed(rows, squeeze):
    return jnp.dot(
        jnp.concatenate(rows, axis=0).astype(BF16), squeeze, preferred_element_type=F32
    ).astype(BF16)


def send_back(wide):
    rows = []
    for channel in range(2):
        for t in range(3):
            parts = []
            for u in range(2):
                lanes = slice((2 * channel + u) * H, (2 * channel + u + 1) * H)
                pair = [
                    jnp.concatenate([wide[8 * a : 8 * a + 8, lanes], wide[48 + 8 * a : 56 + 8 * a, lanes]], axis=0)
                    for a in (2 * t, 2 * t + 1)
                ]
                parts.extend(halves(*pair))
            rows.append(jnp.concatenate(parts, axis=0))
    return by_device(rows).reshape(HALF, 3, 2, H).astype(BF16)


def start_kernel(pair_ref, weight_ref, gain_ref, out_ref, field_ref, gate_ref, scratch):
    field = widen_groups(pair_ref[...].reshape(288, H).astype(F32), scratch)
    field_ref[...] = field.astype(BF16)
    normed = normalize(field, gain_ref[0:1], 1).astype(BF16)
    weight = weight_ref[...]
    out_ref[...] = spread_sides(normed, weight)
    gate_ref[...] = gate_of(normed, weight)


def pack_kernel(both_ref, squeeze_ref, left_ref, right_ref):
    cores = [rows_of(both_ref[core]) for core in range(2)]
    first = lax.axis_index("core") == 0
    rows = []
    for channel in range(2):
        rows.extend(whole_matrix(cores, 0, channel))
    for channel in range(2):
        rows.append(jnp.where(first, *whole_matrix(cores, 1, channel)))
    packed = squeezed(rows, squeeze_ref[...])
    left_ref[...] = packed[:192]
    for x in range(4):
        right_ref[x] = packed[192:]


def outgoing_kernel(left_ref, right_ref, stretch_ref, out_ref):
    wide = []
    for channel in range(2):
        product = lax.dot_general(
            left_ref[96 * channel : 96 * channel + 96],
            right_ref[:, 48 * channel : 48 * channel + 48].reshape(192, 384),
            (((1,), (1,)), ((), ())),
            preferred_element_type=F32,
        ).astype(BF16)
        wide.append(jnp.dot(product, stretch_ref[:192, :256], preferred_element_type=F32))
    out_ref[...] = send_back(jnp.concatenate(wide, axis=1))


def middle_kernel(
    arrived_ref, field_ref, gate_ref, out_weight_ref, weight_ref, gain_ref, out_ref, first_ref, next_gate_ref
):
    first = finish(
        arrived_ref[...], field_ref[...], gate_ref[...], out_weight_ref[0], gain_ref[2:3]
    ).astype(BF16)
    normed = normalize(first.astype(F32), gain_ref[1:2], 1).astype(BF16)
    weight = weight_ref[...]
    out_ref[...] = spread_sides(normed, weight)
    first_ref[...] = first
    next_gate_ref[...] = gate_of(normed, weight)


def incoming_kernel(own_ref, both_ref, squeeze_ref, out_ref):
    cores = [rows_of(both_ref[core]) for core in range(2)]
    own = rows_of(own_ref[...])
    none = jnp.zeros((96, 256), F32)
    rows = []
    for channel in range(2):
        rows.extend(whole_matrix(cores, 0, channel))
    for channel in range(2):
        part = jnp.concatenate(matrix(own, 1, channel), axis=0)
        rows.append(jnp.concatenate([none, part] if channel else [part, none], axis=1))
    packed = squeezed(rows, squeeze_ref[...])
    product = lax.dot_general(
        packed[:192], packed[192:], (((0,), (0,)), ((), ())), preferred_element_type=F32
    ).astype(BF16)
    for x in range(4):
        for z1 in range(2):
            at = 192 * z1 + 48 * x
            out_ref[x, 48 * z1 : 48 * z1 + 48] = product[at : at + 48]


def sum_kernel(parts_ref, stretch_ref, out_ref):
    total = parts_ref[0].astype(F32)
    for x in range(1, 4):
        total = total + parts_ref[x].astype(F32)
    out_ref[...] = send_back(jnp.dot(total.astype(BF16), stretch_ref[...], preferred_element_type=F32))


def end_kernel(arrived_ref, field_ref, gate_ref, out_weight_ref, gain_ref, out_ref, scratch):
    final = finish(
        arrived_ref[...], field_ref[...], gate_ref[...], out_weight_ref[1], gain_ref[3:4]
    )
    for n in range(48):
        scratch[6 * n : 6 * n + 8, :] = final[8 * n : 8 * n + 8]
    out_ref[...] = scratch[0:288, :].reshape(6, 48, H).astype(BF16)


def squeeze_matrix():
    places = np.arange(256).reshape(2, 2, 2, 4, 8)[..., :6].transpose(3, 4, 0, 1, 2).reshape(-1)
    block = np.arange(256)[:, None] == places[None, :]
    return np.kron(np.eye(2, dtype=bool), block).astype(jnp.bfloat16)


def call(kernel, outs, scratch=()):
    return pl.pallas_call(
        kernel,
        out_shape=[jax.ShapeDtypeStruct(shape, dtype) for shape, dtype in outs],
        scratch_shapes=list(scratch),
        compiler_params=pltpu.CompilerParams(vmem_limit_bytes=48 * 1024 * 1024),
        cost_estimate=pl.CostEstimate(flops=20_000_000, bytes_accessed=1_000_000, transcendentals=100_000),
    )


def shards(pair_field, proj_weight, out_weight, in_gain, out_gain):
    exchange = functools.partial(lax.all_to_all, split_axis=0, concat_axis=0, tiled=True)
    squeeze, stretch = jnp.asarray(squeeze_matrix()), jnp.asarray(squeeze_matrix().T)
    pairs, gates = ((384, H), BF16), ((384, H), F32)
    sides, results = ((HALF, 3, 4, H), BF16), ((HALF, 3, 2, H), BF16)
    block, blocks = ((192, 384), BF16), ((4, 96, 384), BF16)
    padded = pltpu.VMEM((296, H), F32)

    gains = jnp.concatenate([in_gain, out_gain], axis=0)
    sent, field, gating = call(start_kernel, [sides, pairs, gates], [padded])(
        pair_field, proj_weight[0], gains
    )
    own = exchange(sent, SPREAD)
    both = lax.all_gather(own, "core", axis=0, tiled=False)
    left, right = call(pack_kernel, [block, blocks])(both, squeeze)
    right = exchange(right, "x")
    [back] = call(outgoing_kernel, [results])(left, right, stretch)
    arrived = exchange(back, SPREAD)

    sent, field, gating = call(middle_kernel, [sides, pairs, gates])(
        arrived, field, gating, out_weight, proj_weight[1], gains
    )
    own = exchange(sent, SPREAD)
    both = lax.all_gather(own, "core", axis=0, tiled=False)
    [parts] = call(incoming_kernel, [blocks])(own, both, squeeze)
    parts = exchange(parts, "x")
    [back] = call(sum_kernel, [results])(parts, stretch)
    arrived = exchange(back, SPREAD)
    [out] = call(end_kernel, [((6, 48, H), BF16)], [padded])(
        arrived, field, gating, out_weight, gains
    )
    return out


def solution(mesh):
    fine = Mesh(mesh.devices.reshape(2, 2, 2, 2, 4, 4, 2), ("yh", "z2", "z1", "z0", "x", "yl", "core"))
    row, col = ("yh", "z2", "z1", "z0", "x"), ("yl", "core")
    return jax.shard_map(
        shards,
        mesh=fine,
        in_specs=(P(row, col, None), P(), P(), P(), P()),
        out_specs=P(row, col, None),
        check_vma=False,
    )
```

```python
import functools

import jax
import jax.numpy as jnp
import numpy as np
from jax import lax
from jax.experimental import pallas as pl
from jax.experimental.pallas import tpu as pltpu
from jax.sharding import Mesh
from jax.sharding import PartitionSpec as P

H = 128
HALF = 64
SPREAD = ("yl", "z1", "yh", "z2", "z0")
F32 = jnp.float32
BF16 = jnp.bfloat16


def normalize(values, gain, axis):
    mean = jnp.mean(values, axis=axis, keepdims=True)
    centred = values - mean
    spread = jnp.mean(centred * centred, axis=axis, keepdims=True)
    return centred * lax.rsqrt(spread + 1e-05) * gain


def halves(top, bottom):
    low = lax.broadcasted_iota(jnp.int32, top.shape, 1) < HALF
    return jnp.where(low, top, pltpu.roll(bottom, HALF, 1)), jnp.where(low, pltpu.roll(top, HALF, 1), bottom)


def by_device(rows):
    return jnp.swapaxes(jnp.stack(rows, axis=0), 0, 1)


def widen_groups(values, scratch):
    scratch[0:288, :] = values
    keep = lax.broadcasted_iota(jnp.int32, (8, H), 0) < 6
    return jnp.concatenate(
        [jnp.where(keep, scratch[6 * n : 6 * n + 8, :], 0.0) for n in range(48)], axis=0
    )


def spread_sides(normed, weight):
    projected = lax.dot_general(
        weight[:, : 4 * H], normed, (((0,), (1,)), ((), ())), preferred_element_type=F32
    )
    rows = []
    for side in range(2):
        value = projected[2 * side * H : (2 * side + 1) * H]
        gate = projected[(2 * side + 1) * H : (2 * side + 2) * H]
        turned = jax.nn.sigmoid(gate) * value
        for channel in range(2):
            part = turned[channel * HALF : (channel + 1) * HALF]
            rows.extend(part[:, t * H : (t + 1) * H] for t in range(3))
    return by_device(rows).reshape(HALF, 3, 4, H).astype(BF16)


def gate_of(normed, weight):
    return jax.nn.sigmoid(jnp.dot(normed, weight[:, 4 * H :], preferred_element_type=F32))


def summed_rows(arrived):
    by_row = jnp.swapaxes(arrived.astype(F32).reshape(HALF, 6, H), 0, 1)
    return [jnp.concatenate([by_row[t], by_row[3 + t]], axis=0) for t in range(3)]


def finish(summed, field, gating, weight, gain):
    column = jnp.swapaxes(jnp.broadcast_to(gain, (8, H)), 0, 1)[:, :1]
    mixed = normalize(summed, column, 0).astype(BF16)
    update = lax.dot_general(
        mixed, weight, (((0,), (0,)), ((), ())), preferred_element_type=F32
    )
    return field.astype(F32) + gating * update


def rows_of(own):
    return jnp.swapaxes(own.astype(F32).reshape(HALF, 12, H), 0, 1)


def matrix(by_row, side, channel):
    found = ([], [])
    for t in range(3):
        part = by_row[6 * side + 3 * channel + t]
        tiles = [halves(part[32 * u : 32 * u + 16], part[32 * u + 16 : 32 * u + 32]) for u in range(2)]
        for e in range(2):
            both = jnp.concatenate([tile[e] for tile in tiles], axis=1)
            for z1 in range(2):
                found[z1].append(both[8 * z1 : 8 * z1 + 8])
    return [jnp.concatenate(pieces, axis=0) for pieces in found]


def whole_matrix(cores, side, channel):
    parts = [matrix(by_row, side, channel) for by_row in cores]
    return [jnp.concatenate([parts[0][z1], parts[1][z1]], axis=1) for z1 in range(2)]


def squeezed(rows, squeeze):
    return jnp.dot(
        jnp.concatenate(rows, axis=0).astype(BF16), squeeze, preferred_element_type=F32
    ).astype(BF16)


def send_back(product, stretch):
    wide = jnp.dot(product.astype(BF16), stretch, preferred_element_type=F32)
    rows = []
    for channel in range(2):
        for t in range(3):
            parts = []
            for u in range(2):
                lanes = slice((2 * channel + u) * H, (2 * channel + u + 1) * H)
                pair = [
                    jnp.concatenate([wide[8 * a : 8 * a + 8, lanes], wide[48 + 8 * a : 56 + 8 * a, lanes]], axis=0)
                    for a in (2 * t, 2 * t + 1)
                ]
                parts.extend(halves(*pair))
            rows.append(jnp.concatenate(parts, axis=0))
    return by_device(rows).reshape(HALF, 3, 2, H).astype(BF16)


def start_kernel(pair_ref, weight_ref, gain_ref, out_ref, field_ref, gate_ref, scratch):
    field = widen_groups(pair_ref[...].reshape(288, H).astype(F32), scratch)
    field_ref[...] = field.astype(BF16)
    normed = normalize(field, gain_ref[0:1], 1).astype(BF16)
    weight = weight_ref[...]
    out_ref[...] = spread_sides(normed, weight)
    gate_ref[...] = gate_of(normed, weight)


def pack_kernel(both_ref, squeeze_ref, left_ref, right_ref):
    cores = [rows_of(both_ref[core]) for core in range(2)]
    first = lax.axis_index("core") == 0
    rows = []
    for channel in range(2):
        rows.extend(whole_matrix(cores, 0, channel))
    for channel in range(2):
        rows.append(jnp.where(first, *whole_matrix(cores, 1, channel)))
    packed = squeezed(rows, squeeze_ref[...])
    left_ref[...] = packed[:192]
    for x in range(4):
        right_ref[x] = packed[192:]


def outgoing_kernel(left_ref, right_ref, stretch_ref, out_ref):
    left = jnp.concatenate([left_ref[:96], left_ref[96:]], axis=1)
    none = jnp.zeros((192, 384), BF16)
    right = [right_ref[:, 48 * channel : 48 * channel + 48].reshape(192, 384) for channel in range(2)]
    right = jnp.concatenate(
        [jnp.concatenate([right[0], none], axis=1), jnp.concatenate([none, right[1]], axis=1)], axis=0
    )
    product = lax.dot_general(left, right, (((1,), (1,)), ((), ())), preferred_element_type=F32)
    out_ref[...] = send_back(product, stretch_ref[...])


def middle_kernel(
    arrived_ref, field_ref, gate_ref, out_weight_ref, weight_ref, gain_ref, out_ref, first_ref, next_gate_ref
):
    first = finish(
        jnp.concatenate(summed_rows(arrived_ref[...]), axis=1), field_ref[...], gate_ref[...], out_weight_ref[0], gain_ref[2:3]
    ).astype(BF16)
    normed = normalize(first.astype(F32), gain_ref[1:2], 1).astype(BF16)
    weight = weight_ref[1]
    out_ref[...] = spread_sides(normed, weight)
    first_ref[...] = first
    next_gate_ref[...] = gate_of(normed, weight)


def incoming_kernel(own_ref, both_ref, squeeze_ref, out_ref):
    cores = [rows_of(both_ref[core]) for core in range(2)]
    own = rows_of(own_ref[...])
    none = jnp.zeros((96, 256), F32)
    rows = []
    for channel in range(2):
        rows.extend(whole_matrix(cores, 0, channel))
    for channel in range(2):
        part = jnp.concatenate(matrix(own, 1, channel), axis=0)
        rows.append(jnp.concatenate([none, part] if channel else [part, none], axis=1))
    packed = squeezed(rows, squeeze_ref[...])
    product = lax.dot_general(
        packed[:192], packed[192:], (((0,), (0,)), ((), ())), preferred_element_type=F32
    ).astype(BF16)
    for x in range(4):
        for z1 in range(2):
            at = 192 * z1 + 48 * x
            out_ref[x, 48 * z1 : 48 * z1 + 48] = product[at : at + 48]


def sum_kernel(parts_ref, stretch_ref, out_ref):
    total = parts_ref[0].astype(F32)
    for x in range(1, 4):
        total = total + parts_ref[x].astype(F32)
    out_ref[...] = send_back(total, stretch_ref[...])


def end_kernel(arrived_ref, field_ref, gate_ref, out_weight_ref, gain_ref, out_hbm, scratch, stage, sems):
    copies = []
    for t, summed in enumerate(summed_rows(arrived_ref[...])):
        pairs = slice(H * t, H * t + H)
        final = finish(summed, field_ref[pairs], gate_ref[pairs], out_weight_ref[1], gain_ref[3:4])
        for n in range(16):
            scratch[t, 6 * n : 6 * n + 8, :] = final[8 * n : 8 * n + 8]
        stage[2 * t : 2 * t + 2] = scratch[t, :96].reshape(2, 48, H).astype(BF16)
        copies.append(
            pltpu.make_async_copy(stage.at[2 * t : 2 * t + 2], out_hbm.at[2 * t : 2 * t + 2], sems.at[t])
        )
        copies[t].start()
    for copy in copies:
        copy.wait()


def squeeze_matrix():
    places = np.arange(256).reshape(2, 2, 2, 4, 8)[..., :6].transpose(3, 4, 0, 1, 2).reshape(-1)
    block = np.arange(256)[:, None] == places[None, :]
    return np.kron(np.eye(2, dtype=bool), block).astype(jnp.bfloat16)


def call(kernel, outs, scratch=(), **specs):
    return pl.pallas_call(
        kernel,
        out_shape=[jax.ShapeDtypeStruct(shape, dtype) for shape, dtype in outs],
        scratch_shapes=list(scratch),
        compiler_params=pltpu.CompilerParams(vmem_limit_bytes=48 * 1024 * 1024),
        cost_estimate=pl.CostEstimate(flops=20_000_000, bytes_accessed=1_000_000, transcendentals=100_000),
        **specs,
    )


def shards(pair_field, proj_weight, out_weight, in_gain, out_gain):
    exchange = functools.partial(lax.all_to_all, split_axis=0, concat_axis=0, tiled=True)
    squeeze, stretch = jnp.asarray(squeeze_matrix()), jnp.asarray(squeeze_matrix().T)
    pairs, gates = ((384, H), BF16), ((384, H), F32)
    sides, results = ((HALF, 3, 4, H), BF16), ((HALF, 3, 2, H), BF16)
    block, blocks = ((192, 384), BF16), ((4, 96, 384), BF16)
    padded = pltpu.VMEM((296, H), F32)

    gains = jnp.concatenate([in_gain, out_gain], axis=0)
    sent, field, gating = call(start_kernel, [sides, pairs, gates], [padded])(
        pair_field, proj_weight[0], gains
    )
    own = exchange(sent, SPREAD)
    both = lax.all_gather(own, "core", axis=0, tiled=False)
    left, right = call(pack_kernel, [block, blocks])(both, squeeze)
    right = exchange(right, "x")
    [back] = call(outgoing_kernel, [results])(left, right, stretch)
    arrived = exchange(back, SPREAD)

    sent, field, gating = call(middle_kernel, [sides, pairs, gates])(
        arrived, field, gating, out_weight, proj_weight, gains
    )
    own = exchange(sent, SPREAD)
    both = lax.all_gather(own, "core", axis=0, tiled=False)
    [parts] = call(incoming_kernel, [blocks])(own, both, squeeze)
    parts = exchange(parts, "x")
    [back] = call(sum_kernel, [results])(parts, stretch)
    arrived = exchange(back, SPREAD)
    [out] = call(
        end_kernel,
        [((6, 48, H), BF16)],
        [pltpu.VMEM((3, 104, H), F32), pltpu.VMEM((6, 48, H), BF16), pltpu.SemaphoreType.DMA((3,))],
        out_specs=[pl.BlockSpec(memory_space=pl.ANY)],
    )(arrived, field, gating, out_weight, gains)
    return out


def solution(mesh):
    fine = Mesh(mesh.devices.reshape(2, 2, 2, 2, 4, 4, 2), ("yh", "z2", "z1", "z0", "x", "yl", "core"))
    row, col = ("yh", "z2", "z1", "z0", "x"), ("yl", "core")
    return jax.shard_map(
        shards,
        mesh=fine,
        in_specs=(P(row, col, None), P(), P(), P(), P()),
        out_specs=P(row, col, None),
        check_vma=False,
    )
```

```python
import functools

import jax
import jax.numpy as jnp
import numpy as np
from jax import lax
from jax.experimental import pallas as pl
from jax.experimental.pallas import tpu as pltpu
from jax.sharding import Mesh
from jax.sharding import PartitionSpec as P

H = 128
HALF = 64
SPREAD = ("yl", "z1", "yh", "z2", "z0")
F32 = jnp.float32
BF16 = jnp.bfloat16


def normalize(values, gain, axis):
    mean = jnp.mean(values, axis=axis, keepdims=True)
    centred = values - mean
    spread = jnp.mean(centred * centred, axis=axis, keepdims=True)
    return centred * lax.rsqrt(spread + 1e-05) * gain


def halves(top, bottom):
    low = lax.broadcasted_iota(jnp.int32, top.shape, 1) < HALF
    return jnp.where(low, top, pltpu.roll(bottom, HALF, 1)), jnp.where(low, pltpu.roll(top, HALF, 1), bottom)


def by_device(rows):
    return jnp.swapaxes(jnp.stack(rows, axis=0), 0, 1)


def spread_sides(normed, weight):
    projected = lax.dot_general(
        weight[:, : 4 * H], normed, (((0,), (1,)), ((), ())), preferred_element_type=F32
    )
    rows, ends = [], []
    for side in range(2):
        value = projected[2 * side * H : (2 * side + 1) * H]
        gate = projected[(2 * side + 1) * H : (2 * side + 2) * H]
        turned = jax.nn.sigmoid(gate) * value
        for channel in range(2):
            part = turned[channel * HALF : (channel + 1) * HALF]
            rows.extend([part[:, :H], part[:, H : 2 * H]])
            ends.append(part[:, 2 * H :])
    rows.extend([jnp.concatenate(ends, axis=1), jnp.zeros((HALF, H), F32)])
    return by_device(rows).reshape(HALF, 5, 2, H).astype(BF16)


def gate_of(normed, weight):
    return jax.nn.sigmoid(jnp.dot(normed, weight[:, 4 * H :], preferred_element_type=F32))


def summed_rows(arrived):
    by_row = jnp.swapaxes(arrived.astype(F32).reshape(HALF, 6, H), 0, 1)
    return jnp.concatenate([jnp.concatenate([by_row[t], by_row[3 + t]], axis=0) for t in range(3)], axis=1)


def finish(summed, field, gating, weight, gain):
    column = jnp.swapaxes(jnp.broadcast_to(gain, (8, H)), 0, 1)[:, :1]
    mixed = normalize(summed, column, 0).astype(BF16)
    update = lax.dot_general(
        mixed, weight, (((0,), (0,)), ((), ())), preferred_element_type=F32
    )
    update = jnp.concatenate([update[HALF * a : HALF * a + 48] for a in range(6)], axis=0)
    return field.astype(F32) + gating * update


def rows_of(own):
    return jnp.swapaxes(own.astype(F32).reshape(HALF, 10, H), 0, 1)


def moved(tile, lanes):
    return pltpu.roll(tile, lanes % H, 1) if lanes % H else tile


def matrix(by_row, side, channel):
    q = 2 * side + channel
    lane = lax.broadcasted_iota(jnp.int32, (16, H), 1)
    cut = lax.broadcasted_iota(jnp.int32, (HALF, H), 1) >= 96
    first, second, last = by_row[2 * q], by_row[2 * q + 1], by_row[8]
    across = jnp.where(cut, first, second)
    begins = ((first, 0), (first, 48), (across, 96), (second, 16), (second, 64), (second, 112))
    found = ([], [])
    for a in range(6):
        row, begin = begins[a]
        tiles = []
        for u in range(2):
            pair = []
            for e in range(2):
                at = slice(32 * u + 16 * e, 32 * u + 16 * e + 16)
                piece = moved(row[at], HALF * e - begin)
                if a == 5:
                    piece = jnp.where(lane < HALF * e + 16, piece, moved(last[at], HALF * e + 16 - 32 * q))
                pair.append(piece)
            tiles.append(jnp.where(lane < HALF, *pair))
        both = jnp.concatenate(tiles, axis=1)
        for half in range(2):
            found[half].append(both[8 * half : 8 * half + 8])
    return [jnp.concatenate(pieces, axis=0) for pieces in found]


def whole_matrix(cores, side, channel):
    parts = [matrix(by_row, side, channel) for by_row in cores]
    return [jnp.concatenate([parts[0][z1], parts[1][z1]], axis=1) for z1 in range(2)]


def squeezed(rows, squeeze):
    return jnp.dot(
        jnp.concatenate(rows, axis=0).astype(BF16), squeeze, preferred_element_type=F32
    ).astype(BF16)


def send_back(product, stretch):
    wide = jnp.dot(product.astype(BF16), stretch, preferred_element_type=F32)
    rows = []
    for channel in range(2):
        for t in range(3):
            parts = []
            for u in range(2):
                lanes = slice((2 * channel + u) * H, (2 * channel + u + 1) * H)
                pair = [
                    jnp.concatenate([wide[8 * a : 8 * a + 8, lanes], wide[48 + 8 * a : 56 + 8 * a, lanes]], axis=0)
                    for a in (2 * t, 2 * t + 1)
                ]
                parts.extend(halves(*pair))
            rows.append(jnp.concatenate(parts, axis=0))
    return by_device(rows).reshape(HALF, 3, 2, H).astype(BF16)


def start_kernel(pair_ref, weight_ref, gain_ref, out_ref, gate_ref):
    field = pair_ref[...].reshape(288, H).astype(F32)
    normed = normalize(field, gain_ref[0:1], 1).astype(BF16)
    weight = weight_ref[...]
    out_ref[...] = spread_sides(normed, weight)
    gate_ref[...] = gate_of(normed, weight)


def pack_kernel(both_ref, squeeze_ref, left_ref, right_ref):
    cores = [rows_of(both_ref[core]) for core in range(2)]
    first = lax.axis_index("core") == 0
    rows = []
    for channel in range(2):
        rows.extend(whole_matrix(cores, 0, channel))
    for channel in range(2):
        rows.append(jnp.where(first, *whole_matrix(cores, 1, channel)))
    packed = squeezed(rows, squeeze_ref[...])
    left_ref[...] = packed[:192]
    for x in range(4):
        right_ref[x] = packed[192:]


def outgoing_kernel(left_ref, right_ref, stretch_ref, out_ref):
    left = jnp.concatenate([left_ref[:96], left_ref[96:]], axis=1)
    none = jnp.zeros((192, 384), BF16)
    right = [right_ref[:, 48 * channel : 48 * channel + 48].reshape(192, 384) for channel in range(2)]
    right = jnp.concatenate(
        [jnp.concatenate([right[0], none], axis=1), jnp.concatenate([none, right[1]], axis=1)], axis=0
    )
    product = lax.dot_general(left, right, (((1,), (1,)), ((), ())), preferred_element_type=F32)
    out_ref[...] = send_back(product, stretch_ref[...])


def middle_kernel(
    arrived_ref, field_ref, gate_ref, out_weight_ref, weight_ref, gain_ref, out_ref, first_ref, next_gate_ref
):
    first = finish(
        summed_rows(arrived_ref[...]), field_ref[...].reshape(288, H), gate_ref[...], out_weight_ref[0], gain_ref[2:3]
    ).astype(BF16)
    normed = normalize(first.astype(F32), gain_ref[1:2], 1).astype(BF16)
    weight = weight_ref[1]
    out_ref[...] = spread_sides(normed, weight)
    first_ref[...] = first.reshape(6, 48, H)
    next_gate_ref[...] = gate_of(normed, weight)


def incoming_kernel(own_ref, both_ref, squeeze_ref, out_ref):
    cores = [rows_of(both_ref[core]) for core in range(2)]
    own = rows_of(own_ref[...])
    none = jnp.zeros((96, 256), F32)
    rows = []
    for channel in range(2):
        rows.extend(whole_matrix(cores, 0, channel))
    for channel in range(2):
        part = jnp.concatenate(matrix(own, 1, channel), axis=0)
        rows.append(jnp.concatenate([none, part] if channel else [part, none], axis=1))
    packed = squeezed(rows, squeeze_ref[...])
    product = lax.dot_general(
        packed[:192], packed[192:], (((0,), (0,)), ((), ())), preferred_element_type=F32
    ).astype(BF16)
    for x in range(4):
        for z1 in range(2):
            at = 192 * z1 + 48 * x
            out_ref[x, 48 * z1 : 48 * z1 + 48] = product[at : at + 48]


def sum_kernel(parts_ref, stretch_ref, out_ref):
    total = parts_ref[0].astype(F32)
    for x in range(1, 4):
        total = total + parts_ref[x].astype(F32)
    out_ref[...] = send_back(total, stretch_ref[...])


def end_kernel(arrived_ref, field_ref, gate_ref, out_weight_ref, gain_ref, out_ref):
    final = finish(
        summed_rows(arrived_ref[...]), field_ref[...].reshape(288, H), gate_ref[...], out_weight_ref[1], gain_ref[3:4]
    )
    out_ref[...] = final.reshape(6, 48, H).astype(BF16)


def squeeze_matrix():
    places = np.pad(np.ones((4, 48), bool), ((0, 0), (0, 16))).reshape(-1).nonzero()[0]
    places = places.reshape(2, 2, 2, 4, 6).transpose(3, 4, 0, 1, 2).reshape(-1)
    block = np.arange(256)[:, None] == places[None, :]
    return np.kron(np.eye(2, dtype=bool), block).astype(jnp.bfloat16)


def call(kernel, outs, scratch=(), **specs):
    return pl.pallas_call(
        kernel,
        out_shape=[jax.ShapeDtypeStruct(shape, dtype) for shape, dtype in outs],
        scratch_shapes=list(scratch),
        compiler_params=pltpu.CompilerParams(vmem_limit_bytes=48 * 1024 * 1024),
        cost_estimate=pl.CostEstimate(flops=20_000_000, bytes_accessed=1_000_000, transcendentals=100_000),
        **specs,
    )


def shards(pair_field, proj_weight, out_weight, in_gain, out_gain):
    exchange = functools.partial(lax.all_to_all, split_axis=0, concat_axis=0, tiled=True)
    squeeze, stretch = jnp.asarray(squeeze_matrix()), jnp.asarray(squeeze_matrix().T)
    pairs, gates = ((6, 48, H), BF16), ((288, H), F32)
    sides, results = ((HALF, 5, 2, H), BF16), ((HALF, 3, 2, H), BF16)
    block, blocks = ((192, 384), BF16), ((4, 96, 384), BF16)

    gains = jnp.concatenate([in_gain, out_gain], axis=0)
    sent, gating = call(start_kernel, [sides, gates])(pair_field, proj_weight[0], gains)
    own = exchange(sent, SPREAD)
    both = lax.all_gather(own, "core", axis=0, tiled=False)
    left, right = call(pack_kernel, [block, blocks])(both, squeeze)
    right = exchange(right, "x")
    [back] = call(outgoing_kernel, [results])(left, right, stretch)
    arrived = exchange(back, SPREAD)

    sent, first_pair, gating = call(middle_kernel, [sides, pairs, gates])(
        arrived, pair_field, gating, out_weight, proj_weight, gains
    )
    own = exchange(sent, SPREAD)
    both = lax.all_gather(own, "core", axis=0, tiled=False)
    [parts] = call(incoming_kernel, [blocks])(own, both, squeeze)
    parts = exchange(parts, "x")
    [back] = call(sum_kernel, [results])(parts, stretch)
    arrived = exchange(back, SPREAD)
    [out] = call(end_kernel, [pairs])(arrived, first_pair, gating, out_weight, gains)
    return out


def solution(mesh):
    fine = Mesh(mesh.devices.reshape(2, 2, 2, 2, 4, 4, 2), ("yh", "z2", "z1", "z0", "x", "yl", "core"))
    row, col = ("yh", "z2", "z1", "z0", "x"), ("yl", "core")
    return jax.shard_map(
        shards,
        mesh=fine,
        in_specs=(P(row, col, None), P(), P(), P(), P()),
        out_specs=P(row, col, None),
        check_vma=False,
    )
```

```python
import functools

import jax
import jax.numpy as jnp
import numpy as np
from jax import lax
from jax.experimental import pallas as pl
from jax.experimental.pallas import tpu as pltpu
from jax.sharding import Mesh
from jax.sharding import PartitionSpec as P

H = 128
HALF = 64
SPREAD = ("yl", "z1", "yh", "z2", "z0")
F32 = jnp.float32
BF16 = jnp.bfloat16


def normalize(values, gain, axis):
    mean = jnp.mean(values, axis=axis, keepdims=True)
    centred = values - mean
    spread = jnp.mean(centred * centred, axis=axis, keepdims=True)
    return centred * lax.rsqrt(spread + 1e-05) * gain


def halves(top, bottom):
    low = lax.broadcasted_iota(jnp.int32, top.shape, 1) < HALF
    return jnp.where(low, top, pltpu.roll(bottom, HALF, 1)), jnp.where(low, pltpu.roll(top, HALF, 1), bottom)


def by_device(rows):
    return jnp.swapaxes(jnp.stack(rows, axis=0), 0, 1)


def spread_sides(normed, weight):
    projected = lax.dot_general(
        weight[:, : 4 * H], normed, (((0,), (1,)), ((), ())), preferred_element_type=F32
    )
    rows, ends = [], []
    for side in range(2):
        value = projected[2 * side * H : (2 * side + 1) * H]
        gate = projected[(2 * side + 1) * H : (2 * side + 2) * H]
        turned = jax.nn.sigmoid(gate) * value
        for channel in range(2):
            part = turned[channel * HALF : (channel + 1) * HALF]
            rows.extend([part[:, :H], part[:, H : 2 * H]])
            ends.append(part[:, 2 * H :])
    rows.extend([jnp.concatenate(ends, axis=1), jnp.zeros((HALF, H), F32)])
    return by_device(rows).reshape(HALF, 5, 2, H).astype(BF16)


def gate_of(normed, weight):
    return jax.nn.sigmoid(jnp.dot(normed, weight[:, 4 * H :], preferred_element_type=F32))


def summed_rows(arrived):
    by_row = jnp.swapaxes(arrived.astype(F32).reshape(HALF, 6, H), 0, 1)
    return jnp.concatenate([jnp.concatenate([by_row[t], by_row[3 + t]], axis=0) for t in range(3)], axis=1)


def finish(summed, field, gating, weight, gain):
    column = jnp.swapaxes(jnp.broadcast_to(gain, (8, H)), 0, 1)[:, :1]
    mixed = normalize(summed, column, 0).astype(BF16)
    update = lax.dot_general(
        mixed, weight, (((0,), (0,)), ((), ())), preferred_element_type=F32
    )
    update = jnp.concatenate([update[HALF * a : HALF * a + 48] for a in range(6)], axis=0)
    return field.astype(F32) + gating * update


def rows_of(own):
    return jnp.swapaxes(own.astype(F32).reshape(HALF, 10, H), 0, 1)


def moved(tile, lanes):
    return pltpu.roll(tile, lanes % H, 1) if lanes % H else tile


def matrix(by_row, side, channel):
    q = 2 * side + channel
    lane = lax.broadcasted_iota(jnp.int32, (16, H), 1)
    cut = lax.broadcasted_iota(jnp.int32, (HALF, H), 1) >= 96
    first, second, last = by_row[2 * q], by_row[2 * q + 1], by_row[8]
    across = jnp.where(cut, first, second)
    begins = ((first, 0), (first, 48), (across, 96), (second, 16), (second, 64), (second, 112))
    found = ([], [])
    for a in range(6):
        row, begin = begins[a]
        tiles = []
        for u in range(2):
            pair = []
            for e in range(2):
                at = slice(32 * u + 16 * e, 32 * u + 16 * e + 16)
                piece = moved(row[at], HALF * e - begin)
                if a == 5:
                    piece = jnp.where(lane < HALF * e + 16, piece, moved(last[at], HALF * e + 16 - 32 * q))
                pair.append(piece)
            tiles.append(jnp.where(lane < HALF, *pair))
        both = jnp.concatenate(tiles, axis=1)
        for half in range(2):
            found[half].append(both[8 * half : 8 * half + 8])
    return [jnp.concatenate(pieces, axis=0) for pieces in found]


def whole_matrix(cores, side, channel):
    parts = [matrix(by_row, side, channel) for by_row in cores]
    return [jnp.concatenate([parts[0][z1], parts[1][z1]], axis=1) for z1 in range(2)]


def squeezed(rows, squeeze):
    return jnp.dot(
        jnp.concatenate(rows, axis=0).astype(BF16), squeeze, preferred_element_type=F32
    ).astype(BF16)


def send_back(product, stretch):
    wide = jnp.dot(product.astype(BF16), stretch, preferred_element_type=F32)
    rows = []
    for channel in range(2):
        for t in range(3):
            parts = []
            for u in range(2):
                lanes = slice((2 * channel + u) * H, (2 * channel + u + 1) * H)
                pair = [
                    jnp.concatenate([wide[8 * a : 8 * a + 8, lanes], wide[48 + 8 * a : 56 + 8 * a, lanes]], axis=0)
                    for a in (2 * t, 2 * t + 1)
                ]
                parts.extend(halves(*pair))
            rows.append(jnp.concatenate(parts, axis=0))
    return by_device(rows).reshape(HALF, 3, 2, H).astype(BF16)


def start_kernel(
    pair_hbm, weight_hbm, in_gain_hbm, out_gain_hbm,
    out_ref, gate_ref, gain_ref,
    pair_ref, weight_ref, in_gain_ref, out_gain_ref, sems,
):
    moves = [
        (pair_hbm, pair_ref),
        (in_gain_hbm, in_gain_ref),
        (weight_hbm.at[0], weight_ref),
        (out_gain_hbm, out_gain_ref),
    ]
    copies = [pltpu.make_async_copy(source, target, sems.at[n]) for n, (source, target) in enumerate(moves)]
    for copy in copies:
        copy.start()
    copies[0].wait()
    copies[1].wait()
    field = pair_ref[...].reshape(288, H).astype(F32)
    normed = normalize(field, in_gain_ref[0:1], 1).astype(BF16)
    copies[2].wait()
    weight = weight_ref[...]
    out_ref[...] = spread_sides(normed, weight)
    gate_ref[...] = gate_of(normed, weight)
    copies[3].wait()
    gain_ref[0:2] = in_gain_ref[...]
    gain_ref[2:4] = out_gain_ref[...]


def pack_kernel(both_ref, squeeze_ref, left_ref, right_ref):
    cores = [rows_of(both_ref[core]) for core in range(2)]
    first = lax.axis_index("core") == 0
    rows = []
    for channel in range(2):
        rows.extend(whole_matrix(cores, 0, channel))
    for channel in range(2):
        rows.append(jnp.where(first, *whole_matrix(cores, 1, channel)))
    packed = squeezed(rows, squeeze_ref[...])
    left_ref[...] = packed[:192]
    for x in range(4):
        right_ref[x] = packed[192:]


def outgoing_kernel(left_ref, right_ref, stretch_ref, out_ref):
    left = jnp.concatenate([left_ref[:96], left_ref[96:]], axis=1)
    none = jnp.zeros((192, 384), BF16)
    right = [right_ref[:, 48 * channel : 48 * channel + 48].reshape(192, 384) for channel in range(2)]
    right = jnp.concatenate(
        [jnp.concatenate([right[0], none], axis=1), jnp.concatenate([none, right[1]], axis=1)], axis=0
    )
    product = lax.dot_general(left, right, (((1,), (1,)), ((), ())), preferred_element_type=F32)
    out_ref[...] = send_back(product, stretch_ref[...])


def middle_kernel(
    arrived_ref, field_ref, gate_ref, out_weight_ref, weight_ref, gain_ref, out_ref, first_ref, next_gate_ref
):
    first = finish(
        summed_rows(arrived_ref[...]), field_ref[...].reshape(288, H), gate_ref[...], out_weight_ref[0], gain_ref[2:3]
    ).astype(BF16)
    normed = normalize(first.astype(F32), gain_ref[1:2], 1).astype(BF16)
    weight = weight_ref[1]
    out_ref[...] = spread_sides(normed, weight)
    first_ref[...] = first.reshape(6, 48, H)
    next_gate_ref[...] = gate_of(normed, weight)


def incoming_kernel(own_ref, both_ref, squeeze_ref, out_ref):
    cores = [rows_of(both_ref[core]) for core in range(2)]
    own = rows_of(own_ref[...])
    none = jnp.zeros((96, 256), F32)
    rows = []
    for channel in range(2):
        rows.extend(whole_matrix(cores, 0, channel))
    for channel in range(2):
        part = jnp.concatenate(matrix(own, 1, channel), axis=0)
        rows.append(jnp.concatenate([none, part] if channel else [part, none], axis=1))
    packed = squeezed(rows, squeeze_ref[...])
    product = lax.dot_general(
        packed[:192], packed[192:], (((0,), (0,)), ((), ())), preferred_element_type=F32
    ).astype(BF16)
    for x in range(4):
        for z1 in range(2):
            at = 192 * z1 + 48 * x
            out_ref[x, 48 * z1 : 48 * z1 + 48] = product[at : at + 48]


def sum_kernel(parts_ref, stretch_ref, out_ref):
    total = parts_ref[0].astype(F32)
    for x in range(1, 4):
        total = total + parts_ref[x].astype(F32)
    out_ref[...] = send_back(total, stretch_ref[...])


def end_kernel(arrived_ref, field_ref, gate_ref, out_weight_ref, gain_ref, out_ref):
    final = finish(
        summed_rows(arrived_ref[...]), field_ref[...].reshape(288, H), gate_ref[...], out_weight_ref[1], gain_ref[3:4]
    )
    out_ref[...] = final.reshape(6, 48, H).astype(BF16)


def squeeze_matrix():
    places = np.pad(np.ones((4, 48), bool), ((0, 0), (0, 16))).reshape(-1).nonzero()[0]
    places = places.reshape(2, 2, 2, 4, 6).transpose(3, 4, 0, 1, 2).reshape(-1)
    block = np.arange(256)[:, None] == places[None, :]
    return np.kron(np.eye(2, dtype=bool), block).astype(jnp.bfloat16)


def call(kernel, outs, scratch=(), **specs):
    return pl.pallas_call(
        kernel,
        out_shape=[jax.ShapeDtypeStruct(shape, dtype) for shape, dtype in outs],
        scratch_shapes=list(scratch),
        compiler_params=pltpu.CompilerParams(vmem_limit_bytes=48 * 1024 * 1024),
        cost_estimate=pl.CostEstimate(flops=20_000_000, bytes_accessed=1_000_000, transcendentals=100_000),
        **specs,
    )


def shards(pair_field, proj_weight, out_weight, in_gain, out_gain):
    exchange = functools.partial(lax.all_to_all, split_axis=0, concat_axis=0, tiled=True)
    squeeze, stretch = jnp.asarray(squeeze_matrix()), jnp.asarray(squeeze_matrix().T)
    pairs, gates = ((6, 48, H), BF16), ((288, H), F32)
    sides, results = ((HALF, 5, 2, H), BF16), ((HALF, 3, 2, H), BF16)
    block, blocks = ((192, 384), BF16), ((4, 96, 384), BF16)

    held = [
        pltpu.with_memory_space_constraint(array, pltpu.HBM)
        for array in (pair_field, proj_weight, in_gain, out_gain)
    ]
    sent, gating, gains = call(
        start_kernel,
        [sides, gates, ((4, H), F32)],
        [
            pltpu.VMEM((6, 48, H), BF16),
            pltpu.VMEM((H, 5 * H), BF16),
            pltpu.VMEM((2, H), F32),
            pltpu.VMEM((2, H), F32),
            pltpu.SemaphoreType.DMA((4,)),
        ],
        in_specs=[pl.BlockSpec(memory_space=pltpu.HBM)] * 4,
    )(*held)
    own = exchange(sent, SPREAD)
    both = lax.all_gather(own, "core", axis=0, tiled=False)
    left, right = call(pack_kernel, [block, blocks])(both, squeeze)
    right = exchange(right, "x")
    [back] = call(outgoing_kernel, [results])(left, right, stretch)
    arrived = exchange(back, SPREAD)

    sent, first_pair, gating = call(middle_kernel, [sides, pairs, gates])(
        arrived, pair_field, gating, out_weight, proj_weight, gains
    )
    own = exchange(sent, SPREAD)
    both = lax.all_gather(own, "core", axis=0, tiled=False)
    [parts] = call(incoming_kernel, [blocks])(own, both, squeeze)
    parts = exchange(parts, "x")
    [back] = call(sum_kernel, [results])(parts, stretch)
    arrived = exchange(back, SPREAD)
    [out] = call(end_kernel, [pairs])(arrived, first_pair, gating, out_weight, gains)
    return out


def solution(mesh):
    fine = Mesh(mesh.devices.reshape(2, 2, 2, 2, 4, 4, 2), ("yh", "z2", "z1", "z0", "x", "yl", "core"))
    row, col = ("yh", "z2", "z1", "z0", "x"), ("yl", "core")
    return jax.shard_map(
        shards,
        mesh=fine,
        in_specs=(P(row, col, None), P(), P(), P(), P()),
        out_specs=P(row, col, None),
        check_vma=False,
    )
```

```python
import functools

import jax
import jax.numpy as jnp
import numpy as np
from jax import lax
from jax.experimental import pallas as pl
from jax.experimental.pallas import tpu as pltpu
from jax.sharding import Mesh
from jax.sharding import PartitionSpec as P

H = 128
HALF = 64
SPREAD = ("yl", "z1", "yh", "z2", "z0")
F32 = jnp.float32
BF16 = jnp.bfloat16


def normalize(values, gain, axis):
    mean = jnp.mean(values, axis=axis, keepdims=True)
    centred = values - mean
    spread = jnp.mean(centred * centred, axis=axis, keepdims=True)
    return centred * lax.rsqrt(spread + 1e-05) * gain


def halves(top, bottom):
    low = lax.broadcasted_iota(jnp.int32, top.shape, 1) < HALF
    return jnp.where(low, top, pltpu.roll(bottom, HALF, 1)), jnp.where(low, pltpu.roll(top, HALF, 1), bottom)


def by_device(rows):
    return jnp.swapaxes(jnp.stack(rows, axis=0), 0, 1)


def spread_sides(normed, weight):
    rows = []
    for core in range(2):
        projected = lax.dot_general(
            weight[:, : 4 * H],
            normed[288 * core : 288 * core + 288],
            (((0,), (1,)), ((), ())),
            preferred_element_type=F32,
        )
        ends = []
        for side in range(2):
            value = projected[2 * side * H : (2 * side + 1) * H]
            gate = projected[(2 * side + 1) * H : (2 * side + 2) * H]
            turned = jax.nn.sigmoid(gate) * value
            for channel in range(2):
                part = turned[channel * HALF : (channel + 1) * HALF]
                rows.extend([part[:, :H], part[:, H : 2 * H]])
                ends.append(part[:, 2 * H :])
        rows.append(jnp.concatenate(ends, axis=1))
    return by_device(rows).reshape(HALF, 9, 2, H).astype(BF16)


def gate_of(normed, weight):
    return jax.nn.sigmoid(jnp.dot(normed, weight[:, 4 * H :], preferred_element_type=F32))


def summed_rows(arrived):
    by_row = jnp.swapaxes(arrived.astype(F32).reshape(HALF, 12, H), 0, 1)
    return jnp.concatenate(
        [jnp.concatenate([by_row[6 * core + t], by_row[6 * core + 3 + t]], axis=0) for core in range(2) for t in range(3)],
        axis=1,
    )


def finish(summed, field, gating, weight, gain):
    column = jnp.swapaxes(jnp.broadcast_to(gain, (8, H)), 0, 1)[:, :1]
    mixed = normalize(summed, column, 0).astype(BF16)
    update = lax.dot_general(
        mixed, weight, (((0,), (0,)), ((), ())), preferred_element_type=F32
    )
    update = jnp.concatenate([update[HALF * a : HALF * a + 48] for a in range(12)], axis=0)
    return field.astype(F32) + gating * update


def rows_of(own):
    by_row = jnp.swapaxes(own.astype(F32).reshape(HALF, 18, H), 0, 1)
    return by_row[:9], by_row[9:]


def moved(tile, lanes):
    return pltpu.roll(tile, lanes % H, 1) if lanes % H else tile


def matrix(by_row, side, channel):
    q = 2 * side + channel
    lane = lax.broadcasted_iota(jnp.int32, (16, H), 1)
    cut = lax.broadcasted_iota(jnp.int32, (HALF, H), 1) >= 96
    first, second, last = by_row[2 * q], by_row[2 * q + 1], by_row[8]
    across = jnp.where(cut, first, second)
    begins = ((first, 0), (first, 48), (across, 96), (second, 16), (second, 64), (second, 112))
    found = ([], [])
    for a in range(6):
        row, begin = begins[a]
        tiles = []
        for u in range(2):
            pair = []
            for e in range(2):
                at = slice(32 * u + 16 * e, 32 * u + 16 * e + 16)
                piece = moved(row[at], HALF * e - begin)
                if a == 5:
                    piece = jnp.where(lane < HALF * e + 16, piece, moved(last[at], HALF * e + 16 - 32 * q))
                pair.append(piece)
            tiles.append(jnp.where(lane < HALF, *pair))
        both = jnp.concatenate(tiles, axis=1)
        for half in range(2):
            found[half].append(both[8 * half : 8 * half + 8])
    return [jnp.concatenate(pieces, axis=0) for pieces in found]


def whole_matrix(cores, side, channel):
    parts = [matrix(by_row, side, channel) for by_row in cores]
    return [jnp.concatenate([parts[0][z1], parts[1][z1]], axis=1) for z1 in range(2)]


def squeezed(rows, squeeze):
    return jnp.dot(
        jnp.concatenate(rows, axis=0).astype(BF16), squeeze, preferred_element_type=F32
    ).astype(BF16)


def send_back(products, stretch):
    wide = jnp.dot(products.astype(BF16), stretch, preferred_element_type=F32)
    rows = []
    for core in range(2):
        for channel in range(2):
            for t in range(3):
                parts = []
                for u in range(2):
                    lanes = slice((2 * core + u) * H, (2 * core + u + 1) * H)
                    pair = [
                        jnp.concatenate([wide[at : at + 8, lanes], wide[at + 48 : at + 56, lanes]], axis=0)
                        for at in (96 * channel + 16 * t, 96 * channel + 16 * t + 8)
                    ]
                    parts.extend(halves(*pair))
                rows.append(jnp.concatenate(parts, axis=0))
    return by_device(rows).reshape(HALF, 3, 4, H).astype(BF16)


def all_rows(own, squeeze):
    cores = rows_of(own)
    rows = []
    for side in range(2):
        for channel in range(2):
            rows.extend(whole_matrix(cores, side, channel))
    return squeezed(rows, squeeze)


def start_kernel(pair_ref, weight_ref, gain_ref, out_ref, gate_ref):
    field = pair_ref[...].reshape(576, H).astype(F32)
    normed = normalize(field, gain_ref[0:1], 1).astype(BF16)
    weight = weight_ref[0]
    out_ref[...] = spread_sides(normed, weight)
    gate_ref[...] = gate_of(normed, weight)


def pack_kernel(own_ref, squeeze_ref, left_ref, right_ref):
    packed = all_rows(own_ref[...], squeeze_ref[...])
    left_ref[...] = packed[:192]
    for x in range(4):
        right_ref[x] = packed[192:]


def outgoing_kernel(left_ref, right_ref, stretch_ref, out_ref):
    products = []
    for channel in range(2):
        right = jnp.concatenate(
            [right_ref[x, 96 * channel + 48 * z1 : 96 * channel + 48 * z1 + 48] for z1 in range(2) for x in range(4)], axis=0
        )
        products.append(
            lax.dot_general(
                left_ref[96 * channel : 96 * channel + 96], right, (((1,), (1,)), ((), ())), preferred_element_type=F32
            )
        )
    out_ref[...] = send_back(jnp.concatenate(products, axis=0), stretch_ref[...])


def middle_kernel(
    arrived_ref, field_ref, gate_ref, out_weight_ref, weight_ref, gain_ref, out_ref, first_ref, next_gate_ref
):
    first = finish(
        summed_rows(arrived_ref[...]), field_ref[...].reshape(576, H), gate_ref[...], out_weight_ref[0], gain_ref[2:3]
    ).astype(BF16)
    normed = normalize(first.astype(F32), gain_ref[1:2], 1).astype(BF16)
    weight = weight_ref[1]
    out_ref[...] = spread_sides(normed, weight)
    first_ref[...] = first
    next_gate_ref[...] = gate_of(normed, weight)


def incoming_kernel(own_ref, squeeze_ref, out_ref):
    packed = all_rows(own_ref[...], squeeze_ref[...])
    for channel in range(2):
        product = lax.dot_general(
            packed[96 * channel : 96 * channel + 96],
            packed[192 + 96 * channel : 288 + 96 * channel],
            (((0,), (0,)), ((), ())),
            preferred_element_type=F32,
        ).astype(BF16)
        for x in range(4):
            for z1 in range(2):
                at, to = 192 * z1 + 48 * x, 96 * channel + 48 * z1
                out_ref[x, to : to + 48] = product[at : at + 48]


def sum_kernel(parts_ref, stretch_ref, out_ref):
    total = parts_ref[0].astype(F32)
    for x in range(1, 4):
        total = total + parts_ref[x].astype(F32)
    out_ref[...] = send_back(total, stretch_ref[...])


def end_kernel(arrived_ref, field_ref, gate_ref, out_weight_ref, gain_ref, other_ref, own_ref):
    final = finish(
        summed_rows(arrived_ref[...]), field_ref[...], gate_ref[...], out_weight_ref[1], gain_ref[3:4]
    ).astype(BF16)
    other_ref[...] = final[:288].reshape(6, 48, H)
    own_ref[...] = final[288:].reshape(6, 48, H)


def squeeze_matrix():
    places = np.pad(np.ones((4, 48), bool), ((0, 0), (0, 16))).reshape(-1).nonzero()[0]
    places = places.reshape(2, 2, 2, 4, 6).transpose(3, 4, 0, 1, 2).reshape(-1)
    block = np.arange(256)[:, None] == places[None, :]
    return np.kron(np.eye(2, dtype=bool), block).astype(jnp.bfloat16)


def call(kernel, outs, scratch=(), **specs):
    return pl.pallas_call(
        kernel,
        out_shape=[jax.ShapeDtypeStruct(shape, dtype) for shape, dtype in outs],
        scratch_shapes=list(scratch),
        compiler_params=pltpu.CompilerParams(vmem_limit_bytes=48 * 1024 * 1024),
        cost_estimate=pl.CostEstimate(flops=20_000_000, bytes_accessed=1_000_000, transcendentals=100_000),
        **specs,
    )


def shards(pair_field, proj_weight, out_weight, in_gain, out_gain):
    leads = lax.axis_index("core") == 1

    def exchange(array, axes):
        swap = functools.partial(lax.all_to_all, axis_name=axes, split_axis=0, concat_axis=0, tiled=True)
        return lax.cond(leads, swap, lambda same: same, array)

    squeeze, stretch = jnp.asarray(squeeze_matrix()), jnp.asarray(squeeze_matrix().T)
    gates, pairs = ((576, H), F32), ((576, H), BF16)
    sides, results = ((HALF, 9, 2, H), BF16), ((HALF, 3, 4, H), BF16)
    block, blocks = ((192, 384), BF16), ((4, 192, 384), BF16)

    gains = jnp.concatenate([in_gain, out_gain], axis=0)
    field = lax.all_gather(pair_field, "core", axis=0, tiled=False)
    sent, gating = call(start_kernel, [sides, gates])(field, proj_weight, gains)
    own = exchange(sent, SPREAD)
    left, right = call(pack_kernel, [block, blocks])(own, squeeze)
    right = exchange(right, "x")
    [back] = call(outgoing_kernel, [results])(left, right, stretch)
    arrived = exchange(back, SPREAD)

    sent, first_pair, gating = call(middle_kernel, [sides, pairs, gates])(
        arrived, field, gating, out_weight, proj_weight, gains
    )
    own = exchange(sent, SPREAD)
    [parts] = call(incoming_kernel, [blocks])(own, squeeze)
    parts = exchange(parts, "x")
    [back] = call(sum_kernel, [results])(parts, stretch)
    arrived = exchange(back, SPREAD)
    one = ((6, 48, H), BF16)
    other, mine = call(end_kernel, [one, one])(arrived, first_pair, gating, out_weight, gains)
    return jnp.where(leads, mine, lax.all_gather(other, "core", axis=0, tiled=False)[1])


def solution(mesh):
    fine = Mesh(mesh.devices.reshape(2, 2, 2, 2, 4, 4, 2), ("yh", "z2", "z1", "z0", "x", "yl", "core"))
    row, col = ("yh", "z2", "z1", "z0", "x"), ("yl", "core")
    return jax.shard_map(
        shards,
        mesh=fine,
        in_specs=(P(row, col, None), P(), P(), P(), P()),
        out_specs=P(row, col, None),
        check_vma=False,
    )
```

```python
import functools

import jax
import jax.numpy as jnp
import numpy as np
from jax import lax
from jax.experimental import pallas as pl
from jax.experimental.pallas import tpu as pltpu
from jax.sharding import Mesh
from jax.sharding import PartitionSpec as P

H = 128
HALF = 64
SPREAD = ("yl", "z1", "yh", "z2", "z0")
F32 = jnp.float32
BF16 = jnp.bfloat16


def normalize(values, gain, axis):
    mean = jnp.mean(values, axis=axis, keepdims=True)
    centred = values - mean
    spread = jnp.mean(centred * centred, axis=axis, keepdims=True)
    return centred * lax.rsqrt(spread + 1e-05) * gain


def halves(top, bottom):
    low = lax.broadcasted_iota(jnp.int32, top.shape, 1) < HALF
    return jnp.where(low, top, pltpu.roll(bottom, HALF, 1)), jnp.where(low, pltpu.roll(top, HALF, 1), bottom)


def by_device(rows):
    return jnp.swapaxes(jnp.stack(rows, axis=0), 0, 1)


def spread_sides(normed, weight):
    rows = []
    for core in range(2):
        projected = lax.dot_general(
            weight[:, : 4 * H],
            normed[288 * core : 288 * core + 288],
            (((0,), (1,)), ((), ())),
            preferred_element_type=F32,
        )
        ends = []
        for side in range(2):
            value = projected[2 * side * H : (2 * side + 1) * H]
            gate = projected[(2 * side + 1) * H : (2 * side + 2) * H]
            turned = jax.nn.sigmoid(gate) * value
            for channel in range(2):
                part = turned[channel * HALF : (channel + 1) * HALF]
                rows.extend([part[:, :H], part[:, H : 2 * H]])
                ends.append(part[:, 2 * H :])
        rows.append(jnp.concatenate(ends, axis=1))
    return by_device(rows).reshape(HALF, 9, 2, H).astype(BF16)


def gate_of(normed, weight):
    return jax.nn.sigmoid(jnp.dot(normed, weight[:, 4 * H :], preferred_element_type=F32))


def summed_rows(arrived):
    by_row = jnp.swapaxes(arrived.astype(F32).reshape(HALF, 12, H), 0, 1)
    return jnp.concatenate(
        [jnp.concatenate([by_row[6 * core + t], by_row[6 * core + 3 + t]], axis=0) for core in range(2) for t in range(3)],
        axis=1,
    )


def finish(summed, field, gating, weight, gain):
    column = jnp.swapaxes(jnp.broadcast_to(gain, (8, H)), 0, 1)[:, :1]
    mixed = normalize(summed, column, 0).astype(BF16)
    update = lax.dot_general(
        mixed, weight, (((0,), (0,)), ((), ())), preferred_element_type=F32
    )
    update = jnp.concatenate([update[HALF * a : HALF * a + 48] for a in range(12)], axis=0)
    return field.astype(F32) + gating * update


def rows_of(own):
    by_row = jnp.swapaxes(own.astype(F32).reshape(HALF, 18, H), 0, 1)
    return by_row[:9], by_row[9:]


def moved(tile, lanes):
    return pltpu.roll(tile, lanes % H, 1) if lanes % H else tile


def matrix(by_row, side, channel):
    q = 2 * side + channel
    lane = lax.broadcasted_iota(jnp.int32, (16, H), 1)
    cut = lax.broadcasted_iota(jnp.int32, (HALF, H), 1) >= 96
    first, second, last = by_row[2 * q], by_row[2 * q + 1], by_row[8]
    across = jnp.where(cut, first, second)
    begins = ((first, 0), (first, 48), (across, 96), (second, 16), (second, 64), (second, 112))
    found = ([], [])
    for a in range(6):
        row, begin = begins[a]
        tiles = []
        for u in range(2):
            pair = []
            for e in range(2):
                at = slice(32 * u + 16 * e, 32 * u + 16 * e + 16)
                piece = moved(row[at], HALF * e - begin)
                if a == 5:
                    piece = jnp.where(lane < HALF * e + 16, piece, moved(last[at], HALF * e + 16 - 32 * q))
                pair.append(piece)
            tiles.append(jnp.where(lane < HALF, *pair))
        both = jnp.concatenate(tiles, axis=1)
        for half in range(2):
            found[half].append(both[8 * half : 8 * half + 8])
    return [jnp.concatenate(pieces, axis=0) for pieces in found]


def whole_matrix(cores, side, channel):
    parts = [matrix(by_row, side, channel) for by_row in cores]
    return [jnp.concatenate([parts[0][z1], parts[1][z1]], axis=1) for z1 in range(2)]


def squeezed(rows, squeeze):
    return jnp.dot(
        jnp.concatenate(rows, axis=0).astype(BF16), squeeze, preferred_element_type=F32
    ).astype(BF16)


def send_back(products, stretch):
    wide = jnp.dot(products.astype(BF16), stretch, preferred_element_type=F32)
    rows = []
    for core in range(2):
        for channel in range(2):
            for t in range(3):
                parts = []
                for u in range(2):
                    lanes = slice((2 * core + u) * H, (2 * core + u + 1) * H)
                    pair = [
                        jnp.concatenate([wide[at : at + 8, lanes], wide[at + 48 : at + 56, lanes]], axis=0)
                        for at in (96 * channel + 16 * t, 96 * channel + 16 * t + 8)
                    ]
                    parts.extend(halves(*pair))
                rows.append(jnp.concatenate(parts, axis=0))
    return by_device(rows).reshape(HALF, 3, 4, H).astype(BF16)


def all_rows(own, squeeze):
    cores = rows_of(own)
    rows = []
    for side in range(2):
        for channel in range(2):
            rows.extend(whole_matrix(cores, side, channel))
    return squeezed(rows, squeeze)


def start_kernel(
    pair_ref, weight_hbm, in_gain_hbm, out_gain_hbm,
    out_ref, gate_ref, gain_ref,
    weight_ref, in_gain_ref, out_gain_ref, sems,
):
    moves = [(in_gain_hbm, in_gain_ref), (weight_hbm.at[0], weight_ref), (out_gain_hbm, out_gain_ref)]
    copies = [pltpu.make_async_copy(source, target, sems.at[n]) for n, (source, target) in enumerate(moves)]
    for copy in copies:
        copy.start()
    field = pair_ref[...].reshape(576, H).astype(F32)
    centred = normalize(field, 1.0, 1)
    copies[0].wait()
    normed = (centred * in_gain_ref[0:1]).astype(BF16)
    copies[1].wait()
    weight = weight_ref[...]
    out_ref[...] = spread_sides(normed, weight)
    gate_ref[...] = gate_of(normed, weight)
    copies[2].wait()
    gain_ref[0:2] = in_gain_ref[...]
    gain_ref[2:4] = out_gain_ref[...]


def pack_kernel(own_ref, squeeze_ref, left_ref, right_ref):
    packed = all_rows(own_ref[...], squeeze_ref[...])
    left_ref[...] = packed[:192]
    for x in range(4):
        right_ref[x] = packed[192:]


def outgoing_kernel(left_ref, right_ref, stretch_ref, out_ref):
    products = []
    for channel in range(2):
        right = jnp.concatenate(
            [right_ref[x, 96 * channel + 48 * z1 : 96 * channel + 48 * z1 + 48] for z1 in range(2) for x in range(4)], axis=0
        )
        products.append(
            lax.dot_general(
                left_ref[96 * channel : 96 * channel + 96], right, (((1,), (1,)), ((), ())), preferred_element_type=F32
            )
        )
    out_ref[...] = send_back(jnp.concatenate(products, axis=0), stretch_ref[...])


def middle_kernel(
    arrived_ref, field_ref, gate_ref, out_weight_ref, weight_ref, gain_ref, out_ref, first_ref, next_gate_ref
):
    first = finish(
        summed_rows(arrived_ref[...]), field_ref[...].reshape(576, H), gate_ref[...], out_weight_ref[0], gain_ref[2:3]
    ).astype(BF16)
    normed = normalize(first.astype(F32), gain_ref[1:2], 1).astype(BF16)
    weight = weight_ref[1]
    out_ref[...] = spread_sides(normed, weight)
    first_ref[...] = first
    next_gate_ref[...] = gate_of(normed, weight)


def incoming_kernel(own_ref, squeeze_ref, out_ref):
    packed = all_rows(own_ref[...], squeeze_ref[...])
    for channel in range(2):
        product = lax.dot_general(
            packed[96 * channel : 96 * channel + 96],
            packed[192 + 96 * channel : 288 + 96 * channel],
            (((0,), (0,)), ((), ())),
            preferred_element_type=F32,
        ).astype(BF16)
        for x in range(4):
            for z1 in range(2):
                at, to = 192 * z1 + 48 * x, 96 * channel + 48 * z1
                out_ref[x, to : to + 48] = product[at : at + 48]


def sum_kernel(parts_ref, stretch_ref, out_ref):
    total = parts_ref[0].astype(F32)
    for x in range(1, 4):
        total = total + parts_ref[x].astype(F32)
    out_ref[...] = send_back(total, stretch_ref[...])


def end_kernel(arrived_ref, field_ref, gate_ref, out_weight_ref, gain_ref, other_ref, own_ref):
    final = finish(
        summed_rows(arrived_ref[...]), field_ref[...], gate_ref[...], out_weight_ref[1], gain_ref[3:4]
    ).astype(BF16)
    other_ref[...] = final[:288].reshape(6, 48, H)
    own_ref[...] = final[288:].reshape(6, 48, H)


def squeeze_matrix():
    places = np.pad(np.ones((4, 48), bool), ((0, 0), (0, 16))).reshape(-1).nonzero()[0]
    places = places.reshape(2, 2, 2, 4, 6).transpose(3, 4, 0, 1, 2).reshape(-1)
    block = np.arange(256)[:, None] == places[None, :]
    return np.kron(np.eye(2, dtype=bool), block).astype(jnp.bfloat16)


def call(kernel, outs, scratch=(), **specs):
    return pl.pallas_call(
        kernel,
        out_shape=[jax.ShapeDtypeStruct(shape, dtype) for shape, dtype in outs],
        scratch_shapes=list(scratch),
        compiler_params=pltpu.CompilerParams(vmem_limit_bytes=48 * 1024 * 1024),
        cost_estimate=pl.CostEstimate(flops=20_000_000, bytes_accessed=1_000_000, transcendentals=100_000),
        **specs,
    )


def shards(pair_field, proj_weight, out_weight, in_gain, out_gain):
    leads = lax.axis_index("core") == 1

    def exchange(array, axes):
        swap = functools.partial(lax.all_to_all, axis_name=axes, split_axis=0, concat_axis=0, tiled=True)
        return lax.cond(leads, swap, jnp.zeros_like, array)

    squeeze, stretch = jnp.asarray(squeeze_matrix()), jnp.asarray(squeeze_matrix().T)
    gates, pairs = ((576, H), F32), ((576, H), BF16)
    sides, results = ((HALF, 9, 2, H), BF16), ((HALF, 3, 4, H), BF16)
    block, blocks = ((192, 384), BF16), ((4, 192, 384), BF16)

    held = [pltpu.with_memory_space_constraint(array, pltpu.HBM) for array in (proj_weight, in_gain, out_gain)]
    field = lax.all_gather(pair_field, "core", axis=0, tiled=False)
    sent, gating, gains = call(
        start_kernel,
        [sides, gates, ((4, H), F32)],
        [
            pltpu.VMEM((H, 5 * H), BF16),
            pltpu.VMEM((2, H), F32),
            pltpu.VMEM((2, H), F32),
            pltpu.SemaphoreType.DMA((3,)),
        ],
        in_specs=[pl.BlockSpec(memory_space=pltpu.VMEM)] + [pl.BlockSpec(memory_space=pltpu.HBM)] * 3,
    )(field, *held)
    own = exchange(sent, SPREAD)
    left, right = call(pack_kernel, [block, blocks])(own, squeeze)
    right = exchange(right, "x")
    [back] = call(outgoing_kernel, [results])(left, right, stretch)
    arrived = exchange(back, SPREAD)

    sent, first_pair, gating = call(middle_kernel, [sides, pairs, gates])(
        arrived, field, gating, out_weight, proj_weight, gains
    )
    own = exchange(sent, SPREAD)
    [parts] = call(incoming_kernel, [blocks])(own, squeeze)
    parts = exchange(parts, "x")
    [back] = call(sum_kernel, [results])(parts, stretch)
    arrived = exchange(back, SPREAD)
    one = ((6, 48, H), BF16)
    other, mine = call(end_kernel, [one, one])(arrived, first_pair, gating, out_weight, gains)
    return jnp.where(leads, mine, lax.all_gather(other, "core", axis=0, tiled=False)[1])


def solution(mesh):
    fine = Mesh(mesh.devices.reshape(2, 2, 2, 2, 4, 4, 2), ("yh", "z2", "z1", "z0", "x", "yl", "core"))
    row, col = ("yh", "z2", "z1", "z0", "x"), ("yl", "core")
    return jax.shard_map(
        shards,
        mesh=fine,
        in_specs=(P(row, col, None), P(), P(), P(), P()),
        out_specs=P(row, col, None),
        check_vma=False,
    )
```

```python
import functools

import jax
import jax.numpy as jnp
import numpy as np
from jax import lax
from jax.experimental import pallas as pl
from jax.experimental.pallas import tpu as pltpu
from jax.sharding import Mesh
from jax.sharding import PartitionSpec as P

H = 128
HALF = 64
SPREAD = ("yl", "z1", "yh", "z2", "z0")
F32 = jnp.float32
BF16 = jnp.bfloat16


def normalize(values, gain, axis):
    mean = jnp.mean(values, axis=axis, keepdims=True)
    centred = values - mean
    spread = jnp.mean(centred * centred, axis=axis, keepdims=True)
    return centred * lax.rsqrt(spread + 1e-05) * gain


def halves(top, bottom):
    low = lax.broadcasted_iota(jnp.int32, top.shape, 1) < HALF
    return jnp.where(low, top, pltpu.roll(bottom, HALF, 1)), jnp.where(low, pltpu.roll(top, HALF, 1), bottom)


def by_device(rows):
    pairs = [jnp.stack(rows[n : n + 2], axis=0) for n in range(0, len(rows), 2)]
    return jnp.transpose(jnp.stack(pairs, axis=0), (2, 0, 1, 3))


def spread_rows(projected):
    rows, ends = [], []
    for side in range(2):
        value = projected[2 * side * H : (2 * side + 1) * H]
        gate = projected[(2 * side + 1) * H : (2 * side + 2) * H]
        turned = jax.nn.sigmoid(gate) * value
        for channel in range(2):
            part = turned[channel * HALF : (channel + 1) * HALF]
            rows.extend([part[:, :H], part[:, H : 2 * H]])
            ends.append(part[:, 2 * H :])
    rows.extend([jnp.concatenate(ends, axis=1), jnp.zeros((HALF, H), F32)])
    return by_device(rows).astype(BF16)


def spread_sides(normed, weight):
    return spread_rows(
        lax.dot_general(weight[:, : 4 * H], normed, (((0,), (1,)), ((), ())), preferred_element_type=F32)
    )


def spread_turned(normed, weight):
    return spread_rows(
        lax.dot_general(weight[:, : 4 * H], normed, (((0,), (0,)), ((), ())), preferred_element_type=F32)
    )


def gate_of(normed, weight):
    return jax.nn.sigmoid(jnp.dot(normed, weight[:, 4 * H :], preferred_element_type=F32))


def summed_rows(arrived):
    by_row = jnp.swapaxes(arrived.astype(F32).reshape(HALF, 6, H), 0, 1)
    return jnp.concatenate([jnp.concatenate([by_row[t], by_row[3 + t]], axis=0) for t in range(3)], axis=1)


def column(gain):
    return jnp.swapaxes(jnp.broadcast_to(gain, (8, H)), 0, 1)[:, :1]


def moved(tile, lanes):
    return pltpu.roll(tile, lanes % H, 1) if lanes % H else tile


def closed_up(summed):
    lane = lax.broadcasted_iota(jnp.int32, (H, H), 1)
    tiles = [summed[:, t * H : (t + 1) * H] for t in range(3)]

    def piece(a, out):
        return moved(tiles[a // 2], 48 * a - HALF * (a % 2) - H * out)

    begin = jnp.where(lane < 48, piece(0, 0), jnp.where(lane < 96, piece(1, 0), piece(2, 0)))
    middle = jnp.where(
        lane < 16, piece(2, 1), jnp.where(lane < 64, piece(3, 1), jnp.where(lane < 112, piece(4, 1), piece(5, 1)))
    )
    return jnp.concatenate([begin, middle, piece(5, 2)[:, :32]], axis=1)


def finish(summed, field, gating, weight, gain):
    mixed = normalize(summed, column(gain), 0).astype(BF16)
    update = lax.dot_general(
        mixed, weight, (((0,), (0,)), ((), ())), preferred_element_type=F32
    )
    update = jnp.concatenate([update[HALF * a : HALF * a + 48] for a in range(6)], axis=0)
    return field.astype(F32) + gating * update


def rows_of(own):
    return jnp.swapaxes(own.astype(F32).reshape(HALF, 10, H), 0, 1)


def matrix(by_row, side, channel):
    q = 2 * side + channel
    lane = lax.broadcasted_iota(jnp.int32, (16, H), 1)
    cut = lax.broadcasted_iota(jnp.int32, (HALF, H), 1) >= 96
    first, second, last = by_row[2 * q], by_row[2 * q + 1], by_row[8]
    across = jnp.where(cut, first, second)
    begins = ((first, 0), (first, 48), (across, 96), (second, 16), (second, 64), (second, 112))
    found = ([], [])
    for a in range(6):
        row, begin = begins[a]
        tiles = []
        for u in range(2):
            pair = []
            for e in range(2):
                at = slice(32 * u + 16 * e, 32 * u + 16 * e + 16)
                piece = moved(row[at], HALF * e - begin)
                if a == 5:
                    piece = jnp.where(lane < HALF * e + 16, piece, moved(last[at], HALF * e + 16 - 32 * q))
                pair.append(piece)
            tiles.append(jnp.where(lane < HALF, *pair))
        both = jnp.concatenate(tiles, axis=1)
        for half in range(2):
            found[half].append(both[8 * half : 8 * half + 8])
    return [jnp.concatenate(pieces, axis=0) for pieces in found]


def whole_matrix(cores, side, channel):
    parts = [matrix(by_row, side, channel) for by_row in cores]
    return [jnp.concatenate([parts[0][z1], parts[1][z1]], axis=1) for z1 in range(2)]


def squeezed(rows, squeeze):
    return jnp.dot(
        jnp.concatenate(rows, axis=0).astype(BF16), squeeze, preferred_element_type=F32
    ).astype(BF16)


def send_back(product, stretch):
    wide = jnp.dot(product.astype(BF16), stretch, preferred_element_type=F32)
    rows = []
    for channel in range(2):
        for t in range(3):
            parts = []
            for u in range(2):
                lanes = slice((2 * channel + u) * H, (2 * channel + u + 1) * H)
                pair = [
                    jnp.concatenate([wide[8 * a : 8 * a + 8, lanes], wide[48 + 8 * a : 56 + 8 * a, lanes]], axis=0)
                    for a in (2 * t, 2 * t + 1)
                ]
                parts.extend(halves(*pair))
            rows.append(jnp.concatenate(parts, axis=0))
    return by_device(rows).astype(BF16)


def start_kernel(pair_ref, weight_ref, gain_ref, out_ref, gate_ref):
    field = pair_ref[...].reshape(288, H).astype(F32)
    normed = normalize(field, gain_ref[0:1], 1).astype(BF16)
    weight = weight_ref[...]
    out_ref[...] = spread_sides(normed, weight)
    gate_ref[...] = gate_of(normed, weight)


def pack_kernel(both_ref, squeeze_ref, left_ref, right_ref):
    cores = [rows_of(both_ref[core]) for core in range(2)]
    first = lax.axis_index("core") == 0
    rows = []
    for channel in range(2):
        rows.extend(whole_matrix(cores, 0, channel))
    for channel in range(2):
        rows.append(jnp.where(first, *whole_matrix(cores, 1, channel)))
    packed = squeezed(rows, squeeze_ref[...])
    left_ref[...] = packed[:192]
    for x in range(4):
        right_ref[x] = packed[192:]


def outgoing_kernel(left_ref, right_ref, stretch_ref, out_ref):
    left = jnp.concatenate([left_ref[:96], left_ref[96:]], axis=1)
    none = jnp.zeros((192, 384), BF16)
    right = [right_ref[:, 48 * channel : 48 * channel + 48].reshape(192, 384) for channel in range(2)]
    right = jnp.concatenate(
        [jnp.concatenate([right[0], none], axis=1), jnp.concatenate([none, right[1]], axis=1)], axis=0
    )
    product = lax.dot_general(left, right, (((1,), (1,)), ((), ())), preferred_element_type=F32)
    out_ref[...] = send_back(product, stretch_ref[...])


def middle_kernel(
    arrived_ref, field_ref, gate_ref, out_weight_ref, weight_ref, gain_ref, out_ref, first_ref, next_gate_ref
):
    field = jnp.swapaxes(field_ref[...].reshape(288, H).astype(F32), 0, 1)
    gating = jnp.swapaxes(gate_ref[...], 0, 1)
    mixed = normalize(closed_up(summed_rows(arrived_ref[...])), column(gain_ref[2:3]), 0).astype(BF16)
    update = lax.dot_general(out_weight_ref[0], mixed, (((0,), (0,)), ((), ())), preferred_element_type=F32)
    first = (field + gating * update).astype(BF16).astype(F32)
    normed = normalize(first, column(gain_ref[1:2]), 0).astype(BF16)
    weight = weight_ref[1]
    out_ref[...] = spread_turned(normed, weight)
    first_ref[...] = jnp.swapaxes(first, 0, 1).reshape(6, 48, H).astype(BF16)
    next_gate_ref[...] = jax.nn.sigmoid(
        lax.dot_general(normed, weight[:, 4 * H :], (((0,), (0,)), ((), ())), preferred_element_type=F32)
    )


def incoming_kernel(both_ref, squeeze_ref, stretch_ref, out_ref):
    cores = [rows_of(both_ref[core]) for core in range(2)]
    own = jnp.where(lax.axis_index("core") == 0, *cores)
    none = jnp.zeros((96, 256), F32)
    left, right = [], []
    for channel in range(2):
        left.extend(whole_matrix(cores, 0, channel))
        part = jnp.concatenate(matrix(own, 1, channel), axis=0)
        right.append(jnp.concatenate([none, part] if channel else [part, none], axis=1))
    left = lax.dot_general(
        stretch_ref[...],
        jnp.concatenate(left, axis=0).astype(BF16),
        (((1,), (1,)), ((), ())),
        preferred_element_type=F32,
    ).astype(BF16)
    product = jnp.dot(left, squeezed(right, squeeze_ref[...]), preferred_element_type=F32).astype(BF16)
    for x in range(4):
        for z1 in range(2):
            at = 192 * z1 + 48 * x
            out_ref[x, 48 * z1 : 48 * z1 + 48] = product[at : at + 48]


def sum_kernel(parts_ref, stretch_ref, out_ref):
    total = parts_ref[0].astype(F32)
    for x in range(1, 4):
        total = total + parts_ref[x].astype(F32)
    out_ref[...] = send_back(total, stretch_ref[...])


def end_kernel(arrived_ref, field_ref, gate_ref, out_weight_ref, gain_ref, out_ref):
    final = finish(
        summed_rows(arrived_ref[...]), field_ref[...].reshape(288, H), gate_ref[...], out_weight_ref[1], gain_ref[3:4]
    )
    out_ref[...] = final.reshape(6, 48, H).astype(BF16)


def squeeze_matrix():
    places = np.pad(np.ones((4, 48), bool), ((0, 0), (0, 16))).reshape(-1).nonzero()[0]
    places = places.reshape(2, 2, 2, 4, 6).transpose(3, 4, 0, 1, 2).reshape(-1)
    block = np.arange(256)[:, None] == places[None, :]
    return np.kron(np.eye(2, dtype=bool), block).astype(jnp.bfloat16)


def call(kernel, outs, scratch=(), **specs):
    return pl.pallas_call(
        kernel,
        out_shape=[jax.ShapeDtypeStruct(shape, dtype) for shape, dtype in outs],
        scratch_shapes=list(scratch),
        compiler_params=pltpu.CompilerParams(vmem_limit_bytes=48 * 1024 * 1024),
        cost_estimate=pl.CostEstimate(flops=20_000_000, bytes_accessed=1_000_000, transcendentals=100_000),
        **specs,
    )


def shards(pair_field, proj_weight, out_weight, in_gain, out_gain):
    exchange = functools.partial(lax.all_to_all, split_axis=0, concat_axis=0, tiled=True)
    squeeze, stretch = jnp.asarray(squeeze_matrix()), jnp.asarray(squeeze_matrix().T)
    pairs, gates = ((6, 48, H), BF16), ((288, H), F32)
    sides, results = ((HALF, 5, 2, H), BF16), ((HALF, 3, 2, H), BF16)
    block, blocks = ((192, 384), BF16), ((4, 96, 384), BF16)

    gains = jnp.concatenate([in_gain, out_gain], axis=0)
    sent, gating = call(start_kernel, [sides, gates])(pair_field, proj_weight[0], gains)
    own = exchange(sent, SPREAD)
    both = lax.all_gather(own, "core", axis=0, tiled=False)
    left, right = call(pack_kernel, [block, blocks])(both, squeeze)
    right = exchange(right, "x")
    [back] = call(outgoing_kernel, [results])(left, right, stretch)
    arrived = exchange(back, SPREAD)

    sent, first_pair, gating = call(middle_kernel, [sides, pairs, gates])(
        arrived, pair_field, gating, out_weight, proj_weight, gains
    )
    own = exchange(sent, SPREAD)
    both = lax.all_gather(own, "core", axis=0, tiled=False)
    [parts] = call(incoming_kernel, [blocks])(both, squeeze, stretch)
    parts = exchange(parts, "x")
    [back] = call(sum_kernel, [results])(parts, stretch)
    arrived = exchange(back, SPREAD)
    [out] = call(end_kernel, [pairs])(arrived, first_pair, gating, out_weight, gains)
    return out


def solution(mesh):
    fine = Mesh(mesh.devices.reshape(2, 2, 2, 2, 4, 4, 2), ("yh", "z2", "z1", "z0", "x", "yl", "core"))
    row, col = ("yh", "z2", "z1", "z0", "x"), ("yl", "core")
    return jax.shard_map(
        shards,
        mesh=fine,
        in_specs=(P(row, col, None), P(), P(), P(), P()),
        out_specs=P(row, col, None),
        check_vma=False,
    )
```

```python
import functools

import jax
import jax.numpy as jnp
import numpy as np
from jax import lax
from jax.experimental import pallas as pl
from jax.experimental.pallas import tpu as pltpu
from jax.sharding import Mesh
from jax.sharding import PartitionSpec as P

H = 128
HALF = 64
SPREAD = ("yl", "z1", "yh", "z2", "z0")
F32 = jnp.float32
BF16 = jnp.bfloat16


def normalize(values, gain, axis):
    mean = jnp.mean(values, axis=axis, keepdims=True)
    centred = values - mean
    spread = jnp.mean(centred * centred, axis=axis, keepdims=True)
    return centred * lax.rsqrt(spread + 1e-05) * gain


def halves(top, bottom):
    low = lax.broadcasted_iota(jnp.int32, top.shape, 1) < HALF
    return jnp.where(low, top, pltpu.roll(bottom, HALF, 1)), jnp.where(low, pltpu.roll(top, HALF, 1), bottom)


def by_device(rows):
    pairs = [jnp.stack(rows[n : n + 2], axis=0) for n in range(0, len(rows), 2)]
    return jnp.transpose(jnp.stack(pairs, axis=0), (2, 0, 1, 3))


def spread_rows(projected):
    rows, ends = [], []
    for side in range(2):
        value = projected[2 * side * H : (2 * side + 1) * H]
        gate = projected[(2 * side + 1) * H : (2 * side + 2) * H]
        turned = jax.nn.sigmoid(gate) * value
        for channel in range(2):
            part = turned[channel * HALF : (channel + 1) * HALF]
            rows.extend([part[:, :H], part[:, H : 2 * H]])
            ends.append(part[:, 2 * H :])
    rows.extend([jnp.concatenate(ends, axis=1), jnp.zeros((HALF, H), F32)])
    return by_device(rows).astype(BF16)


def spread_sides(normed, weight):
    return spread_rows(
        lax.dot_general(weight[:, : 4 * H], normed, (((0,), (1,)), ((), ())), preferred_element_type=F32)
    )


def spread_turned(normed, weight):
    return spread_rows(
        lax.dot_general(weight[:, : 4 * H], normed, (((0,), (0,)), ((), ())), preferred_element_type=F32)
    )


def gate_of(normed, weight):
    return jax.nn.sigmoid(jnp.dot(normed, weight[:, 4 * H :], preferred_element_type=F32))


def summed_rows(arrived):
    by_row = jnp.swapaxes(arrived.astype(F32).reshape(HALF, 6, H), 0, 1)
    return jnp.concatenate([jnp.concatenate([by_row[t], by_row[3 + t]], axis=0) for t in range(3)], axis=1)


def column(gain):
    return jnp.swapaxes(jnp.broadcast_to(gain, (8, H)), 0, 1)[:, :1]


def moved(tile, lanes):
    return pltpu.roll(tile, lanes % H, 1) if lanes % H else tile


def closed_up(summed):
    lane = lax.broadcasted_iota(jnp.int32, (H, H), 1)
    tiles = [summed[:, t * H : (t + 1) * H] for t in range(3)]

    def piece(a, out):
        return moved(tiles[a // 2], 48 * a - HALF * (a % 2) - H * out)

    begin = jnp.where(lane < 48, piece(0, 0), jnp.where(lane < 96, piece(1, 0), piece(2, 0)))
    middle = jnp.where(
        lane < 16, piece(2, 1), jnp.where(lane < 64, piece(3, 1), jnp.where(lane < 112, piece(4, 1), piece(5, 1)))
    )
    return jnp.concatenate([begin, middle, piece(5, 2)[:, :32]], axis=1)


def finish(summed, field, gating, weight, gain):
    mixed = normalize(summed, column(gain), 0).astype(BF16)
    update = lax.dot_general(
        mixed, weight, (((0,), (0,)), ((), ())), preferred_element_type=F32
    )
    update = jnp.concatenate([update[HALF * a : HALF * a + 48] for a in range(6)], axis=0)
    return field.astype(F32) + gating * update


def rows_of(own):
    return jnp.swapaxes(own.astype(F32).reshape(HALF, 10, H), 0, 1)


def matrix(by_row, side, channel):
    q = 2 * side + channel
    lane = lax.broadcasted_iota(jnp.int32, (16, H), 1)
    cut = lax.broadcasted_iota(jnp.int32, (HALF, H), 1) >= 96
    first, second, last = by_row[2 * q], by_row[2 * q + 1], by_row[8]
    across = jnp.where(cut, first, second)
    begins = ((first, 0), (first, 48), (across, 96), (second, 16), (second, 64), (second, 112))
    found = ([], [])
    for a in range(6):
        row, begin = begins[a]
        tiles = []
        for u in range(2):
            pair = []
            for e in range(2):
                at = slice(32 * u + 16 * e, 32 * u + 16 * e + 16)
                piece = moved(row[at], HALF * e - begin)
                if a == 5:
                    piece = jnp.where(lane < HALF * e + 16, piece, moved(last[at], HALF * e + 16 - 32 * q))
                pair.append(piece)
            tiles.append(jnp.where(lane < HALF, *pair))
        both = jnp.concatenate(tiles, axis=1)
        for half in range(2):
            found[half].append(both[8 * half : 8 * half + 8])
    return [jnp.concatenate(pieces, axis=0) for pieces in found]


def whole_matrix(cores, side, channel):
    parts = [matrix(by_row, side, channel) for by_row in cores]
    return [jnp.concatenate([parts[0][z1], parts[1][z1]], axis=1) for z1 in range(2)]


def squeezed(rows, squeeze):
    return jnp.dot(
        jnp.concatenate(rows, axis=0).astype(BF16), squeeze, preferred_element_type=F32
    ).astype(BF16)


def send_back(product, stretch):
    wide = jnp.dot(product.astype(BF16), stretch, preferred_element_type=F32)
    rows = []
    for channel in range(2):
        for t in range(3):
            parts = []
            for u in range(2):
                lanes = slice((2 * channel + u) * H, (2 * channel + u + 1) * H)
                pair = [
                    jnp.concatenate([wide[8 * a : 8 * a + 8, lanes], wide[48 + 8 * a : 56 + 8 * a, lanes]], axis=0)
                    for a in (2 * t, 2 * t + 1)
                ]
                parts.extend(halves(*pair))
            rows.append(jnp.concatenate(parts, axis=0))
    return by_device(rows).astype(BF16)


def start_kernel(
    pair_hbm, weight_hbm, in_gain_hbm, out_gain_hbm,
    out_ref, gate_ref, gain_ref,
    pair_ref, weight_ref, in_gain_ref, out_gain_ref, sems,
):
    moves = [(in_gain_hbm, in_gain_ref)]
    moves.extend((pair_hbm.at[n : n + 3], pair_ref.at[n : n + 3]) for n in (0, 3))
    moves.extend((weight_hbm.at[0, n : n + 32], weight_ref.at[n : n + 32]) for n in range(0, H, 32))
    moves.append((out_gain_hbm, out_gain_ref))
    copies = [pltpu.make_async_copy(source, target, sems.at[n]) for n, (source, target) in enumerate(moves)]
    for copy in copies:
        copy.start()
    for copy in copies[:3]:
        copy.wait()
    field = pair_ref[...].reshape(288, H).astype(F32)
    normed = normalize(field, in_gain_ref[0:1], 1).astype(BF16)
    for copy in copies[3:]:
        copy.wait()
    weight = weight_ref[...]
    out_ref[...] = spread_sides(normed, weight)
    gate_ref[...] = gate_of(normed, weight)
    gain_ref[0:2] = in_gain_ref[...]
    gain_ref[2:4] = out_gain_ref[...]


def pack_kernel(both_ref, squeeze_ref, left_ref, right_ref):
    cores = [rows_of(both_ref[core]) for core in range(2)]
    first = lax.axis_index("core") == 0
    rows = []
    for channel in range(2):
        rows.extend(whole_matrix(cores, 0, channel))
    for channel in range(2):
        rows.append(jnp.where(first, *whole_matrix(cores, 1, channel)))
    packed = squeezed(rows, squeeze_ref[...])
    left_ref[...] = packed[:192]
    for x in range(4):
        right_ref[x] = packed[192:]


def outgoing_kernel(left_ref, right_ref, stretch_ref, out_ref):
    left = jnp.concatenate([left_ref[:96], left_ref[96:]], axis=1)
    none = jnp.zeros((192, 384), BF16)
    right = [right_ref[:, 48 * channel : 48 * channel + 48].reshape(192, 384) for channel in range(2)]
    right = jnp.concatenate(
        [jnp.concatenate([right[0], none], axis=1), jnp.concatenate([none, right[1]], axis=1)], axis=0
    )
    product = lax.dot_general(left, right, (((1,), (1,)), ((), ())), preferred_element_type=F32)
    out_ref[...] = send_back(product, stretch_ref[...])


def middle_kernel(
    arrived_ref, field_ref, gate_ref, out_weight_ref, weight_ref, gain_ref, out_ref, first_ref, next_gate_ref
):
    field = jnp.swapaxes(field_ref[...].reshape(288, H).astype(F32), 0, 1)
    gating = jnp.swapaxes(gate_ref[...], 0, 1)
    mixed = normalize(closed_up(summed_rows(arrived_ref[...])), column(gain_ref[2:3]), 0).astype(BF16)
    update = lax.dot_general(out_weight_ref[0], mixed, (((0,), (0,)), ((), ())), preferred_element_type=F32)
    first = (field + gating * update).astype(BF16).astype(F32)
    normed = normalize(first, column(gain_ref[1:2]), 0).astype(BF16)
    weight = weight_ref[1]
    out_ref[...] = spread_turned(normed, weight)
    first_ref[...] = jnp.swapaxes(first, 0, 1).reshape(6, 48, H).astype(BF16)
    next_gate_ref[...] = jax.nn.sigmoid(
        lax.dot_general(normed, weight[:, 4 * H :], (((0,), (0,)), ((), ())), preferred_element_type=F32)
    )


def incoming_kernel(both_ref, squeeze_ref, stretch_ref, out_ref):
    cores = [rows_of(both_ref[core]) for core in range(2)]
    own = jnp.where(lax.axis_index("core") == 0, *cores)
    none = jnp.zeros((96, 256), F32)
    left, right = [], []
    for channel in range(2):
        left.extend(whole_matrix(cores, 0, channel))
        part = jnp.concatenate(matrix(own, 1, channel), axis=0)
        right.append(jnp.concatenate([none, part] if channel else [part, none], axis=1))
    left = lax.dot_general(
        stretch_ref[...],
        jnp.concatenate(left, axis=0).astype(BF16),
        (((1,), (1,)), ((), ())),
        preferred_element_type=F32,
    ).astype(BF16)
    product = jnp.dot(left, squeezed(right, squeeze_ref[...]), preferred_element_type=F32).astype(BF16)
    for x in range(4):
        for z1 in range(2):
            at = 192 * z1 + 48 * x
            out_ref[x, 48 * z1 : 48 * z1 + 48] = product[at : at + 48]


def sum_kernel(parts_ref, stretch_ref, out_ref):
    total = parts_ref[0].astype(F32)
    for x in range(1, 4):
        total = total + parts_ref[x].astype(F32)
    out_ref[...] = send_back(total, stretch_ref[...])


def end_kernel(arrived_ref, field_ref, gate_ref, out_weight_ref, gain_ref, out_ref):
    final = finish(
        summed_rows(arrived_ref[...]), field_ref[...].reshape(288, H), gate_ref[...], out_weight_ref[1], gain_ref[3:4]
    )
    out_ref[...] = final.reshape(6, 48, H).astype(BF16)


def squeeze_matrix():
    places = np.pad(np.ones((4, 48), bool), ((0, 0), (0, 16))).reshape(-1).nonzero()[0]
    places = places.reshape(2, 2, 2, 4, 6).transpose(3, 4, 0, 1, 2).reshape(-1)
    block = np.arange(256)[:, None] == places[None, :]
    return np.kron(np.eye(2, dtype=bool), block).astype(jnp.bfloat16)


def call(kernel, outs, scratch=(), **specs):
    return pl.pallas_call(
        kernel,
        out_shape=[jax.ShapeDtypeStruct(shape, dtype) for shape, dtype in outs],
        scratch_shapes=list(scratch),
        compiler_params=pltpu.CompilerParams(vmem_limit_bytes=48 * 1024 * 1024),
        cost_estimate=pl.CostEstimate(flops=20_000_000, bytes_accessed=1_000_000, transcendentals=100_000),
        **specs,
    )


def shards(pair_field, proj_weight, out_weight, in_gain, out_gain):
    exchange = functools.partial(lax.all_to_all, split_axis=0, concat_axis=0, tiled=True)
    squeeze, stretch = jnp.asarray(squeeze_matrix()), jnp.asarray(squeeze_matrix().T)
    pairs, gates = ((6, 48, H), BF16), ((288, H), F32)
    sides, results = ((HALF, 5, 2, H), BF16), ((HALF, 3, 2, H), BF16)
    block, blocks = ((192, 384), BF16), ((4, 96, 384), BF16)

    held = [
        pltpu.with_memory_space_constraint(array, pltpu.HBM)
        for array in (pair_field, proj_weight, in_gain, out_gain)
    ]
    sent, gating, gains = call(
        start_kernel,
        [sides, gates, ((4, H), F32)],
        [
            pltpu.VMEM((6, 48, H), BF16),
            pltpu.VMEM((H, 5 * H), BF16),
            pltpu.VMEM((2, H), F32),
            pltpu.VMEM((2, H), F32),
            pltpu.SemaphoreType.DMA((8,)),
        ],
        in_specs=[pl.BlockSpec(memory_space=pltpu.HBM)] * 4,
    )(*held)
    own = exchange(sent, SPREAD)
    both = lax.all_gather(own, "core", axis=0, tiled=False)
    left, right = call(pack_kernel, [block, blocks])(both, squeeze)
    right = exchange(right, "x")
    [back] = call(outgoing_kernel, [results])(left, right, stretch)
    arrived = exchange(back, SPREAD)

    sent, first_pair, gating = call(middle_kernel, [sides, pairs, gates])(
        arrived, pair_field, gating, out_weight, proj_weight, gains
    )
    own = exchange(sent, SPREAD)
    both = lax.all_gather(own, "core", axis=0, tiled=False)
    [parts] = call(incoming_kernel, [blocks])(both, squeeze, stretch)
    parts = exchange(parts, "x")
    [back] = call(sum_kernel, [results])(parts, stretch)
    arrived = exchange(back, SPREAD)
    [out] = call(end_kernel, [pairs])(arrived, first_pair, gating, out_weight, gains)
    return out


def solution(mesh):
    fine = Mesh(mesh.devices.reshape(2, 2, 2, 2, 4, 4, 2), ("yh", "z2", "z1", "z0", "x", "yl", "core"))
    row, col = ("yh", "z2", "z1", "z0", "x"), ("yl", "core")
    return jax.shard_map(
        shards,
        mesh=fine,
        in_specs=(P(row, col, None), P(), P(), P(), P()),
        out_specs=P(row, col, None),
        check_vma=False,
    )
```

```python
import functools

import jax
import jax.numpy as jnp
import numpy as np
from jax import lax
from jax.experimental import pallas as pl
from jax.experimental.pallas import tpu as pltpu
from jax.sharding import Mesh
from jax.sharding import PartitionSpec as P

H = 128
HALF = 64
SPREAD = ("yl", "z1", "yh", "z2", "z0")
F32 = jnp.float32
BF16 = jnp.bfloat16


def normalize(values, gain, axis):
    mean = jnp.mean(values, axis=axis, keepdims=True)
    centred = values - mean
    spread = jnp.mean(centred * centred, axis=axis, keepdims=True)
    return centred * lax.rsqrt(spread + 1e-05) * gain


def halves(top, bottom):
    low = lax.broadcasted_iota(jnp.int32, top.shape, 1) < HALF
    return jnp.where(low, top, pltpu.roll(bottom, HALF, 1)), jnp.where(low, pltpu.roll(top, HALF, 1), bottom)


def by_device(rows):
    pairs = [jnp.stack(rows[n : n + 2], axis=0) for n in range(0, len(rows), 2)]
    return jnp.transpose(jnp.stack(pairs, axis=0), (2, 0, 1, 3))


def spread_rows(projected):
    rows, ends = [], []
    for side in range(2):
        value = projected[2 * side * H : (2 * side + 1) * H]
        gate = projected[(2 * side + 1) * H : (2 * side + 2) * H]
        turned = jax.nn.sigmoid(gate) * value
        for channel in range(2):
            part = turned[channel * HALF : (channel + 1) * HALF]
            rows.extend([part[:, :H], part[:, H : 2 * H]])
            ends.append(part[:, 2 * H :])
    rows.extend([jnp.concatenate(ends, axis=1), jnp.zeros((HALF, H), F32)])
    return by_device(rows).astype(BF16)


def spread_sides(normed, weight):
    return spread_rows(
        lax.dot_general(weight[:, : 4 * H], normed, (((0,), (1,)), ((), ())), preferred_element_type=F32)
    )


def spread_turned(normed, weight):
    return spread_rows(
        lax.dot_general(weight[:, : 4 * H], normed, (((0,), (0,)), ((), ())), preferred_element_type=F32)
    )


def gate_of(normed, weight):
    return jax.nn.sigmoid(jnp.dot(normed, weight[:, 4 * H :], preferred_element_type=F32))


def summed_rows(arrived):
    by_row = jnp.swapaxes(arrived.astype(F32).reshape(HALF, 6, H), 0, 1)
    return jnp.concatenate([jnp.concatenate([by_row[t], by_row[3 + t]], axis=0) for t in range(3)], axis=1)


def column(gain):
    return jnp.swapaxes(jnp.broadcast_to(gain, (8, H)), 0, 1)[:, :1]


def moved(tile, lanes):
    return pltpu.roll(tile, lanes % H, 1) if lanes % H else tile


def closed_up(summed):
    lane = lax.broadcasted_iota(jnp.int32, (H, H), 1)
    tiles = [summed[:, t * H : (t + 1) * H] for t in range(3)]

    def piece(a, out):
        return moved(tiles[a // 2], 48 * a - HALF * (a % 2) - H * out)

    begin = jnp.where(lane < 48, piece(0, 0), jnp.where(lane < 96, piece(1, 0), piece(2, 0)))
    middle = jnp.where(
        lane < 16, piece(2, 1), jnp.where(lane < 64, piece(3, 1), jnp.where(lane < 112, piece(4, 1), piece(5, 1)))
    )
    return jnp.concatenate([begin, middle, piece(5, 2)[:, :32]], axis=1)


def finish(summed, field, gating, weight, gain):
    mixed = normalize(summed, column(gain), 0).astype(BF16)
    update = lax.dot_general(
        mixed, weight, (((0,), (0,)), ((), ())), preferred_element_type=F32
    )
    update = jnp.concatenate([update[HALF * a : HALF * a + 48] for a in range(6)], axis=0)
    return field.astype(F32) + gating * update


def rows_of(own):
    return jnp.swapaxes(own.astype(F32).reshape(HALF, 10, H), 0, 1)


def matrix(by_row, side, channel):
    q = 2 * side + channel
    lane = lax.broadcasted_iota(jnp.int32, (16, H), 1)
    cut = lax.broadcasted_iota(jnp.int32, (HALF, H), 1) >= 96
    first, second, last = by_row[2 * q], by_row[2 * q + 1], by_row[8]
    across = jnp.where(cut, first, second)
    begins = ((first, 0), (first, 48), (across, 96), (second, 16), (second, 64), (second, 112))
    found = ([], [])
    for a in range(6):
        row, begin = begins[a]
        tiles = []
        for u in range(2):
            pair = []
            for e in range(2):
                at = slice(32 * u + 16 * e, 32 * u + 16 * e + 16)
                piece = moved(row[at], HALF * e - begin)
                if a == 5:
                    piece = jnp.where(lane < HALF * e + 16, piece, moved(last[at], HALF * e + 16 - 32 * q))
                pair.append(piece)
            tiles.append(jnp.where(lane < HALF, *pair))
        both = jnp.concatenate(tiles, axis=1)
        for half in range(2):
            found[half].append(both[8 * half : 8 * half + 8])
    return [jnp.concatenate(pieces, axis=0) for pieces in found]


def whole_matrix(cores, side, channel):
    parts = [matrix(by_row, side, channel) for by_row in cores]
    return [jnp.concatenate([parts[0][z1], parts[1][z1]], axis=1) for z1 in range(2)]


def squeezed(rows, squeeze):
    return jnp.dot(
        jnp.concatenate(rows, axis=0).astype(BF16), squeeze, preferred_element_type=F32
    ).astype(BF16)


def send_back(product, stretch):
    wide = jnp.dot(product.astype(BF16), stretch, preferred_element_type=F32)
    rows = []
    for channel in range(2):
        for t in range(3):
            parts = []
            for u in range(2):
                lanes = slice((2 * channel + u) * H, (2 * channel + u + 1) * H)
                pair = [
                    jnp.concatenate([wide[8 * a : 8 * a + 8, lanes], wide[48 + 8 * a : 56 + 8 * a, lanes]], axis=0)
                    for a in (2 * t, 2 * t + 1)
                ]
                parts.extend(halves(*pair))
            rows.append(jnp.concatenate(parts, axis=0))
    return by_device(rows).astype(BF16)


def start_kernel(pair_ref, weight_ref, gain_ref, out_ref, gate_ref):
    field = pair_ref[...].reshape(288, H).astype(F32)
    normed = normalize(field, gain_ref[0:1], 1).astype(BF16)
    weight = weight_ref[...]
    out_ref[...] = spread_sides(normed, weight)
    gate_ref[...] = gate_of(normed, weight)


def pack_kernel(both_ref, squeeze_ref, left_ref, right_ref):
    cores = [rows_of(both_ref[core]) for core in range(2)]
    first = lax.axis_index("core") == 0
    rows = []
    for channel in range(2):
        rows.extend(whole_matrix(cores, 0, channel))
    for channel in range(2):
        rows.append(jnp.where(first, *whole_matrix(cores, 1, channel)))
    packed = squeezed(rows, squeeze_ref[...])
    left_ref[...] = packed[:192]
    for x in range(4):
        right_ref[x] = packed[192:]


def outgoing_kernel(left_ref, right_ref, stretch_ref, out_ref):
    left = jnp.concatenate([left_ref[:96], left_ref[96:]], axis=1)
    none = jnp.zeros((192, 384), BF16)
    right = [right_ref[:, 48 * channel : 48 * channel + 48].reshape(192, 384) for channel in range(2)]
    right = jnp.concatenate(
        [jnp.concatenate([right[0], none], axis=1), jnp.concatenate([none, right[1]], axis=1)], axis=0
    )
    product = lax.dot_general(left, right, (((1,), (1,)), ((), ())), preferred_element_type=F32)
    out_ref[...] = send_back(product, stretch_ref[...])


def middle_kernel(
    arrived_ref, field_ref, gate_ref, out_weight_ref, weight_ref, gain_ref, out_ref, first_ref, next_gate_ref
):
    field = jnp.swapaxes(field_ref[...].reshape(288, H).astype(F32), 0, 1)
    gating = jnp.swapaxes(gate_ref[...], 0, 1)
    mixed = normalize(closed_up(summed_rows(arrived_ref[...])), column(gain_ref[2:3]), 0).astype(BF16)
    update = lax.dot_general(out_weight_ref[0], mixed, (((0,), (0,)), ((), ())), preferred_element_type=F32)
    first = (field + gating * update).astype(BF16).astype(F32)
    normed = normalize(first, column(gain_ref[1:2]), 0).astype(BF16)
    weight = weight_ref[1]
    out_ref[...] = spread_turned(normed, weight)
    first_ref[...] = jnp.swapaxes(first, 0, 1).reshape(6, 48, H).astype(BF16)
    next_gate_ref[...] = jax.nn.sigmoid(
        lax.dot_general(normed, weight[:, 4 * H :], (((0,), (0,)), ((), ())), preferred_element_type=F32)
    )


def incoming_kernel(both_ref, squeeze_ref, stretch_ref, out_ref):
    cores = [rows_of(both_ref[core]) for core in range(2)]
    own = jnp.where(lax.axis_index("core") == 0, *cores)
    left, right = [], []
    for channel in range(2):
        left.extend(whole_matrix(cores, 0, channel))
        right.append(squeezed(matrix(own, 1, channel), squeeze_ref[256 * channel : 256 * channel + 256]))
    left = lax.dot_general(
        stretch_ref[...],
        jnp.concatenate(left, axis=0).astype(BF16),
        (((1,), (1,)), ((), ())),
        preferred_element_type=F32,
    ).astype(BF16)
    product = jnp.dot(left, jnp.concatenate(right, axis=0), preferred_element_type=F32).astype(BF16)
    for x in range(4):
        for z1 in range(2):
            at = 192 * z1 + 48 * x
            out_ref[x, 48 * z1 : 48 * z1 + 48] = product[at : at + 48]


def sum_kernel(parts_ref, stretch_ref, out_ref):
    total = parts_ref[0].astype(F32)
    for x in range(1, 4):
        total = total + parts_ref[x].astype(F32)
    out_ref[...] = send_back(total, stretch_ref[...])


def end_kernel(arrived_ref, field_ref, gate_ref, out_weight_ref, gain_ref, out_ref):
    final = finish(
        summed_rows(arrived_ref[...]), field_ref[...].reshape(288, H), gate_ref[...], out_weight_ref[1], gain_ref[3:4]
    )
    out_ref[...] = final.reshape(6, 48, H).astype(BF16)


def squeeze_matrix():
    places = np.pad(np.ones((4, 48), bool), ((0, 0), (0, 16))).reshape(-1).nonzero()[0]
    places = places.reshape(2, 2, 2, 4, 6).transpose(3, 4, 0, 1, 2).reshape(-1)
    block = np.arange(256)[:, None] == places[None, :]
    return np.kron(np.eye(2, dtype=bool), block).astype(jnp.bfloat16)


def call(kernel, outs, scratch=(), **specs):
    return pl.pallas_call(
        kernel,
        out_shape=[jax.ShapeDtypeStruct(shape, dtype) for shape, dtype in outs],
        scratch_shapes=list(scratch),
        compiler_params=pltpu.CompilerParams(vmem_limit_bytes=48 * 1024 * 1024),
        cost_estimate=pl.CostEstimate(flops=20_000_000, bytes_accessed=1_000_000, transcendentals=100_000),
        **specs,
    )


def shards(pair_field, proj_weight, out_weight, in_gain, out_gain):
    exchange = functools.partial(lax.all_to_all, split_axis=0, concat_axis=0, tiled=True)
    squeeze, stretch = jnp.asarray(squeeze_matrix()), jnp.asarray(squeeze_matrix().T)
    pairs, gates = ((6, 48, H), BF16), ((288, H), F32)
    sides, results = ((HALF, 5, 2, H), BF16), ((HALF, 3, 2, H), BF16)
    block, blocks = ((192, 384), BF16), ((4, 96, 384), BF16)

    gains = jnp.concatenate([in_gain, out_gain], axis=0)
    sent, gating = call(start_kernel, [sides, gates])(pair_field, proj_weight[0], gains)
    own = exchange(sent, SPREAD)
    both = lax.all_gather(own, "core", axis=0, tiled=False)
    left, right = call(pack_kernel, [block, blocks])(both, squeeze)
    right = exchange(right, "x")
    [back] = call(outgoing_kernel, [results])(left, right, stretch)
    arrived = exchange(back, SPREAD)

    sent, first_pair, gating = call(middle_kernel, [sides, pairs, gates])(
        arrived, pair_field, gating, out_weight, proj_weight, gains
    )
    own = exchange(sent, SPREAD)
    both = lax.all_gather(own, "core", axis=0, tiled=False)
    [parts] = call(incoming_kernel, [blocks])(both, squeeze, stretch)
    parts = exchange(parts, "x")
    [back] = call(sum_kernel, [results])(parts, stretch)
    arrived = exchange(back, SPREAD)
    [out] = call(end_kernel, [pairs])(arrived, first_pair, gating, out_weight, gains)
    return out


def solution(mesh):
    fine = Mesh(mesh.devices.reshape(2, 2, 2, 2, 4, 4, 2), ("yh", "z2", "z1", "z0", "x", "yl", "core"))
    row, col = ("yh", "z2", "z1", "z0", "x"), ("yl", "core")
    return jax.shard_map(
        shards,
        mesh=fine,
        in_specs=(P(row, col, None), P(), P(), P(), P()),
        out_specs=P(row, col, None),
        check_vma=False,
    )
```

```python
import functools

import jax
import jax.numpy as jnp
import numpy as np
from jax import lax
from jax.experimental import pallas as pl
from jax.experimental.pallas import tpu as pltpu
from jax.sharding import Mesh
from jax.sharding import PartitionSpec as P

H = 128
HALF = 64
SPREAD = ("yl", "z1", "yh", "z2", "z0")
F32 = jnp.float32
BF16 = jnp.bfloat16


def normalize(values, gain, axis):
    mean = jnp.mean(values, axis=axis, keepdims=True)
    centred = values - mean
    spread = jnp.mean(centred * centred, axis=axis, keepdims=True)
    return centred * lax.rsqrt(spread + 1e-05) * gain


def halves(top, bottom):
    low = lax.broadcasted_iota(jnp.int32, top.shape, 1) < HALF
    return jnp.where(low, top, pltpu.roll(bottom, HALF, 1)), jnp.where(low, pltpu.roll(top, HALF, 1), bottom)


def by_device(rows):
    pairs = [jnp.stack(rows[n : n + 2], axis=0) for n in range(0, len(rows), 2)]
    return jnp.transpose(jnp.stack(pairs, axis=0), (2, 0, 1, 3))


def spread_rows(projected):
    rows, ends = [], []
    for side in range(2):
        value = projected[2 * side * H : (2 * side + 1) * H]
        gate = projected[(2 * side + 1) * H : (2 * side + 2) * H]
        turned = jax.nn.sigmoid(gate) * value
        for channel in range(2):
            part = turned[channel * HALF : (channel + 1) * HALF]
            rows.extend([part[:, :H], part[:, H : 2 * H]])
            ends.append(part[:, 2 * H :])
    rows.extend([jnp.concatenate(ends, axis=1), jnp.zeros((HALF, H), F32)])
    return by_device(rows).astype(BF16)


def spread_turned(normed, weight):
    return spread_rows(
        lax.dot_general(weight[:, : 4 * H], normed, (((0,), (0,)), ((), ())), preferred_element_type=F32)
    )


def summed_rows(arrived):
    by_row = jnp.swapaxes(arrived.astype(F32).reshape(HALF, 6, H), 0, 1)
    return jnp.concatenate([jnp.concatenate([by_row[t], by_row[3 + t]], axis=0) for t in range(3)], axis=1)


def column(gain):
    return jnp.swapaxes(jnp.broadcast_to(gain, (8, H)), 0, 1)[:, :1]


def moved(tile, lanes):
    return pltpu.roll(tile, lanes % H, 1) if lanes % H else tile


def closed_up(summed):
    lane = lax.broadcasted_iota(jnp.int32, (H, H), 1)
    tiles = [summed[:, t * H : (t + 1) * H] for t in range(3)]

    def piece(a, out):
        return moved(tiles[a // 2], 48 * a - HALF * (a % 2) - H * out)

    begin = jnp.where(lane < 48, piece(0, 0), jnp.where(lane < 96, piece(1, 0), piece(2, 0)))
    middle = jnp.where(
        lane < 16, piece(2, 1), jnp.where(lane < 64, piece(3, 1), jnp.where(lane < 112, piece(4, 1), piece(5, 1)))
    )
    return jnp.concatenate([begin, middle, piece(5, 2)[:, :32]], axis=1)


def finish(summed, field, gating, weight, gain):
    mixed = normalize(summed, column(gain), 0).astype(BF16)
    update = lax.dot_general(
        mixed, weight, (((0,), (0,)), ((), ())), preferred_element_type=F32
    )
    update = jnp.concatenate([update[HALF * a : HALF * a + 48] for a in range(6)], axis=0)
    return field.astype(F32) + gating * update


def rows_of(own):
    return jnp.swapaxes(own.astype(F32).reshape(HALF, 10, H), 0, 1)


def matrix(by_row, side, channel):
    q = 2 * side + channel
    lane = lax.broadcasted_iota(jnp.int32, (16, H), 1)
    cut = lax.broadcasted_iota(jnp.int32, (HALF, H), 1) >= 96
    first, second, last = by_row[2 * q], by_row[2 * q + 1], by_row[8]
    across = jnp.where(cut, first, second)
    begins = ((first, 0), (first, 48), (across, 96), (second, 16), (second, 64), (second, 112))
    found = ([], [])
    for a in range(6):
        row, begin = begins[a]
        tiles = []
        for u in range(2):
            pair = []
            for e in range(2):
                at = slice(32 * u + 16 * e, 32 * u + 16 * e + 16)
                piece = moved(row[at], HALF * e - begin)
                if a == 5:
                    piece = jnp.where(lane < HALF * e + 16, piece, moved(last[at], HALF * e + 16 - 32 * q))
                pair.append(piece)
            tiles.append(jnp.where(lane < HALF, *pair))
        both = jnp.concatenate(tiles, axis=1)
        for half in range(2):
            found[half].append(both[8 * half : 8 * half + 8])
    return [jnp.concatenate(pieces, axis=0) for pieces in found]


def whole_matrix(cores, side, channel):
    parts = [matrix(by_row, side, channel) for by_row in cores]
    return [jnp.concatenate([parts[0][z1], parts[1][z1]], axis=1) for z1 in range(2)]


def squeezed(rows, squeeze):
    return jnp.dot(
        jnp.concatenate(rows, axis=0).astype(BF16), squeeze, preferred_element_type=F32
    ).astype(BF16)


def send_back(product, stretch):
    wide = jnp.dot(product.astype(BF16), stretch, preferred_element_type=F32)
    rows = []
    for channel in range(2):
        for t in range(3):
            parts = []
            for u in range(2):
                lanes = slice((2 * channel + u) * H, (2 * channel + u + 1) * H)
                pair = [
                    jnp.concatenate([wide[8 * a : 8 * a + 8, lanes], wide[48 + 8 * a : 56 + 8 * a, lanes]], axis=0)
                    for a in (2 * t, 2 * t + 1)
                ]
                parts.extend(halves(*pair))
            rows.append(jnp.concatenate(parts, axis=0))
    return by_device(rows).astype(BF16)


def start_kernel(pair_ref, weight_ref, gain_ref, out_ref, gate_ref):
    field = pair_ref[...].reshape(288, H).astype(F32)
    normed = normalize(field, gain_ref[0:1], 1).astype(BF16)
    projected = lax.dot_general(
        weight_ref[...], normed, (((0,), (1,)), ((), ())), preferred_element_type=F32
    )
    out_ref[...] = spread_rows(projected[: 4 * H])
    gate_ref[...] = jax.nn.sigmoid(projected[4 * H :])


def pack_kernel(both_ref, squeeze_ref, left_ref, right_ref):
    cores = [rows_of(both_ref[core]) for core in range(2)]
    first = lax.axis_index("core") == 0
    rows = []
    for channel in range(2):
        rows.extend(whole_matrix(cores, 0, channel))
    for channel in range(2):
        rows.append(jnp.where(first, *whole_matrix(cores, 1, channel)))
    packed = squeezed(rows, squeeze_ref[...])
    left_ref[...] = packed[:192]
    for x in range(4):
        right_ref[x] = packed[192:]


def outgoing_kernel(left_ref, right_ref, stretch_ref, out_ref):
    left = jnp.concatenate([left_ref[:96], left_ref[96:]], axis=1)
    none = jnp.zeros((192, 384), BF16)
    right = [right_ref[:, 48 * channel : 48 * channel + 48].reshape(192, 384) for channel in range(2)]
    right = jnp.concatenate(
        [jnp.concatenate([right[0], none], axis=1), jnp.concatenate([none, right[1]], axis=1)], axis=0
    )
    product = lax.dot_general(left, right, (((1,), (1,)), ((), ())), preferred_element_type=F32)
    out_ref[...] = send_back(product, stretch_ref[...])


def middle_kernel(
    arrived_ref, field_ref, gate_ref, out_weight_ref, weight_ref, gain_ref, out_ref, first_ref, next_gate_ref
):
    field = jnp.swapaxes(field_ref[...].reshape(288, H).astype(F32), 0, 1)
    mixed = normalize(closed_up(summed_rows(arrived_ref[...])), column(gain_ref[2:3]), 0).astype(BF16)
    update = lax.dot_general(out_weight_ref[0], mixed, (((0,), (0,)), ((), ())), preferred_element_type=F32)
    first = (field + gate_ref[...] * update).astype(BF16).astype(F32)
    normed = normalize(first, column(gain_ref[1:2]), 0).astype(BF16)
    weight = weight_ref[1]
    out_ref[...] = spread_turned(normed, weight)
    first_ref[...] = jnp.swapaxes(first, 0, 1).reshape(6, 48, H).astype(BF16)
    next_gate_ref[...] = jax.nn.sigmoid(
        lax.dot_general(normed, weight[:, 4 * H :], (((0,), (0,)), ((), ())), preferred_element_type=F32)
    )


def incoming_kernel(both_ref, squeeze_ref, stretch_ref, out_ref):
    cores = [rows_of(both_ref[core]) for core in range(2)]
    own = jnp.where(lax.axis_index("core") == 0, *cores)
    none = jnp.zeros((96, 256), F32)
    left, right = [], []
    for channel in range(2):
        left.extend(whole_matrix(cores, 0, channel))
        part = jnp.concatenate(matrix(own, 1, channel), axis=0)
        right.append(jnp.concatenate([none, part] if channel else [part, none], axis=1))
    left = lax.dot_general(
        stretch_ref[...],
        jnp.concatenate(left, axis=0).astype(BF16),
        (((1,), (1,)), ((), ())),
        preferred_element_type=F32,
    ).astype(BF16)
    product = jnp.dot(left, squeezed(right, squeeze_ref[...]), preferred_element_type=F32).astype(BF16)
    for x in range(4):
        for z1 in range(2):
            at = 192 * z1 + 48 * x
            out_ref[x, 48 * z1 : 48 * z1 + 48] = product[at : at + 48]


def sum_kernel(parts_ref, stretch_ref, out_ref):
    total = parts_ref[0].astype(F32)
    for x in range(1, 4):
        total = total + parts_ref[x].astype(F32)
    out_ref[...] = send_back(total, stretch_ref[...])


def end_kernel(arrived_ref, field_ref, gate_ref, out_weight_ref, gain_ref, out_ref):
    final = finish(
        summed_rows(arrived_ref[...]), field_ref[...].reshape(288, H), gate_ref[...], out_weight_ref[1], gain_ref[3:4]
    )
    out_ref[...] = final.reshape(6, 48, H).astype(BF16)


def squeeze_matrix():
    places = np.pad(np.ones((4, 48), bool), ((0, 0), (0, 16))).reshape(-1).nonzero()[0]
    places = places.reshape(2, 2, 2, 4, 6).transpose(3, 4, 0, 1, 2).reshape(-1)
    block = np.arange(256)[:, None] == places[None, :]
    return np.kron(np.eye(2, dtype=bool), block).astype(jnp.bfloat16)


def call(kernel, outs, scratch=(), **specs):
    return pl.pallas_call(
        kernel,
        out_shape=[jax.ShapeDtypeStruct(shape, dtype) for shape, dtype in outs],
        scratch_shapes=list(scratch),
        compiler_params=pltpu.CompilerParams(vmem_limit_bytes=48 * 1024 * 1024),
        cost_estimate=pl.CostEstimate(flops=20_000_000, bytes_accessed=1_000_000, transcendentals=100_000),
        **specs,
    )


def shards(pair_field, proj_weight, out_weight, in_gain, out_gain):
    exchange = functools.partial(lax.all_to_all, split_axis=0, concat_axis=0, tiled=True)
    squeeze, stretch = jnp.asarray(squeeze_matrix()), jnp.asarray(squeeze_matrix().T)
    pairs, gates = ((6, 48, H), BF16), ((288, H), F32)
    sides, results = ((HALF, 5, 2, H), BF16), ((HALF, 3, 2, H), BF16)
    block, blocks = ((192, 384), BF16), ((4, 96, 384), BF16)

    gains = jnp.concatenate([in_gain, out_gain], axis=0)
    sent, gating = call(start_kernel, [sides, ((H, 288), F32)])(pair_field, proj_weight[0], gains)
    own = exchange(sent, SPREAD)
    both = lax.all_gather(own, "core", axis=0, tiled=False)
    left, right = call(pack_kernel, [block, blocks])(both, squeeze)
    right = exchange(right, "x")
    [back] = call(outgoing_kernel, [results])(left, right, stretch)
    arrived = exchange(back, SPREAD)

    sent, first_pair, gating = call(middle_kernel, [sides, pairs, gates])(
        arrived, pair_field, gating, out_weight, proj_weight, gains
    )
    own = exchange(sent, SPREAD)
    both = lax.all_gather(own, "core", axis=0, tiled=False)
    [parts] = call(incoming_kernel, [blocks])(both, squeeze, stretch)
    parts = exchange(parts, "x")
    [back] = call(sum_kernel, [results])(parts, stretch)
    arrived = exchange(back, SPREAD)
    [out] = call(end_kernel, [pairs])(arrived, first_pair, gating, out_weight, gains)
    return out


def solution(mesh):
    fine = Mesh(mesh.devices.reshape(2, 2, 2, 2, 4, 4, 2), ("yh", "z2", "z1", "z0", "x", "yl", "core"))
    row, col = ("yh", "z2", "z1", "z0", "x"), ("yl", "core")
    return jax.shard_map(
        shards,
        mesh=fine,
        in_specs=(P(row, col, None), P(), P(), P(), P()),
        out_specs=P(row, col, None),
        check_vma=False,
    )
```
